512 devices in a mesh: dir: 8 (over z), gx: 64 (over x, y, core).
Axes of the slice: x: 4, y: 8, z: 8, core: 2. Of those that a mesh axis runs over, the one named last changes fastest.
Arguments:
- cotangent: float32 [8, 256, 32, 512], P('dir', 'gx'), may hold values from -24 to 24
- potential: float32 [8, 256, 32, 512], P('dir', 'gx'), may hold values from -0.6 to 0.6
- height: float32 [256, 512], P('gx'), may hold values from 0 to 1
Outputs:
- adjoint: float32 [8, 256, 32, 512], P('dir', 'gx')
- gradient: float32 [256, 512], P('gx', 'dir')
The draws below stay inside these ranges and needn't reach their ends.
All inputs are finite; a program needn't handle non-finite values.
Results may differ from the reference program's by a relative error of at most 0.0002.
Values sent between devices are 32-bit elements; how exact they have to be, the bound alone decides.
A program may use at most 64 MiB of HBM per device.

```python
import jax
import jax.numpy as jnp
from jax import lax

NZ = 32
NY = 512
LEVELS = 3
SWEEPS = 2
COARSE_SWEEPS = 8
NDIR = 8
NX = 256


def draw_cotangent(key, part):
    key = jax.random.fold_in(key, 7)
    extent = (NDIR, NX, NZ, NY)
    return jnp.clip(6.0 * jax.random.normal(key, extent, jnp.float32), -24.0, 24.0)


def with_spikes(entries, rng, source, target, shards_of, factor):
    def block_of(dim):
        return (jnp.arange(entries.shape[dim]) // (entries.shape[dim] // shards_of)).reshape((-1,) + (1,) * (entries.ndim - 1 - dim))

    first = jax.random.permutation(rng, shards_of)[block_of(target)]
    other_side = (block_of(target) + shards_of // 2) % shards_of
    return jnp.where((block_of(source) == first) | (block_of(source) == other_side), factor * entries, entries)


def level_of(rng, dims, cuts, least, high):
    def one(axis_at, shards_of):
        draws = jax.random.uniform(jax.random.fold_in(jax.random.fold_in(rng, 6), axis_at), (shards_of,), jnp.float32, least / len(cuts), high / len(cuts))
        return jnp.repeat(jnp.exp(draws), dims[axis_at] // shards_of).reshape((-1,) + (1,) * (len(dims) - axis_at - 1))

    factor_of = one(*cuts[0])
    for cut in cuts[1:]:
        factor_of = factor_of * one(*cut)
    return factor_of


def noise_with(stream_key, shape, spread, limit, shards, heavy, kind=jnp.bfloat16):
    entries = spread * jax.random.normal(stream_key, shape, jnp.float32)
    if shards:
        entries = entries * level_of(stream_key, shape, shards, -0.22, 0.18)
    return jnp.clip(with_spikes(entries, jax.random.fold_in(stream_key, 3), *heavy), -limit, limit).astype(kind)


def setup_inputs(seed: int = 0) -> dict:
    splits = jax.random.split(jax.random.key(seed), 4)
    cotangent = draw_cotangent(jax.random.fold_in(splits[3], 71), 0)
    potential = noise_with(splits[1], (NDIR, NX, NZ, NY), 0.1, 0.6, ((0, 8), (1, 64)), (0, 3, 8, 2.0), jnp.float32)
    height = jnp.clip(1.0 * jax.random.uniform(splits[2], (NX, NY), jnp.float32) ** level_of(splits[2], (NX, NY), ((0, 64),), -0.2, 0.2), 0.0, 1.0)
    return dict(cotangent=cotangent, potential=potential, height=height)


damping = 0.7
anisotropy = 4.0
ceiling = 1.5


def harmonic(first_side, second_side, factor):
    return factor * 2.0 * first_side * second_side / (first_side + second_side)


def side_sum(weights, axis_pos):
    pad_before = [(0, 0)] * weights.ndim
    pad_after = [(0, 0)] * weights.ndim
    pad_before[axis_pos] = (1, 0)
    pad_after[axis_pos] = (0, 1)
    return jnp.pad(weights, pad_before) + jnp.pad(weights, pad_after)


def level_data(terrain, factor):
    x_faces = jnp.pad(harmonic(terrain[:-1], terrain[1:], factor), ((1, 1), (0, 0)))
    y_faces = jnp.pad(harmonic(terrain[:, :-1], terrain[:, 1:], factor), ((1, 1), (0, 0)))
    z_weight = jnp.pad(factor * anisotropy / terrain, ((1, 1), (0, 0)))
    centre = side_sum(x_faces, 0) + side_sum(y_faces, 1)
    return (x_faces, y_faces, z_weight, centre, 1)


def diagonal_rows(operator, first_row, row_count, depth_count):
    x_faces, y_faces, z_weight, centre, rim_width = operator
    layer_weight = jnp.where(jnp.arange(depth_count) == 0, 1.0, 2.0)
    centre_rows = centre[first_row:first_row + row_count][:, None, :]
    z_rows = z_weight[first_row:first_row + row_count][:, None, :]
    return centre_rows + z_rows * layer_weight[None, :, None]


def apply_rows(estimate, margin, operator):
    x_faces, y_faces, z_weight, centre, rim_width = operator
    row_count = estimate.shape[0] - 2
    first_row = rim_width - margin + 1
    middle = estimate[1:-1]
    diagonal = diagonal_rows(operator, first_row, row_count, estimate.shape[1])
    west_weight = x_faces[first_row - 1:first_row - 1 + row_count][:, None, :]
    east_weight = x_faces[first_row:first_row + row_count][:, None, :]
    y_weight = y_faces[first_row:first_row + row_count][:, None, :]
    z_rows = z_weight[first_row:first_row + row_count][:, None, :]
    y_terms = jnp.pad(y_weight * middle[:, :, 1:], ((0, 0), (0, 0), (0, 1))) + jnp.pad(y_weight * middle[:, :, :-1], ((0, 0), (0, 0), (1, 0)))
    z_terms = z_rows * (jnp.pad(middle[:, 1:], ((0, 0), (0, 1), (0, 0))) + jnp.pad(middle[:, :-1], ((0, 0), (1, 0), (0, 0))))
    applied = diagonal * middle - west_weight * estimate[:-2] - east_weight * estimate[2:] - y_terms - z_terms
    return applied, diagonal


def jacobi(estimate, margin, forcing, operator):
    applied, diagonal = apply_rows(estimate, margin, operator)
    return estimate[1:-1] + damping * (forcing - applied) / diagonal


def pad_rows(estimate):
    return jnp.pad(estimate, ((1, 1), (0, 0), (0, 0)))


def restrict(fine_values):
    extent = fine_values.shape
    return fine_values.reshape(extent[0] // 2, 2, extent[1] // 2, 2, extent[2] // 2, 2).sum(axis=(1, 3, 5))


def prolong(coarse_values):
    return jnp.repeat(jnp.repeat(jnp.repeat(coarse_values, 2, 0), 2, 1), 2, 2)


def shrink(terrain):
    extent = terrain.shape
    return terrain.reshape(extent[0] // 2, 2, extent[1] // 2, 2).mean(axis=(1, 3))


def vcycle(forcing, depth_level, terrain):
    operator = level_data(terrain, 2.0 ** depth_level)
    estimate = damping * forcing / diagonal_rows(operator, 1, forcing.shape[0], forcing.shape[1])
    if depth_level == LEVELS - 1:
        for sweep_index in range(COARSE_SWEEPS - 1):
            estimate = jacobi(pad_rows(estimate), 1, forcing, operator)
        return estimate
    for sweep_index in range(SWEEPS - 1):
        estimate = jacobi(pad_rows(estimate), 1, forcing, operator)
    applied, unused = apply_rows(pad_rows(estimate), 1, operator)
    correction = vcycle(restrict(forcing - applied), depth_level + 1, shrink(terrain))
    estimate = estimate + prolong(correction)
    for sweep_index in range(SWEEPS):
        estimate = jacobi(pad_rows(estimate), 1, forcing, operator)
    return estimate


def terrain_term(adjoint, potential, depth_map):
    x_prod = jnp.sum((adjoint[1:] - adjoint[:-1]) * (potential[1:] - potential[:-1]), axis=1)
    west_depth = depth_map[:-1]
    east_depth = depth_map[1:]
    summed = (west_depth + east_depth) * (west_depth + east_depth)
    west_share = 2.0 * east_depth * east_depth / summed * x_prod
    east_share = 2.0 * west_depth * west_depth / summed * x_prod
    x_term = jnp.pad(west_share, ((0, 1), (0, 0))) + jnp.pad(east_share, ((1, 0), (0, 0)))
    y_prod = jnp.sum((adjoint[:, :, 1:] - adjoint[:, :, :-1]) * (potential[:, :, 1:] - potential[:, :, :-1]), axis=1)
    south_depth = depth_map[:, :-1]
    north_depth = depth_map[:, 1:]
    y_summed = (south_depth + north_depth) * (south_depth + north_depth)
    south_share = 2.0 * north_depth * north_depth / y_summed * y_prod
    north_share = 2.0 * south_depth * south_depth / y_summed * y_prod
    y_term = jnp.pad(south_share, ((0, 0), (0, 1))) + jnp.pad(north_share, ((0, 0), (1, 0)))
    z_prod = jnp.sum((adjoint[:, 1:] - adjoint[:, :-1]) * (potential[:, 1:] - potential[:, :-1]), axis=1) + adjoint[:, -1] * potential[:, -1]
    z_term = -anisotropy / (depth_map * depth_map) * z_prod
    return x_term + y_term + z_term


def reference(cotangent, potential, height):
    depth_map = ceiling - height

    def one_direction(inputs_pair):
        forcing, forward = inputs_pair
        adjoint = vcycle(forcing, 0, depth_map)
        return adjoint, terrain_term(adjoint, forward, depth_map)

    adjoint, dir_terms = lax.map(one_direction, (cotangent, potential))
    return adjoint, jnp.sum(dir_terms, axis=0)
```

```python
import functools

import jax
import jax.numpy as jnp
from jax import lax
from jax.experimental import pallas as pl
from jax.experimental.pallas import tpu as pltpu
from jax.sharding import PartitionSpec as P

MESH = pl.DeviceIdType.MESH
DAMPING = 0.7
ANISOTROPY = 4.0
CEILING = 1.5
REACH = 9
C, CW, CE, CS, CN, CZ, RHO, SIG, DINV = range(9)
GW, GE, GS, GN, GZ = range(9, 14)


def iota(shape, dim):
    return lax.broadcasted_iota(jnp.int32, shape, dim)


def spread_lanes(cols):
    shape = cols[0].shape
    lane = iota(shape, 1)
    block, inner = lane >> 5, lane & 31
    turned = [
        jnp.take_along_axis(col, 4 * inner + ((block - c) & 3), axis=1, mode="promise_in_bounds")
        for c, col in enumerate(cols)
    ]
    out = []
    for p in range(4):
        mixed = turned[(3 - p) % 4]
        for b in range(3):
            mixed = jnp.where(block == b, turned[(b - p) % 4], mixed)
        out.append(mixed if p == 0 else pltpu.roll(mixed, 128 - 32 * p, 1))
    return out


def join_lanes(classes):
    shape = classes[0].shape
    lane = iota(shape, 1)
    block = lane >> 5
    turned = [cl if p == 0 else pltpu.roll(cl, 32 * p, 1) for p, cl in enumerate(classes)]
    out = []
    for c in range(4):
        mixed = turned[(3 - c) % 4]
        for b in range(3):
            mixed = jnp.where(block == b, turned[(b - c) % 4], mixed)
        source = (((lane + c) & 3) << 5) + (lane >> 2)
        out.append(jnp.take_along_axis(mixed, source, axis=1, mode="promise_in_bounds"))
    return out


def harmonic(a, b, scale):
    return scale * 2.0 * a * b / (a + b)


def level_weights(mid, west, east, open_west, open_east, scale):
    count = len(mid)
    lane = iota(mid[0].shape, 1)
    w_west = [jnp.where(open_west, harmonic(a, b, scale), 0.0) for a, b in zip(mid, west)]
    w_east = [jnp.where(open_east, harmonic(a, b, scale), 0.0) for a, b in zip(mid, east)]
    w_north = [harmonic(mid[p], mid[p + 1], scale) for p in range(count - 1)]
    last = harmonic(mid[count - 1], pltpu.roll(mid[0], 127, 1), scale)
    w_north.append(jnp.where(lane < 127, last, 0.0))
    w_south = [pltpu.roll(w_north[count - 1], 1, 1)] + w_north[:-1]
    out = []
    for p in range(count):
        w_z = (scale * ANISOTROPY) / mid[p]
        low = w_west[p] + w_east[p] + w_south[p] + w_north[p] + w_z
        full = low + w_z
        c = DAMPING / full
        out.append(
            (c, c * w_west[p], c * w_east[p], c * w_south[p], c * w_north[p], c * w_z, full / low, low / full, full / DAMPING)
        )
    return out


def terrain_weights(mid, west, east, open_west, open_east):
    lane = iota(mid[0].shape, 1)

    def share(own, other):
        both = own + other
        return 2.0 * other * other / (both * both)

    out = []
    for p in range(4):
        south = mid[p - 1] if p else pltpu.roll(mid[3], 1, 1)
        north = mid[p + 1] if p < 3 else pltpu.roll(mid[0], 127, 1)
        g_south, g_north = share(mid[p], south), share(mid[p], north)
        out.append(
            (
                jnp.where(open_west, share(mid[p], west[p]), 0.0),
                jnp.where(open_east, share(mid[p], east[p]), 0.0),
                g_south if p else jnp.where(lane > 0, g_south, 0.0),
                g_north if p < 3 else jnp.where(lane < 127, g_north, 0.0),
                -ANISOTROPY / (mid[p] * mid[p]),
            )
        )
    return out


def north_of(v, q, p):
    return v[q][p + 1] if p + 1 < len(v[q]) else pltpu.roll(v[q][0], 127, 1)


def south_of(v, q, p):
    return v[q][p - 1] if p else pltpu.roll(v[q][-1], 1, 1)


def above(v, q, p, top):
    return v[q + 1][p] if q + 1 < len(v) else jnp.where(top, 0.0, pltpu.roll(v[0][p], 7, 0))


def below(v, q, p, bottom):
    return v[q - 1][p] if q else jnp.where(bottom, 0.0, pltpu.roll(v[-1][p], 1, 0))


def around(v, v_west, v_east, w, bottom, top):
    out = []
    for q in range(len(v)):
        line = []
        for p in range(len(v[q])):
            total = w(CZ, p) * (above(v, q, p, top) + below(v, q, p, bottom))
            total = total + w(CS, p) * south_of(v, q, p) + w(CN, p) * north_of(v, q, p)
            if v_west is not None:
                total = total + w(CW, p) * v_west[q][p]
            if v_east is not None:
                total = total + w(CE, p) * v_east[q][p]
            line.append(total)
        out.append(line)
    return out


def swept(v, v_west, v_east, start, w, bottom, top):
    near = around(v, v_west, v_east, w, bottom, top)
    out = []
    for q in range(len(v)):
        line = []
        for p in range(len(v[q])):
            move = near[q][p] if q else near[q][p] * jnp.where(bottom, w(RHO, p), 1.0)
            line.append((1.0 - DAMPING) * v[q][p] + start[q][p] + move)
        out.append(line)
    return out


def restricted(v, v_west, v_east, start, w, bottom, top):
    near = around(v, v_west, v_east, w, bottom, top)
    half = len(v) // 2
    out = [[0.0] * half for _ in range(half)]
    for q1 in range(half):
        for p in range(len(v)):
            part = 0.0
            for q in (2 * q1, 2 * q1 + 1):
                own = -DAMPING * v[q][p] if start is None else start[q][p] - DAMPING * v[q][p]
                if q == 0:
                    own = own * jnp.where(bottom, w(SIG, p), 1.0)
                part = part + (near[q][p] + own)
            out[q1][p // 2] = out[q1][p // 2] + w(DINV, p) * part
    return out


def edge_restricted(v, kind, w):
    half = len(v) // 2
    return [
        [sum((w(DINV, p) * w(kind, p)) * (v[2 * q1][p] + v[2 * q1 + 1][p]) for p in (2 * p1, 2 * p1 + 1)) for p1 in range(half)]
        for q1 in range(half)
    ]


def edge_swept(v, kind, w, bottom):
    return [
        [w(kind, p) * (v[q][p] if q else v[q][p] * jnp.where(bottom, w(RHO, p), 1.0)) for p in range(len(v[q]))]
        for q in range(len(v))
    ]


def added(a, b):
    return [[s + t for s, t in zip(x, y)] for x, y in zip(a, b)]


def first_guess(f, w, bottom):
    return [
        [w(C, p) * (f[q][p] if q else f[q][p] * jnp.where(bottom, w(RHO, p), 1.0)) for p in range(len(f[q]))]
        for q in range(len(f))
    ]


def grid_of(block, count):
    return [[block[q * count + p] for p in range(count)] for q in range(count)]


def table(ref, row):
    @functools.cache
    def weight(kind, p):
        return ref[kind, p, pl.ds(row, 1), :]

    return weight


def put_row(ref, row, tiles):
    count = len(tiles)
    for q in range(count):
        for p in range(count):
            ref[row, q * count + p] = tiles[q][p]


def kernel(
    n_dir, n_gx,
    cot, pot, height, adjoint, gradient,
    h_in, c_in, p_in, a_out, mixed,
    hs, fs, ps, ds, w0, de, d1, w1, df, d2s, d2, w2,
    v0, v1, v2, v3,
    f1p, f1e, f2p, f2e, f2own, f2r, f1, u0, u1, u2, u3,
    gn, er,
    local_sem, send_sem, recv_sem,
):
    me_dir, me = lax.axis_index("dir"), lax.axis_index("gx")

    def strip(offset):
        return {"gx": lax.rem(me + offset + REACH * n_gx, n_gx)}

    barrier = pltpu.get_barrier_semaphore()
    reach = [o for o in range(-REACH, REACH + 1) if o]
    for offset in reach:
        pl.semaphore_signal(barrier, inc=1, device_id=strip(offset), device_id_type=MESH)
    for step in range(1, n_dir):
        pl.semaphore_signal(
            barrier, inc=1, device_id={"dir": lax.rem(me_dir + step, n_dir)}, device_id_type=MESH
        )

    height_in = pltpu.make_async_copy(height, h_in, local_sem.at[0])
    cot_in = pltpu.make_async_copy(cot.at[0], c_in, local_sem.at[1])
    pot_in = pltpu.make_async_copy(pot.at[0], p_in, local_sem.at[2])
    height_in.start()
    cot_in.start()
    pot_in.start()

    sent = []

    def send(source, target, device):
        index = len(sent)
        copy = pltpu.make_async_remote_copy(
            src_ref=source, dst_ref=target, send_sem=send_sem.at[index], recv_sem=recv_sem.at[index],
            device_id=device, device_id_type=MESH,
        )
        copy.start()
        sent.append(copy)
        return copy

    bottom, top = iota((8, 128), 0) == 0, iota((8, 128), 0) == 7

    for p in range(4):
        ds[p, 24:32, :] = jnp.ones((8, 128), jnp.float32)
    d2[...] = jnp.ones(d2.shape, jnp.float32)
    d1[...] = jnp.ones(d1.shape, jnp.float32)

    height_in.wait()
    raw = h_in[...]
    for p, cl in enumerate(spread_lanes([raw[:, 128 * c : 128 * c + 128] for c in range(4)])):
        hs[3, 4 * p : 4 * p + 4, :] = CEILING - cl

    pl.semaphore_wait(barrier, len(reach) + n_dir - 1)
    depth_copies = [send(hs.at[3], hs.at[3 - o], strip(o)) for o in (-1, 1, -2, 2, -3, 3)]

    def spread_row(source, target, row, slot):
        block = source[row]
        for p, cl in enumerate(spread_lanes([block[:, 128 * c : 128 * c + 128] for c in range(4)])):
            target[slot, p] = cl

    cot_in.wait()
    for x in range(0, 4):
        spread_row(c_in, fs, x, x + 4)
    field_copies = [
        send(fs.at[pl.ds(4, 4)], fs.at[pl.ds(4 - 4 * o, 4)], strip(o)) for o in (-1, 1)
    ]

    def field_row(ref, slot):
        return [[ref[slot, p, pl.ds(q, 8, stride=4), :] for p in range(4)] for q in range(4)]

    for copy in depth_copies:
        copy.wait_recv()
    for o in range(7):
        for p in range(4):
            ds[p, 4 * o : 4 * o + 4, :] = hs[o, 4 * p : 4 * p + 4, :]
    for p1 in range(2):
        de[p1] = ds[2 * p1] + ds[2 * p1 + 1]
    for p1 in range(2):
        d1[p1, 0:16, :] = 0.25 * (de[p1, pl.ds(0, 16, stride=2), :] + de[p1, pl.ds(1, 16, stride=2), :])
    df[...] = d1[0] + d1[1]
    d2s[1] = 0.25 * (df[pl.ds(0, 8, stride=2), :] + df[pl.ds(1, 8, stride=2), :])
    d2_copies = [send(d2s.at[1], d2s.at[1 - s], strip(7 * s)) for s in (-1, 1)]

    def faces(rows, per_strip, first):
        size = n_gx * per_strip
        place = (me * per_strip + first + REACH * size + iota((rows, 128), 0)) & (size - 1)
        return place != 0, place != size - 1

    open_west, open_east = faces(16, 4, -4)
    mid = [ds[p, 8:24, :] for p in range(4)]
    west = [ds[p, 7:23, :] for p in range(4)]
    east = [ds[p, 9:25, :] for p in range(4)]
    for p, kinds in enumerate(level_weights(mid, west, east, open_west, open_east, 1.0)):
        for kind, value in enumerate(kinds):
            w0[kind, p] = value
    open_west, open_east = faces(16, 2, -5)
    mid1 = [d1[p, 1:17, :] for p in range(2)]
    west1 = [d1[p, 0:16, :] for p in range(2)]
    east1 = [d1[p, 2:18, :] for p in range(2)]
    for p, kinds in enumerate(level_weights(mid1, west1, east1, open_west, open_east, 2.0)):
        for kind, value in enumerate(kinds):
            w1[kind, p] = value

    def guess_row(i):
        put_row(v0, i, first_guess(field_row(fs, i), table(w0, i), bottom))

    def row_of(ref, i, count=4):
        return grid_of(ref[i], count)

    def smooth_rows(source, target, low, high):
        have = {i: row_of(source, i) for i in range(low - 1, high + 1)}
        for i in range(low, high):
            put_row(target, i, swept(have[i], have[i - 1], have[i + 1], row_of(v0, i), table(w0, i), bottom, top))

    for i in range(4, 8):
        guess_row(i)
    have = [None] + [row_of(v0, i) for i in range(4, 8)] + [None]
    put_row(v1, 3, edge_swept(have[1], CE, table(w0, 3), bottom))
    for i in range(4, 8):
        put_row(v1, i, swept(have[i - 3], have[i - 4], have[i - 2], have[i - 3], table(w0, i), bottom, top))
    put_row(v1, 8, edge_swept(have[4], CW, table(w0, 8), bottom))
    have = [None] + [row_of(v1, i) for i in range(3, 9)] + [None]
    rest = {i: restricted(have[i - 2], have[i - 3], have[i - 1], row_of(v0, i) if 4 <= i <= 7 else None, table(w0, i), bottom, top) for i in range(3, 9)}
    rest[2] = edge_restricted(have[1], CE, table(w0, 2))
    rest[9] = edge_restricted(have[6], CW, table(w0, 9))
    for i in range(4):
        put_row(f1p, i, added(rest[2 * i + 2], rest[2 * i + 3]))

    begin = {i: first_guess(grid_of(f1p[i - 4], 2), table(w1, i), bottom) for i in range(4, 8)}
    next_row = {i: swept(begin[i], begin.get(i - 1), begin.get(i + 1), begin[i], table(w1, i), bottom, top) for i in range(4, 8)}
    next_row[3] = edge_swept(begin[4], CE, table(w1, 3), bottom)
    next_row[8] = edge_swept(begin[7], CW, table(w1, 8), bottom)
    rest = {
        i: restricted(next_row[i], next_row.get(i - 1), next_row.get(i + 1), begin.get(i), table(w1, i), bottom, top)
        for i in range(3, 9)
    }
    rest[2] = edge_restricted(next_row[3], CE, table(w1, 2))
    rest[9] = edge_restricted(next_row[8], CW, table(w1, 9))
    for coarse, near_rows in enumerate(((2,), (3, 4), (5, 6), (7, 8), (9,))):
        f2p[coarse] = sum(rest[i][0][0] for i in near_rows)
    slot_of = {2: 0, 1: 1, -1: 2, -2: 3}
    f2_copies = [send(f2p.at[2 + o], f2e.at[slot_of[o]], strip(o)) for o in (-1, 1, -2, 2)]
    f1_copies = [send(f1p.at[0], f1e.at[1], strip(-1)), send(f1p.at[3], f1e.at[0], strip(1))]

    pot_in.wait()
    for x in range(0, 4):
        spread_row(p_in, ps, x, x + 1)
    potential_copies = [send(ps.at[1], ps.at[5], strip(-1)), send(ps.at[4], ps.at[0], strip(1))]

    for copy in d2_copies:
        copy.wait_recv()
    d2[0:8, :] = d2s[0]
    d2[7:15, :] = d2s[1]
    d2[14:22, :] = d2s[2]
    open_west, open_east = faces(24, 1, -9)
    for kind, value in enumerate(
        level_weights([d2[1:25, :]], [d2[0:24, :]], [d2[2:26, :]], open_west, open_east, 4.0)[0]
    ):
        w2[kind, 0] = value

    for copy in f2_copies:
        copy.wait_recv()
    f2own[0] = f2p[2] + ((f2e[0] + f2e[1]) + (f2e[2] + f2e[3]))
    place_of = {o: (o + REACH if o < 0 else o + REACH - 1) for o in reach}
    row_copies = [send(f2own.at[0], f2r.at[place_of[-o]], strip(o)) for s in range(1, REACH + 1) for o in (-s, s)]
    for copy in f1_copies:
        copy.wait_recv()
    f1[6] = f1p[1] + f1e[0]
    f1[7] = f1p[2] + f1e[1]
    f1_copies = [
        send(f1.at[pl.ds(6, 2)], f1.at[pl.ds(6 - 2 * o, 2)], strip(o)) for o in (-1, 1, -2, 2, -3, 3)
    ]

    terrain = terrain_weights(
        [ds[p, 8:24, :] for p in range(4)], [ds[p, 7:23, :] for p in range(4)], [ds[p, 9:25, :] for p in range(4)],
        *faces(16, 4, -4),
    )
    for p, kinds in enumerate(terrain):
        for kind, value in enumerate(kinds):
            w0[GW + kind, p] = value
    for copy in field_copies:
        copy.wait_recv()
    for i in range(0, 4):
        guess_row(i)
    for i in range(8, 12):
        guess_row(i)
    smooth_rows(v0, v1, 1, 11)

    for copy in f1_copies:
        copy.wait_recv()
    for i in range(0, 12):
        put_row(u0, i, first_guess(grid_of(f1[i + 1], 2), table(w1, i), bottom))
    for i in range(1, 11):
        rows = [row_of(u0, i + d, 2) for d in (0, -1, 1)]
        put_row(u1, i, swept(*rows, row_of(u0, i, 2), table(w1, i), bottom, top))

    for copy in row_copies:
        copy.wait_recv()
    start = []
    for o in range(-REACH, REACH + 1):
        source = f2r[place_of[o]] if o else f2own[0]
        start.append(first_guess([[source]], table(w2, o + REACH), bottom))
    now = start
    for sweep in range(7):
        later = [None] * len(now)
        for i in range(sweep + 1, len(now) - sweep - 1):
            later[i] = swept(now[i], now[i - 1], now[i + 1], start[i], table(w2, i), bottom, top)
        now = later

    for i in range(1, 11):
        fix = now[(i - 5) // 2 + REACH][0][0]
        put_row(u1, i, [[t + fix for t in line] for line in row_of(u1, i, 2)])
    for source, target, low, high in ((u1, u2, 2, 10), (u2, u3, 3, 9)):
        for i in range(low, high):
            rows = [row_of(source, i + d, 2) for d in (0, -1, 1)]
            put_row(target, i, swept(*rows, row_of(u0, i, 2), table(w1, i), bottom, top))

    def corrected_row(i):
        fix = row_of(u3, (i - 4 + 8) // 2 + 1, 2)
        now_row = row_of(v1, i)
        put_row(v1, i, [[now_row[q][p] + fix[q // 2][p // 2] for p in range(4)] for q in range(4)])

    for i in range(1, 11):
        corrected_row(i)
    smooth_rows(v1, v2, 2, 10)
    smooth_rows(v2, v3, 3, 9)

    for copy in potential_copies:
        copy.wait_recv()

    def terrain_row(x):
        w = table(w0, x + 4)
        a, a_west, a_east = (row_of(v3, x + 4 + d) for d in (0, -1, 1))
        b, b_west, b_east = (field_row(ps, x + 1 + d) for d in (0, -1, 1))
        zeros = jnp.zeros((8, 128), jnp.float32)
        by_z, by_west, by_east, by_north = ([zeros] * 4 for _ in range(4))
        for q in range(4):
            for p in range(4):
                by_z[p] += (above(a, q, p, top) - a[q][p]) * (above(b, q, p, top) - b[q][p])
                by_west[p] += (a[q][p] - a_west[q][p]) * (b[q][p] - b_west[q][p])
                by_east[p] += (a_east[q][p] - a[q][p]) * (b_east[q][p] - b[q][p])
                by_north[p] += (north_of(a, q, p) - a[q][p]) * (north_of(b, q, p) - b[q][p])
        out = []
        for p in range(4):
            by_south = by_north[p - 1] if p else pltpu.roll(by_north[3], 1, 1)
            total = w(GW, p) * by_west[p] + w(GE, p) * by_east[p] + w(GN, p) * by_north[p]
            total = total + w(GS, p) * by_south + w(GZ, p) * by_z[p]
            out.append(jnp.sum(total, axis=0, keepdims=True))
        return out

    sums = [terrain_row(x) for x in range(4)]
    blank = jnp.zeros((4, 128), jnp.float32)
    packed = [jnp.concatenate([sums[x][p] for x in range(4)] + [blank], axis=0) for p in range(4)]
    for c, tile in enumerate(join_lanes(packed)):
        gn[c] = tile
    dir_copies = []
    for step in range(1, n_dir):
        target = lax.rem(me_dir + step, n_dir)
        dir_copies.append(send(gn.at[target // (n_dir // 4)], er.at[step - 1], {"dir": target}))

    def natural_row(x):
        now_row = row_of(v3, x + 4)
        for p in range(4):
            for q in range(4):
                mixed[x, p, pl.ds(q, 8, stride=4), :] = now_row[q][p]
        for c, tile in enumerate(join_lanes([mixed[x, p] for p in range(4)])):
            a_out[x, :, 128 * c : 128 * c + 128] = tile

    for i in range(0, 4):
        natural_row(i)
    out_copy = pltpu.make_async_copy(a_out, adjoint.at[0], local_sem.at[3])
    out_copy.start()

    for copy in dir_copies:
        copy.wait_recv()
    total = gn[me_dir // (n_dir // 4)]
    for step in range(1, n_dir):
        total = total + er[step - 1]
    part = lax.rem(me_dir, n_dir // 4)
    mine = total
    width = gradient.shape[1]
    for k in range(1, 128 // width):
        mine = jnp.where(iota((8, 128), 0) * 0 + part == k, pltpu.roll(total, 128 - k * width, 1), mine)
    gradient[...] = mine[0:4, 0:width]

    out_copy.wait()
    for copy in sent:
        copy.wait_send()


def body(cotangent, potential, height):
    n_dir, n_gx = lax.axis_size("dir"), lax.axis_size("gx")
    f32 = jnp.float32
    shapes = [
        (4, 512), (4, 32, 512), (4, 32, 512), (4, 32, 512), (4, 4, 32, 128),
        (7, 16, 128), (12, 4, 32, 128), (6, 4, 32, 128), (4, 32, 128), (14, 4, 16, 128),
        (2, 32, 128), (2, 24, 128), (9, 2, 16, 128), (24, 128), (3, 8, 128), (32, 128), (9, 1, 24, 128),
        (12, 16, 8, 128), (12, 16, 8, 128), (12, 16, 8, 128), (12, 16, 8, 128),
        (4, 4, 8, 128), (2, 4, 8, 128), (5, 8, 128), (4, 8, 128), (1, 8, 128), (18, 8, 128), (14, 4, 8, 128),
        (12, 4, 8, 128), (12, 4, 8, 128), (12, 4, 8, 128), (12, 4, 8, 128),
        (4, 8, 128), (n_dir - 1, 8, 128),
    ]
    copies = 6 + 2 + 2 + 4 + 2 + 2 + 2 * REACH + 6 + n_dir - 1
    return pl.pallas_call(
        functools.partial(kernel, n_dir, n_gx),
        out_shape=(
            jax.ShapeDtypeStruct(cotangent.shape, f32),
            jax.ShapeDtypeStruct((height.shape[0], height.shape[1] // n_dir), f32),
        ),
        in_specs=[pl.BlockSpec(memory_space=pltpu.HBM)] * 3,
        out_specs=(pl.BlockSpec(memory_space=pl.ANY), pl.BlockSpec(memory_space=pltpu.VMEM)),
        scratch_shapes=[pltpu.VMEM(shape, f32) for shape in shapes]
        + [pltpu.SemaphoreType.DMA((4,)), pltpu.SemaphoreType.DMA((copies,)), pltpu.SemaphoreType.DMA((copies,))],
        compiler_params=pltpu.CompilerParams(
            collective_id=0, has_side_effects=True, vmem_limit_bytes=60 * 1024 * 1024
        ),
        name="vcycle",
    )(cotangent, potential, height)


def solution(mesh):
    placed = (P("dir", "gx", None, None), P("dir", "gx", None, None), P("gx", None))
    return jax.shard_map(
        body,
        mesh=mesh,
        in_specs=placed,
        out_specs=(P("dir", "gx", None, None), P("gx", "dir")),
        check_vma=False,
    )
```

```python
import functools

import jax
import jax.numpy as jnp
from jax import lax
from jax.experimental import pallas as pl
from jax.experimental.pallas import tpu as pltpu
from jax.sharding import PartitionSpec as P

MESH = pl.DeviceIdType.MESH
DAMPING = 0.7
ANISOTROPY = 4.0
CEILING = 1.5
REACH = 9
GREET = 4
C, CW, CE, CS, CN, CZ, RHO, SIG, DINV = range(9)
GW, GE, GS, GN, GZ = range(9, 14)


def iota(shape, dim):
    return lax.broadcasted_iota(jnp.int32, shape, dim)


def spread_lanes(cols):
    shape = cols[0].shape
    lane = iota(shape, 1)
    block, inner = lane >> 5, lane & 31
    turned = [
        jnp.take_along_axis(col, 4 * inner + ((block - c) & 3), axis=1, mode="promise_in_bounds")
        for c, col in enumerate(cols)
    ]
    out = []
    for p in range(4):
        mixed = turned[(3 - p) % 4]
        for b in range(3):
            mixed = jnp.where(block == b, turned[(b - p) % 4], mixed)
        out.append(mixed if p == 0 else pltpu.roll(mixed, 128 - 32 * p, 1))
    return out


def join_lanes(classes):
    shape = classes[0].shape
    lane = iota(shape, 1)
    block = lane >> 5
    turned = [cl if p == 0 else pltpu.roll(cl, 32 * p, 1) for p, cl in enumerate(classes)]
    out = []
    for c in range(4):
        mixed = turned[(3 - c) % 4]
        for b in range(3):
            mixed = jnp.where(block == b, turned[(b - c) % 4], mixed)
        source = (((lane + c) & 3) << 5) + (lane >> 2)
        out.append(jnp.take_along_axis(mixed, source, axis=1, mode="promise_in_bounds"))
    return out


def harmonic(a, b, scale):
    return scale * 2.0 * a * b / (a + b)


def level_weights(mid, west, east, open_west, open_east, scale):
    count = len(mid)
    lane = iota(mid[0].shape, 1)
    w_west = [jnp.where(open_west, harmonic(a, b, scale), 0.0) for a, b in zip(mid, west)]
    w_east = [jnp.where(open_east, harmonic(a, b, scale), 0.0) for a, b in zip(mid, east)]
    w_north = [harmonic(mid[p], mid[p + 1], scale) for p in range(count - 1)]
    last = harmonic(mid[count - 1], pltpu.roll(mid[0], 127, 1), scale)
    w_north.append(jnp.where(lane < 127, last, 0.0))
    w_south = [pltpu.roll(w_north[count - 1], 1, 1)] + w_north[:-1]
    out = []
    for p in range(count):
        w_z = (scale * ANISOTROPY) / mid[p]
        low = w_west[p] + w_east[p] + w_south[p] + w_north[p] + w_z
        full = low + w_z
        c = DAMPING / full
        out.append(
            (c, c * w_west[p], c * w_east[p], c * w_south[p], c * w_north[p], c * w_z, full / low, low / full, full / DAMPING)
        )
    return out


def terrain_weights(mid, west, east, open_west, open_east):
    lane = iota(mid[0].shape, 1)

    def share(own, other):
        both = own + other
        return 2.0 * other * other / (both * both)

    out = []
    for p in range(4):
        south = mid[p - 1] if p else pltpu.roll(mid[3], 1, 1)
        north = mid[p + 1] if p < 3 else pltpu.roll(mid[0], 127, 1)
        g_south, g_north = share(mid[p], south), share(mid[p], north)
        out.append(
            (
                jnp.where(open_west, share(mid[p], west[p]), 0.0),
                jnp.where(open_east, share(mid[p], east[p]), 0.0),
                g_south if p else jnp.where(lane > 0, g_south, 0.0),
                g_north if p < 3 else jnp.where(lane < 127, g_north, 0.0),
                -ANISOTROPY / (mid[p] * mid[p]),
            )
        )
    return out


def north_of(v, q, p):
    return v[q][p + 1] if p + 1 < len(v[q]) else pltpu.roll(v[q][0], 127, 1)


def south_of(v, q, p):
    return v[q][p - 1] if p else pltpu.roll(v[q][-1], 1, 1)


def above(v, q, p, top):
    return v[q + 1][p] if q + 1 < len(v) else jnp.where(top, 0.0, pltpu.roll(v[0][p], 7, 0))


def below(v, q, p, bottom):
    return v[q - 1][p] if q else jnp.where(bottom, 0.0, pltpu.roll(v[-1][p], 1, 0))


def around(v, v_west, v_east, w, bottom, top):
    out = []
    for q in range(len(v)):
        line = []
        for p in range(len(v[q])):
            total = w(CZ, p) * (above(v, q, p, top) + below(v, q, p, bottom))
            total = total + w(CS, p) * south_of(v, q, p) + w(CN, p) * north_of(v, q, p)
            if v_west is not None:
                total = total + w(CW, p) * v_west[q][p]
            if v_east is not None:
                total = total + w(CE, p) * v_east[q][p]
            line.append(total)
        out.append(line)
    return out


def swept(v, v_west, v_east, start, w, bottom, top):
    near = around(v, v_west, v_east, w, bottom, top)
    out = []
    for q in range(len(v)):
        line = []
        for p in range(len(v[q])):
            move = near[q][p] if q else near[q][p] * jnp.where(bottom, w(RHO, p), 1.0)
            line.append((1.0 - DAMPING) * v[q][p] + start[q][p] + move)
        out.append(line)
    return out


def restricted(v, v_west, v_east, start, w, bottom, top):
    near = around(v, v_west, v_east, w, bottom, top)
    half = len(v) // 2
    out = [[0.0] * half for _ in range(half)]
    for q1 in range(half):
        for p in range(len(v)):
            part = 0.0
            for q in (2 * q1, 2 * q1 + 1):
                own = -DAMPING * v[q][p] if start is None else start[q][p] - DAMPING * v[q][p]
                if q == 0:
                    own = own * jnp.where(bottom, w(SIG, p), 1.0)
                part = part + (near[q][p] + own)
            out[q1][p // 2] = out[q1][p // 2] + w(DINV, p) * part
    return out


def edge_restricted(v, kind, w):
    half = len(v) // 2
    return [
        [sum((w(DINV, p) * w(kind, p)) * (v[2 * q1][p] + v[2 * q1 + 1][p]) for p in (2 * p1, 2 * p1 + 1)) for p1 in range(half)]
        for q1 in range(half)
    ]


def edge_swept(v, kind, w, bottom):
    return [
        [w(kind, p) * (v[q][p] if q else v[q][p] * jnp.where(bottom, w(RHO, p), 1.0)) for p in range(len(v[q]))]
        for q in range(len(v))
    ]


def added(a, b):
    return [[s + t for s, t in zip(x, y)] for x, y in zip(a, b)]


def first_guess(f, w, bottom):
    return [
        [w(C, p) * (f[q][p] if q else f[q][p] * jnp.where(bottom, w(RHO, p), 1.0)) for p in range(len(f[q]))]
        for q in range(len(f))
    ]


def grid_of(block, count):
    return [[block[q * count + p] for p in range(count)] for q in range(count)]


def table(ref, row):
    @functools.cache
    def weight(kind, p):
        return ref[kind, p, pl.ds(row, 1), :]

    return weight


def put_row(ref, row, tiles):
    count = len(tiles)
    for q in range(count):
        for p in range(count):
            ref[row, q * count + p] = tiles[q][p]


def kernel(
    n_dir, n_gx,
    cot, pot, height, adjoint, gradient,
    h_in, c_in, p_in, a_out, mixed,
    hs, fs, ps, ds, w0, de, d1, w1, df, d2s, d2, w2,
    v0, v1, v2, v3,
    packet, from_west, from_east, from_west2, from_east2, from_west3, from_east3, f2own, f2r, f1, u0, u1, u2, u3,
    gn, er,
    local_sem, send_sem, recv_sem,
):
    me_dir, me = lax.axis_index("dir"), lax.axis_index("gx")

    def strip(offset):
        return {"gx": lax.rem(me + offset + 9 * n_gx, n_gx)}

    barrier = pltpu.get_barrier_semaphore()
    greeted = [o for s in range(1, GREET + 1) for o in (-s, s)]
    for offset in greeted:
        pl.semaphore_signal(barrier, inc=1, device_id=strip(offset), device_id_type=MESH)
    for step in range(1, n_dir):
        pl.semaphore_signal(
            barrier, inc=1, device_id={"dir": lax.rem(me_dir + step, n_dir)}, device_id_type=MESH
        )

    height_in = pltpu.make_async_copy(height, h_in, local_sem.at[0])
    cot_in = pltpu.make_async_copy(cot.at[0], c_in, local_sem.at[1])
    pot_in = pltpu.make_async_copy(pot.at[0], p_in, local_sem.at[2])
    height_in.start()
    cot_in.start()
    pot_in.start()

    sent = []

    def send(source, target, device):
        index = len(sent)
        copy = pltpu.make_async_remote_copy(
            src_ref=source, dst_ref=target, send_sem=send_sem.at[index], recv_sem=recv_sem.at[index],
            device_id=device, device_id_type=MESH,
        )
        copy.start()
        sent.append(copy)
        return copy

    bottom, top = iota((8, 128), 0) == 0, iota((8, 128), 0) == 7

    for p in range(4):
        ds[p, 24:32, :] = jnp.ones((8, 128), jnp.float32)
    d2[...] = jnp.ones(d2.shape, jnp.float32)
    d1[...] = jnp.ones(d1.shape, jnp.float32)

    height_in.wait()
    raw = h_in[...]
    for p, cl in enumerate(spread_lanes([raw[:, 128 * c : 128 * c + 128] for c in range(4)])):
        hs[3, 4 * p : 4 * p + 4, :] = CEILING - cl

    pl.semaphore_wait(barrier, len(greeted) + n_dir - 1)
    depth_copies = [send(hs.at[3], hs.at[3 - o], strip(o)) for o in (-1, 1, -2, 2, -3, 3)]

    def spread_row(source, target, row, slot):
        block = source[row]
        for p, cl in enumerate(spread_lanes([block[:, 128 * c : 128 * c + 128] for c in range(4)])):
            target[slot, p] = cl

    cot_in.wait()
    for x in range(0, 4):
        spread_row(c_in, fs, x, x + 4)
    field_copies = [
        send(fs.at[pl.ds(4, 4)], fs.at[pl.ds(4 - 4 * o, 4)], strip(o)) for o in (-1, 1)
    ]

    def field_row(ref, slot):
        return [[ref[slot, p, pl.ds(q, 8, stride=4), :] for p in range(4)] for q in range(4)]

    for copy in depth_copies:
        copy.wait_recv()
    for o in range(7):
        for p in range(4):
            ds[p, 4 * o : 4 * o + 4, :] = hs[o, 4 * p : 4 * p + 4, :]
    for p1 in range(2):
        de[p1] = ds[2 * p1] + ds[2 * p1 + 1]
    for p1 in range(2):
        d1[p1, 0:16, :] = 0.25 * (de[p1, pl.ds(0, 16, stride=2), :] + de[p1, pl.ds(1, 16, stride=2), :])
    df[...] = d1[0] + d1[1]
    d2s[1] = 0.25 * (df[pl.ds(0, 8, stride=2), :] + df[pl.ds(1, 8, stride=2), :])
    d2_copies = [send(d2s.at[1], d2s.at[1 - s], strip(7 * s)) for s in (-1, 1)]

    def faces(rows, per_strip, first):
        size = n_gx * per_strip
        place = (me * per_strip + first + REACH * size + iota((rows, 128), 0)) & (size - 1)
        return place != 0, place != size - 1

    open_west, open_east = faces(16, 4, -4)
    mid = [ds[p, 8:24, :] for p in range(4)]
    west = [ds[p, 7:23, :] for p in range(4)]
    east = [ds[p, 9:25, :] for p in range(4)]
    for p, kinds in enumerate(level_weights(mid, west, east, open_west, open_east, 1.0)):
        for kind, value in enumerate(kinds):
            w0[kind, p] = value
    open_west, open_east = faces(16, 2, -5)
    mid1 = [d1[p, 1:17, :] for p in range(2)]
    west1 = [d1[p, 0:16, :] for p in range(2)]
    east1 = [d1[p, 2:18, :] for p in range(2)]
    for p, kinds in enumerate(level_weights(mid1, west1, east1, open_west, open_east, 2.0)):
        for kind, value in enumerate(kinds):
            w1[kind, p] = value

    def guess_row(i):
        put_row(v0, i, first_guess(field_row(fs, i), table(w0, i), bottom))

    def row_of(ref, i, count=4):
        return grid_of(ref[i], count)

    def smooth_rows(source, target, low, high):
        have = {i: row_of(source, i) for i in range(low - 1, high + 1)}
        for i in range(low, high):
            put_row(target, i, swept(have[i], have[i - 1], have[i + 1], row_of(v0, i), table(w0, i), bottom, top))

    for i in range(4, 8):
        guess_row(i)
    have = [None] + [row_of(v0, i) for i in range(4, 8)] + [None]
    put_row(v1, 3, edge_swept(have[1], CE, table(w0, 3), bottom))
    for i in range(4, 8):
        put_row(v1, i, swept(have[i - 3], have[i - 4], have[i - 2], have[i - 3], table(w0, i), bottom, top))
    put_row(v1, 8, edge_swept(have[4], CW, table(w0, 8), bottom))
    have = [None] + [row_of(v1, i) for i in range(3, 9)] + [None]
    rest = {i: restricted(have[i - 2], have[i - 3], have[i - 1], row_of(v0, i) if 4 <= i <= 7 else None, table(w0, i), bottom, top) for i in range(3, 9)}
    rest[2] = edge_restricted(have[1], CE, table(w0, 2))
    rest[9] = edge_restricted(have[6], CW, table(w0, 9))
    f1p = [added(rest[2 * i + 2], rest[2 * i + 3]) for i in range(4)]
    for q in range(2):
        for p in range(2):
            packet[2 * q + p] = f1p[0][q][p]
            packet[9 + 2 * q + p] = f1p[3][q][p]

    begin = {i: first_guess(f1p[i - 4], table(w1, i), bottom) for i in range(4, 8)}
    next_row = {i: swept(begin[i], begin.get(i - 1), begin.get(i + 1), begin[i], table(w1, i), bottom, top) for i in range(4, 8)}
    next_row[3] = edge_swept(begin[4], CE, table(w1, 3), bottom)
    next_row[8] = edge_swept(begin[7], CW, table(w1, 8), bottom)
    rest = {
        i: restricted(next_row[i], next_row.get(i - 1), next_row.get(i + 1), begin.get(i), table(w1, i), bottom, top)
        for i in range(3, 9)
    }
    rest[2] = edge_restricted(next_row[3], CE, table(w1, 2))
    rest[9] = edge_restricted(next_row[8], CW, table(w1, 9))
    f2p = [sum(rest[i][0][0] for i in rows) for rows in ((2,), (3, 4), (5, 6), (7, 8), (9,))]
    for k in range(5):
        packet[4 + k] = f2p[k]
    sum_copies = [
        send(packet.at[pl.ds(0, 7)], from_east, strip(-1)),
        send(packet.at[pl.ds(6, 7)], from_west, strip(1)),
        send(packet.at[pl.ds(4, 2)], from_east2, strip(-2)),
        send(packet.at[pl.ds(7, 2)], from_west2, strip(2)),
        send(packet.at[4], from_east3.at[0], strip(-3)),
        send(packet.at[8], from_west3.at[0], strip(3)),
    ]

    pot_in.wait()
    for x in range(0, 4):
        spread_row(p_in, ps, x, x + 1)
    potential_copies = [send(ps.at[1], ps.at[5], strip(-1)), send(ps.at[4], ps.at[0], strip(1))]

    for copy in d2_copies:
        copy.wait_recv()
    d2[0:8, :] = d2s[0]
    d2[7:15, :] = d2s[1]
    d2[14:22, :] = d2s[2]
    open_west, open_east = faces(24, 1, -9)
    for kind, value in enumerate(
        level_weights([d2[1:25, :]], [d2[0:24, :]], [d2[2:26, :]], open_west, open_east, 4.0)[0]
    ):
        w2[kind, 0] = value

    for copy in sum_copies:
        copy.wait_recv()
    f2own[0] = (f2p[1] + from_west[0]) + (from_east[4] + from_west2[0]) + from_west3[0]
    f2own[1] = (f2p[2] + from_west[1]) + (from_east[5] + from_west2[1]) + from_east2[0]
    f2own[2] = (f2p[3] + from_west[2]) + (from_east[6] + from_east2[1]) + from_east3[0]
    slots = (-9, -6, -3, 3, 6, 9)
    row_copies = [send(f2own, f2r.at[slots.index(-o)], strip(o)) for o in (-9, 9, -6, 6, -3, 3)]
    for q in range(2):
        for p in range(2):
            f1[6, 2 * q + p] = f1p[1][q][p] + from_west[3 + 2 * q + p]
            f1[7, 2 * q + p] = f1p[2][q][p] + from_east[2 * q + p]
    f1_copies = [send(f1.at[pl.ds(6, 2)], f1.at[pl.ds(6 - 2 * o, 2)], strip(o)) for o in (-1, 1, -2, 2)]
    f1_copies += [send(f1.at[6], f1.at[12], strip(-3)), send(f1.at[7], f1.at[1], strip(3))]

    terrain = terrain_weights(
        [ds[p, 8:24, :] for p in range(4)], [ds[p, 7:23, :] for p in range(4)], [ds[p, 9:25, :] for p in range(4)],
        *faces(16, 4, -4),
    )
    for p, kinds in enumerate(terrain):
        for kind, value in enumerate(kinds):
            w0[GW + kind, p] = value
    for copy in field_copies:
        copy.wait_recv()
    for i in range(0, 4):
        guess_row(i)
    for i in range(8, 12):
        guess_row(i)
    smooth_rows(v0, v1, 1, 11)

    for copy in f1_copies:
        copy.wait_recv()
    for i in range(0, 12):
        put_row(u0, i, first_guess(grid_of(f1[i + 1], 2), table(w1, i), bottom))
    for i in range(1, 11):
        rows = [row_of(u0, i + d, 2) for d in (0, -1, 1)]
        put_row(u1, i, swept(*rows, row_of(u0, i, 2), table(w1, i), bottom, top))

    for copy in row_copies:
        copy.wait_recv()
    start = []
    for o in range(-REACH, REACH + 1):
        block = (o + 10) // 3 * 3 - 9
        source = f2own[o + 1] if block == 0 else f2r[slots.index(block), o - block + 1]
        start.append(first_guess([[source]], table(w2, o + REACH), bottom))
    now = start
    for sweep in range(7):
        later = [None] * len(now)
        for i in range(sweep + 1, len(now) - sweep - 1):
            later[i] = swept(now[i], now[i - 1], now[i + 1], start[i], table(w2, i), bottom, top)
        now = later

    for i in range(1, 11):
        fix = now[(i - 5) // 2 + REACH][0][0]
        put_row(u1, i, [[t + fix for t in line] for line in row_of(u1, i, 2)])
    for source, target, low, high in ((u1, u2, 2, 10), (u2, u3, 3, 9)):
        for i in range(low, high):
            rows = [row_of(source, i + d, 2) for d in (0, -1, 1)]
            put_row(target, i, swept(*rows, row_of(u0, i, 2), table(w1, i), bottom, top))

    def corrected_row(i):
        fix = row_of(u3, (i - 4 + 8) // 2 + 1, 2)
        now_row = row_of(v1, i)
        put_row(v1, i, [[now_row[q][p] + fix[q // 2][p // 2] for p in range(4)] for q in range(4)])

    for i in range(1, 11):
        corrected_row(i)
    smooth_rows(v1, v2, 2, 10)
    smooth_rows(v2, v3, 3, 9)

    for copy in potential_copies:
        copy.wait_recv()

    def terrain_row(x):
        w = table(w0, x + 4)
        a, a_west, a_east = (row_of(v3, x + 4 + d) for d in (0, -1, 1))
        b, b_west, b_east = (field_row(ps, x + 1 + d) for d in (0, -1, 1))
        zeros = jnp.zeros((8, 128), jnp.float32)
        by_z, by_west, by_east, by_north = ([zeros] * 4 for _ in range(4))
        for q in range(4):
            for p in range(4):
                by_z[p] += (above(a, q, p, top) - a[q][p]) * (above(b, q, p, top) - b[q][p])
                by_west[p] += (a[q][p] - a_west[q][p]) * (b[q][p] - b_west[q][p])
                by_east[p] += (a_east[q][p] - a[q][p]) * (b_east[q][p] - b[q][p])
                by_north[p] += (north_of(a, q, p) - a[q][p]) * (north_of(b, q, p) - b[q][p])
        out = []
        for p in range(4):
            by_south = by_north[p - 1] if p else pltpu.roll(by_north[3], 1, 1)
            total = w(GW, p) * by_west[p] + w(GE, p) * by_east[p] + w(GN, p) * by_north[p]
            total = total + w(GS, p) * by_south + w(GZ, p) * by_z[p]
            out.append(jnp.sum(total, axis=0, keepdims=True))
        return out

    sums = [terrain_row(x) for x in range(4)]
    blank = jnp.zeros((4, 128), jnp.float32)
    packed = [jnp.concatenate([sums[x][p] for x in range(4)] + [blank], axis=0) for p in range(4)]
    for c, tile in enumerate(join_lanes(packed)):
        gn[c] = tile
    dir_copies = []
    for step in range(1, n_dir):
        target = lax.rem(me_dir + step, n_dir)
        dir_copies.append(send(gn.at[target // (n_dir // 4)], er.at[step - 1], {"dir": target}))

    def natural_row(x):
        now_row = row_of(v3, x + 4)
        for p in range(4):
            for q in range(4):
                mixed[x, p, pl.ds(q, 8, stride=4), :] = now_row[q][p]
        for c, tile in enumerate(join_lanes([mixed[x, p] for p in range(4)])):
            a_out[x, :, 128 * c : 128 * c + 128] = tile

    for i in range(0, 4):
        natural_row(i)
    out_copy = pltpu.make_async_copy(a_out, adjoint.at[0], local_sem.at[3])
    out_copy.start()

    for copy in dir_copies:
        copy.wait_recv()
    total = gn[me_dir // (n_dir // 4)]
    for step in range(1, n_dir):
        total = total + er[step - 1]
    part = lax.rem(me_dir, n_dir // 4)
    mine = total
    width = gradient.shape[1]
    for k in range(1, 128 // width):
        mine = jnp.where(iota((8, 128), 0) * 0 + part == k, pltpu.roll(total, 128 - k * width, 1), mine)
    gradient[...] = mine[0:4, 0:width]

    out_copy.wait()
    for copy in sent:
        copy.wait_send()


def body(cotangent, potential, height):
    n_dir, n_gx = lax.axis_size("dir"), lax.axis_size("gx")
    f32 = jnp.float32
    shapes = [
        (4, 512), (4, 32, 512), (4, 32, 512), (4, 32, 512), (4, 4, 32, 128),
        (7, 16, 128), (12, 4, 32, 128), (6, 4, 32, 128), (4, 32, 128), (14, 4, 16, 128),
        (2, 32, 128), (2, 24, 128), (9, 2, 16, 128), (24, 128), (3, 8, 128), (32, 128), (9, 1, 24, 128),
        (12, 16, 8, 128), (12, 16, 8, 128), (12, 16, 8, 128), (12, 16, 8, 128),
        (13, 8, 128), (7, 8, 128), (7, 8, 128), (2, 8, 128), (2, 8, 128), (1, 8, 128), (1, 8, 128), (3, 8, 128), (6, 3, 8, 128), (14, 4, 8, 128),
        (12, 4, 8, 128), (12, 4, 8, 128), (12, 4, 8, 128), (12, 4, 8, 128),
        (4, 8, 128), (n_dir - 1, 8, 128),
    ]
    copies = 6 + 2 + 2 + 2 + 6 + 6 + 6 + n_dir - 1
    return pl.pallas_call(
        functools.partial(kernel, n_dir, n_gx),
        out_shape=(
            pltpu.VMEM(cotangent.shape, f32),
            pltpu.VMEM((height.shape[0], height.shape[1] // n_dir), f32),
        ),
        in_specs=[pl.BlockSpec(memory_space=pltpu.HBM)] * 3,
        out_specs=(pl.BlockSpec(memory_space=pl.ANY), pl.BlockSpec(memory_space=pltpu.VMEM)),
        scratch_shapes=[pltpu.VMEM(shape, f32) for shape in shapes]
        + [pltpu.SemaphoreType.DMA((4,)), pltpu.SemaphoreType.DMA((copies,)), pltpu.SemaphoreType.DMA((copies,))],
        compiler_params=pltpu.CompilerParams(
            collective_id=0, has_side_effects=True, vmem_limit_bytes=60 * 1024 * 1024
        ),
        name="vcycle",
    )(cotangent, potential, height)


def solution(mesh):
    placed = (P("dir", "gx", None, None), P("dir", "gx", None, None), P("gx", None))
    return jax.shard_map(
        body,
        mesh=mesh,
        in_specs=placed,
        out_specs=(P("dir", "gx", None, None), P("gx", "dir")),
        check_vma=False,
    )
```

```python
import functools

import jax
import jax.numpy as jnp
from jax import lax
from jax.experimental import pallas as pl
from jax.experimental.pallas import tpu as pltpu
from jax.sharding import PartitionSpec as P

MESH = pl.DeviceIdType.MESH
DAMPING = 0.7
ANISOTROPY = 4.0
CEILING = 1.5
REACH = 9
GREET = 4
C, CW, CE, CS, CN, CZ, RHO, SIG, DINV = range(9)
GW, GE, GS, GN, GZ = range(9, 14)


def iota(shape, dim):
    return lax.broadcasted_iota(jnp.int32, shape, dim)


def spread_lanes(cols):
    shape = cols[0].shape
    lane = iota(shape, 1)
    block, inner = lane >> 5, lane & 31
    turned = [
        jnp.take_along_axis(col, 4 * inner + ((block - c) & 3), axis=1, mode="promise_in_bounds")
        for c, col in enumerate(cols)
    ]
    out = []
    for p in range(4):
        mixed = turned[(3 - p) % 4]
        for b in range(3):
            mixed = jnp.where(block == b, turned[(b - p) % 4], mixed)
        out.append(mixed if p == 0 else pltpu.roll(mixed, 128 - 32 * p, 1))
    return out


def join_lanes(classes):
    shape = classes[0].shape
    lane = iota(shape, 1)
    block = lane >> 5
    turned = [cl if p == 0 else pltpu.roll(cl, 32 * p, 1) for p, cl in enumerate(classes)]
    out = []
    for c in range(4):
        mixed = turned[(3 - c) % 4]
        for b in range(3):
            mixed = jnp.where(block == b, turned[(b - c) % 4], mixed)
        source = (((lane + c) & 3) << 5) + (lane >> 2)
        out.append(jnp.take_along_axis(mixed, source, axis=1, mode="promise_in_bounds"))
    return out


def harmonic(a, b, scale):
    return scale * 2.0 * a * b / (a + b)


def level_weights(mid, west, east, open_west, open_east, scale):
    count = len(mid)
    lane = iota(mid[0].shape, 1)
    w_west = [jnp.where(open_west, harmonic(a, b, scale), 0.0) for a, b in zip(mid, west)]
    w_east = [jnp.where(open_east, harmonic(a, b, scale), 0.0) for a, b in zip(mid, east)]
    w_north = [harmonic(mid[p], mid[p + 1], scale) for p in range(count - 1)]
    last = harmonic(mid[count - 1], pltpu.roll(mid[0], 127, 1), scale)
    w_north.append(jnp.where(lane < 127, last, 0.0))
    w_south = [pltpu.roll(w_north[count - 1], 1, 1)] + w_north[:-1]
    out = []
    for p in range(count):
        w_z = (scale * ANISOTROPY) / mid[p]
        low = w_west[p] + w_east[p] + w_south[p] + w_north[p] + w_z
        full = low + w_z
        c = DAMPING / full
        out.append(
            (c, c * w_west[p], c * w_east[p], c * w_south[p], c * w_north[p], c * w_z, full / low, low / full, full / DAMPING)
        )
    return out


def terrain_weights(mid, west, east, open_west, open_east):
    lane = iota(mid[0].shape, 1)

    def share(own, other):
        both = own + other
        return 2.0 * other * other / (both * both)

    out = []
    for p in range(4):
        south = mid[p - 1] if p else pltpu.roll(mid[3], 1, 1)
        north = mid[p + 1] if p < 3 else pltpu.roll(mid[0], 127, 1)
        g_south, g_north = share(mid[p], south), share(mid[p], north)
        out.append(
            (
                jnp.where(open_west, share(mid[p], west[p]), 0.0),
                jnp.where(open_east, share(mid[p], east[p]), 0.0),
                g_south if p else jnp.where(lane > 0, g_south, 0.0),
                g_north if p < 3 else jnp.where(lane < 127, g_north, 0.0),
                -ANISOTROPY / (mid[p] * mid[p]),
            )
        )
    return out


def north_of(v, q, p):
    return v[q][p + 1] if p + 1 < len(v[q]) else pltpu.roll(v[q][0], 127, 1)


def south_of(v, q, p):
    return v[q][p - 1] if p else pltpu.roll(v[q][-1], 1, 1)


def above(v, q, p, top):
    return v[q + 1][p] if q + 1 < len(v) else jnp.where(top, 0.0, pltpu.roll(v[0][p], 7, 0))


def below(v, q, p, bottom):
    return v[q - 1][p] if q else jnp.where(bottom, 0.0, pltpu.roll(v[-1][p], 1, 0))


def around(v, v_west, v_east, w, bottom, top):
    out = []
    for q in range(len(v)):
        line = []
        for p in range(len(v[q])):
            total = w(CZ, p) * (above(v, q, p, top) + below(v, q, p, bottom))
            total = total + w(CS, p) * south_of(v, q, p) + w(CN, p) * north_of(v, q, p)
            if v_west is not None:
                total = total + w(CW, p) * v_west[q][p]
            if v_east is not None:
                total = total + w(CE, p) * v_east[q][p]
            line.append(total)
        out.append(line)
    return out


def swept(v, v_west, v_east, start, w, bottom, top):
    near = around(v, v_west, v_east, w, bottom, top)
    out = []
    for q in range(len(v)):
        line = []
        for p in range(len(v[q])):
            move = near[q][p] if q else near[q][p] * jnp.where(bottom, w(RHO, p), 1.0)
            line.append((1.0 - DAMPING) * v[q][p] + start[q][p] + move)
        out.append(line)
    return out


def restricted(v, v_west, v_east, start, w, bottom, top):
    near = around(v, v_west, v_east, w, bottom, top)
    half = len(v) // 2
    out = [[0.0] * half for _ in range(half)]
    for q1 in range(half):
        for p in range(len(v)):
            part = 0.0
            for q in (2 * q1, 2 * q1 + 1):
                own = -DAMPING * v[q][p] if start is None else start[q][p] - DAMPING * v[q][p]
                if q == 0:
                    own = own * jnp.where(bottom, w(SIG, p), 1.0)
                part = part + (near[q][p] + own)
            out[q1][p // 2] = out[q1][p // 2] + w(DINV, p) * part
    return out


def edge_restricted(v, kind, w):
    half = len(v) // 2
    return [
        [sum((w(DINV, p) * w(kind, p)) * (v[2 * q1][p] + v[2 * q1 + 1][p]) for p in (2 * p1, 2 * p1 + 1)) for p1 in range(half)]
        for q1 in range(half)
    ]


def edge_swept(v, kind, w, bottom):
    return [
        [w(kind, p) * (v[q][p] if q else v[q][p] * jnp.where(bottom, w(RHO, p), 1.0)) for p in range(len(v[q]))]
        for q in range(len(v))
    ]


def added(a, b):
    return [[s + t for s, t in zip(x, y)] for x, y in zip(a, b)]


def first_guess(f, w, bottom):
    return [
        [w(C, p) * (f[q][p] if q else f[q][p] * jnp.where(bottom, w(RHO, p), 1.0)) for p in range(len(f[q]))]
        for q in range(len(f))
    ]


def grid_of(block, count):
    return [[block[q * count + p] for p in range(count)] for q in range(count)]


def table(ref, row):
    @functools.cache
    def weight(kind, p):
        return ref[kind, p, pl.ds(row, 1), :]

    return weight


def put_row(ref, row, tiles):
    count = len(tiles)
    for q in range(count):
        for p in range(count):
            ref[row, q * count + p] = tiles[q][p]


def kernel(
    n_dir, n_gx,
    cot, pot, height, adjoint, gradient,
    h_in, c_in, p_in, a_out, mixed,
    hs, fs, ps, ds, w0, de, d1, w1, df, d2s, d2, w2,
    v0, v1, v2, v3,
    packet, from_west, from_east, from_west2, from_east2, from_west3, from_east3, f2own, f2r, f1, u0, u1, u2, u3,
    gn, er,
    local_sem, send_sem, recv_sem,
):
    me_dir, me = lax.axis_index("dir"), lax.axis_index("gx")

    def strip(offset):
        return {"gx": lax.rem(me + offset + 9 * n_gx, n_gx)}

    barrier = pltpu.get_barrier_semaphore()
    greeted = [o for s in range(1, GREET + 1) for o in (-s, s)]
    for offset in greeted:
        pl.semaphore_signal(barrier, inc=1, device_id=strip(offset), device_id_type=MESH)
    for step in range(1, n_dir):
        pl.semaphore_signal(
            barrier, inc=1, device_id={"dir": lax.rem(me_dir + step, n_dir)}, device_id_type=MESH
        )

    height_in = pltpu.make_async_copy(height, h_in, local_sem.at[0])
    cot_in = pltpu.make_async_copy(cot.at[0], c_in, local_sem.at[1])
    pot_in = pltpu.make_async_copy(pot.at[0], p_in, local_sem.at[2])
    height_in.start()
    cot_in.start()
    pot_in.start()

    sent = []

    def send(source, target, device):
        index = len(sent)
        copy = pltpu.make_async_remote_copy(
            src_ref=source, dst_ref=target, send_sem=send_sem.at[index], recv_sem=recv_sem.at[index],
            device_id=device, device_id_type=MESH,
        )
        copy.start()
        sent.append(copy)
        return copy

    bottom, top = iota((8, 128), 0) == 0, iota((8, 128), 0) == 7

    for p in range(4):
        ds[p, 24:32, :] = jnp.ones((8, 128), jnp.float32)
    d2[...] = jnp.ones(d2.shape, jnp.float32)
    d1[...] = jnp.ones(d1.shape, jnp.float32)

    height_in.wait()
    raw = h_in[...]
    for p, cl in enumerate(spread_lanes([raw[:, 128 * c : 128 * c + 128] for c in range(4)])):
        hs[3, 4 * p : 4 * p + 4, :] = CEILING - cl

    pl.semaphore_wait(barrier, len(greeted) + n_dir - 1)
    depth_copies = [send(hs.at[3], hs.at[3 - o], strip(o)) for o in (-1, 1, -2, 2, -3, 3)]

    def spread_row(source, target, row, slot):
        block = source[row]
        for p, cl in enumerate(spread_lanes([block[:, 128 * c : 128 * c + 128] for c in range(4)])):
            target[slot, p] = cl

    cot_in.wait()
    for x in range(0, 4):
        spread_row(c_in, fs, x, x + 4)
    field_copies = [
        send(fs.at[pl.ds(4, 4)], fs.at[pl.ds(4 - 4 * o, 4)], strip(o)) for o in (-1, 1)
    ]

    def field_row(ref, slot):
        return [[ref[slot, p, pl.ds(q, 8, stride=4), :] for p in range(4)] for q in range(4)]

    for copy in depth_copies:
        copy.wait_recv()
    for o in range(7):
        for p in range(4):
            ds[p, 4 * o : 4 * o + 4, :] = hs[o, 4 * p : 4 * p + 4, :]
    for p1 in range(2):
        de[p1] = ds[2 * p1] + ds[2 * p1 + 1]
    for p1 in range(2):
        d1[p1, 0:16, :] = 0.25 * (de[p1, pl.ds(0, 16, stride=2), :] + de[p1, pl.ds(1, 16, stride=2), :])
    df[...] = d1[0] + d1[1]
    d2s[1] = 0.25 * (df[pl.ds(0, 8, stride=2), :] + df[pl.ds(1, 8, stride=2), :])
    d2_copies = [send(d2s.at[1], d2s.at[1 - s], strip(7 * s)) for s in (-1, 1)]

    def faces(rows, per_strip, first):
        size = n_gx * per_strip
        place = (me * per_strip + first + REACH * size + iota((rows, 128), 0)) & (size - 1)
        return place != 0, place != size - 1

    open_west, open_east = faces(16, 4, -4)
    mid = [ds[p, 8:24, :] for p in range(4)]
    west = [ds[p, 7:23, :] for p in range(4)]
    east = [ds[p, 9:25, :] for p in range(4)]
    for p, kinds in enumerate(level_weights(mid, west, east, open_west, open_east, 1.0)):
        for kind, value in enumerate(kinds):
            w0[kind, p] = value
    open_west, open_east = faces(16, 2, -5)
    mid1 = [d1[p, 1:17, :] for p in range(2)]
    west1 = [d1[p, 0:16, :] for p in range(2)]
    east1 = [d1[p, 2:18, :] for p in range(2)]
    for p, kinds in enumerate(level_weights(mid1, west1, east1, open_west, open_east, 2.0)):
        for kind, value in enumerate(kinds):
            w1[kind, p] = value

    def guess_row(i):
        put_row(v0, i, first_guess(field_row(fs, i), table(w0, i), bottom))

    def row_of(ref, i, count=4):
        return grid_of(ref[i], count)

    def smooth_rows(source, target, low, high):
        have = {i: row_of(source, i) for i in range(low - 1, high + 1)}
        for i in range(low, high):
            put_row(target, i, swept(have[i], have[i - 1], have[i + 1], row_of(v0, i), table(w0, i), bottom, top))

    for i in range(4, 8):
        guess_row(i)
    have = [None] + [row_of(v0, i) for i in range(4, 8)] + [None]
    put_row(v1, 3, edge_swept(have[1], CE, table(w0, 3), bottom))
    for i in range(4, 8):
        put_row(v1, i, swept(have[i - 3], have[i - 4], have[i - 2], have[i - 3], table(w0, i), bottom, top))
    put_row(v1, 8, edge_swept(have[4], CW, table(w0, 8), bottom))
    have = [None] + [row_of(v1, i) for i in range(3, 9)] + [None]
    rest = {i: restricted(have[i - 2], have[i - 3], have[i - 1], row_of(v0, i) if 4 <= i <= 7 else None, table(w0, i), bottom, top) for i in range(3, 9)}
    rest[2] = edge_restricted(have[1], CE, table(w0, 2))
    rest[9] = edge_restricted(have[6], CW, table(w0, 9))
    f1p = [added(rest[2 * i + 2], rest[2 * i + 3]) for i in range(4)]
    for q in range(2):
        for p in range(2):
            packet[2 * q + p] = f1p[0][q][p]
            packet[9 + 2 * q + p] = f1p[3][q][p]

    begin = {i: first_guess(f1p[i - 4], table(w1, i), bottom) for i in range(4, 8)}
    next_row = {i: swept(begin[i], begin.get(i - 1), begin.get(i + 1), begin[i], table(w1, i), bottom, top) for i in range(4, 8)}
    next_row[3] = edge_swept(begin[4], CE, table(w1, 3), bottom)
    next_row[8] = edge_swept(begin[7], CW, table(w1, 8), bottom)
    rest = {
        i: restricted(next_row[i], next_row.get(i - 1), next_row.get(i + 1), begin.get(i), table(w1, i), bottom, top)
        for i in range(3, 9)
    }
    rest[2] = edge_restricted(next_row[3], CE, table(w1, 2))
    rest[9] = edge_restricted(next_row[8], CW, table(w1, 9))
    f2p = [sum(rest[i][0][0] for i in rows) for rows in ((2,), (3, 4), (5, 6), (7, 8), (9,))]
    for k in range(5):
        packet[4 + k] = f2p[k]
    sum_copies = [
        send(packet.at[pl.ds(0, 7)], from_east, strip(-1)),
        send(packet.at[pl.ds(6, 7)], from_west, strip(1)),
        send(packet.at[pl.ds(4, 2)], from_east2, strip(-2)),
        send(packet.at[pl.ds(7, 2)], from_west2, strip(2)),
        send(packet.at[4], from_east3.at[0], strip(-3)),
        send(packet.at[8], from_west3.at[0], strip(3)),
    ]

    pot_in.wait()
    for x in range(0, 4):
        spread_row(p_in, ps, x, x + 1)

    for copy in d2_copies:
        copy.wait_recv()
    d2[0:8, :] = d2s[0]
    d2[7:15, :] = d2s[1]
    d2[14:22, :] = d2s[2]
    open_west, open_east = faces(24, 1, -9)
    for kind, value in enumerate(
        level_weights([d2[1:25, :]], [d2[0:24, :]], [d2[2:26, :]], open_west, open_east, 4.0)[0]
    ):
        w2[kind, 0] = value

    for copy in sum_copies:
        copy.wait_recv()
    f2own[0] = (f2p[1] + from_west[0]) + (from_east[4] + from_west2[0]) + from_west3[0]
    f2own[1] = (f2p[2] + from_west[1]) + (from_east[5] + from_west2[1]) + from_east2[0]
    f2own[2] = (f2p[3] + from_west[2]) + (from_east[6] + from_east2[1]) + from_east3[0]
    slots = (-9, -6, -3, 3, 6, 9)
    row_copies = [send(f2own, f2r.at[slots.index(-o)], strip(o)) for o in (-9, 9, -6, 6, -3, 3)]
    for q in range(2):
        for p in range(2):
            f1[6, 2 * q + p] = f1p[1][q][p] + from_west[3 + 2 * q + p]
            f1[7, 2 * q + p] = f1p[2][q][p] + from_east[2 * q + p]
    f1_copies = [send(f1.at[pl.ds(6, 2)], f1.at[pl.ds(6 - 2 * o, 2)], strip(o)) for o in (-1, 1, -2, 2)]
    f1_copies += [send(f1.at[6], f1.at[12], strip(-3)), send(f1.at[7], f1.at[1], strip(3))]

    potential_copies = [send(ps.at[1], ps.at[5], strip(-1)), send(ps.at[4], ps.at[0], strip(1))]

    terrain = terrain_weights(
        [ds[p, 8:24, :] for p in range(4)], [ds[p, 7:23, :] for p in range(4)], [ds[p, 9:25, :] for p in range(4)],
        *faces(16, 4, -4),
    )
    for p, kinds in enumerate(terrain):
        for kind, value in enumerate(kinds):
            w0[GW + kind, p] = value
    for copy in field_copies:
        copy.wait_recv()
    for i in range(0, 4):
        guess_row(i)
    for i in range(8, 12):
        guess_row(i)
    smooth_rows(v0, v1, 1, 11)

    for copy in row_copies:
        copy.wait_recv()
    start = []
    for o in range(-REACH, REACH + 1):
        block = (o + 10) // 3 * 3 - 9
        source = f2own[o + 1] if block == 0 else f2r[slots.index(block), o - block + 1]
        start.append(first_guess([[source]], table(w2, o + REACH), bottom))
    now = start
    for sweep in range(7):
        later = [None] * len(now)
        for i in range(sweep + 1, len(now) - sweep - 1):
            later[i] = swept(now[i], now[i - 1], now[i + 1], start[i], table(w2, i), bottom, top)
        now = later

    for copy in f1_copies:
        copy.wait_recv()
    for i in range(0, 12):
        put_row(u0, i, first_guess(grid_of(f1[i + 1], 2), table(w1, i), bottom))
    for i in range(1, 11):
        rows = [row_of(u0, i + d, 2) for d in (0, -1, 1)]
        put_row(u1, i, swept(*rows, row_of(u0, i, 2), table(w1, i), bottom, top))
    for i in range(1, 11):
        fix = now[(i - 5) // 2 + REACH][0][0]
        put_row(u1, i, [[t + fix for t in line] for line in row_of(u1, i, 2)])
    for source, target, low, high in ((u1, u2, 2, 10), (u2, u3, 3, 9)):
        for i in range(low, high):
            rows = [row_of(source, i + d, 2) for d in (0, -1, 1)]
            put_row(target, i, swept(*rows, row_of(u0, i, 2), table(w1, i), bottom, top))

    def corrected_row(i):
        fix = row_of(u3, (i - 4 + 8) // 2 + 1, 2)
        now_row = row_of(v1, i)
        put_row(v1, i, [[now_row[q][p] + fix[q // 2][p // 2] for p in range(4)] for q in range(4)])

    for i in range(1, 11):
        corrected_row(i)
    smooth_rows(v1, v2, 2, 10)
    smooth_rows(v2, v3, 3, 9)

    for copy in potential_copies:
        copy.wait_recv()

    def terrain_row(x):
        w = table(w0, x + 4)
        a, a_west, a_east = (row_of(v3, x + 4 + d) for d in (0, -1, 1))
        b, b_west, b_east = (field_row(ps, x + 1 + d) for d in (0, -1, 1))
        zeros = jnp.zeros((8, 128), jnp.float32)
        by_z, by_west, by_east, by_north = ([zeros] * 4 for _ in range(4))
        for q in range(4):
            for p in range(4):
                by_z[p] += (above(a, q, p, top) - a[q][p]) * (above(b, q, p, top) - b[q][p])
                by_west[p] += (a[q][p] - a_west[q][p]) * (b[q][p] - b_west[q][p])
                by_east[p] += (a_east[q][p] - a[q][p]) * (b_east[q][p] - b[q][p])
                by_north[p] += (north_of(a, q, p) - a[q][p]) * (north_of(b, q, p) - b[q][p])
        out = []
        for p in range(4):
            by_south = by_north[p - 1] if p else pltpu.roll(by_north[3], 1, 1)
            total = w(GW, p) * by_west[p] + w(GE, p) * by_east[p] + w(GN, p) * by_north[p]
            total = total + w(GS, p) * by_south + w(GZ, p) * by_z[p]
            out.append(jnp.sum(total, axis=0, keepdims=True))
        return out

    sums = [terrain_row(x) for x in range(4)]
    blank = jnp.zeros((4, 128), jnp.float32)
    packed = [jnp.concatenate([sums[x][p] for x in range(4)] + [blank], axis=0) for p in range(4)]
    for c, tile in enumerate(join_lanes(packed)):
        gn[c] = tile
    dir_copies = []
    for step in range(1, n_dir):
        target = lax.rem(me_dir + step, n_dir)
        dir_copies.append(send(gn.at[target // (n_dir // 4)], er.at[step - 1], {"dir": target}))

    def natural_row(x):
        now_row = row_of(v3, x + 4)
        for p in range(4):
            for q in range(4):
                mixed[x, p, pl.ds(q, 8, stride=4), :] = now_row[q][p]
        for c, tile in enumerate(join_lanes([mixed[x, p] for p in range(4)])):
            a_out[x, :, 128 * c : 128 * c + 128] = tile

    for i in range(0, 4):
        natural_row(i)
    out_copy = pltpu.make_async_copy(a_out, adjoint.at[0], local_sem.at[3])
    out_copy.start()

    for copy in dir_copies:
        copy.wait_recv()
    total = gn[me_dir // (n_dir // 4)]
    for step in range(1, n_dir):
        total = total + er[step - 1]
    part = lax.rem(me_dir, n_dir // 4)
    mine = total
    width = gradient.shape[1]
    for k in range(1, 128 // width):
        mine = jnp.where(iota((8, 128), 0) * 0 + part == k, pltpu.roll(total, 128 - k * width, 1), mine)
    gradient[...] = mine[0:4, 0:width]

    out_copy.wait()
    for copy in sent:
        copy.wait_send()


def body(cotangent, potential, height):
    n_dir, n_gx = lax.axis_size("dir"), lax.axis_size("gx")
    f32 = jnp.float32
    shapes = [
        (4, 512), (4, 32, 512), (4, 32, 512), (4, 32, 512), (4, 4, 32, 128),
        (7, 16, 128), (12, 4, 32, 128), (6, 4, 32, 128), (4, 32, 128), (14, 4, 16, 128),
        (2, 32, 128), (2, 24, 128), (9, 2, 16, 128), (24, 128), (3, 8, 128), (32, 128), (9, 1, 24, 128),
        (12, 16, 8, 128), (12, 16, 8, 128), (12, 16, 8, 128), (12, 16, 8, 128),
        (13, 8, 128), (7, 8, 128), (7, 8, 128), (2, 8, 128), (2, 8, 128), (1, 8, 128), (1, 8, 128), (3, 8, 128), (6, 3, 8, 128), (14, 4, 8, 128),
        (12, 4, 8, 128), (12, 4, 8, 128), (12, 4, 8, 128), (12, 4, 8, 128),
        (4, 8, 128), (n_dir - 1, 8, 128),
    ]
    copies = 6 + 2 + 2 + 2 + 6 + 6 + 6 + n_dir - 1
    return pl.pallas_call(
        functools.partial(kernel, n_dir, n_gx),
        out_shape=(
            pltpu.VMEM(cotangent.shape, f32),
            pltpu.VMEM((height.shape[0], height.shape[1] // n_dir), f32),
        ),
        in_specs=[pl.BlockSpec(memory_space=pltpu.HBM)] * 3,
        out_specs=(pl.BlockSpec(memory_space=pl.ANY), pl.BlockSpec(memory_space=pltpu.VMEM)),
        scratch_shapes=[pltpu.VMEM(shape, f32) for shape in shapes]
        + [pltpu.SemaphoreType.DMA((4,)), pltpu.SemaphoreType.DMA((copies,)), pltpu.SemaphoreType.DMA((copies,))],
        compiler_params=pltpu.CompilerParams(
            collective_id=0, has_side_effects=True, vmem_limit_bytes=60 * 1024 * 1024
        ),
        name="vcycle",
    )(cotangent, potential, height)


def solution(mesh):
    placed = (P("dir", "gx", None, None), P("dir", "gx", None, None), P("gx", None))
    return jax.shard_map(
        body,
        mesh=mesh,
        in_specs=placed,
        out_specs=(P("dir", "gx", None, None), P("gx", "dir")),
        check_vma=False,
    )
```

```python
import functools

import jax
import jax.numpy as jnp
from jax import lax
from jax.experimental import pallas as pl
from jax.experimental.pallas import tpu as pltpu
from jax.sharding import PartitionSpec as P

MESH = pl.DeviceIdType.MESH
DAMPING = 0.7
ANISOTROPY = 4.0
CEILING = 1.5
REACH = 9
GREET = 4
C, CW, CE, CS, CN, CZ, RHO, SIG, DINV = range(9)
GW, GE, GS, GN, GZ = range(9, 14)


def iota(shape, dim):
    return lax.broadcasted_iota(jnp.int32, shape, dim)


def spread_lanes(cols):
    shape = cols[0].shape
    lane = iota(shape, 1)
    block, inner = lane >> 5, lane & 31
    turned = [
        jnp.take_along_axis(col, 4 * inner + ((block - c) & 3), axis=1, mode="promise_in_bounds")
        for c, col in enumerate(cols)
    ]
    out = []
    for p in range(4):
        mixed = turned[(3 - p) % 4]
        for b in range(3):
            mixed = jnp.where(block == b, turned[(b - p) % 4], mixed)
        out.append(mixed if p == 0 else pltpu.roll(mixed, 128 - 32 * p, 1))
    return out


def join_lanes(classes):
    shape = classes[0].shape
    lane = iota(shape, 1)
    block = lane >> 5
    turned = [cl if p == 0 else pltpu.roll(cl, 32 * p, 1) for p, cl in enumerate(classes)]
    out = []
    for c in range(4):
        mixed = turned[(3 - c) % 4]
        for b in range(3):
            mixed = jnp.where(block == b, turned[(b - c) % 4], mixed)
        source = (((lane + c) & 3) << 5) + (lane >> 2)
        out.append(jnp.take_along_axis(mixed, source, axis=1, mode="promise_in_bounds"))
    return out


def harmonic(a, b, scale):
    return scale * 2.0 * a * b / (a + b)


def level_weights(mid, west, east, open_west, open_east, scale):
    count = len(mid)
    lane = iota(mid[0].shape, 1)
    w_west = [jnp.where(open_west, harmonic(a, b, scale), 0.0) for a, b in zip(mid, west)]
    w_east = [jnp.where(open_east, harmonic(a, b, scale), 0.0) for a, b in zip(mid, east)]
    w_north = [harmonic(mid[p], mid[p + 1], scale) for p in range(count - 1)]
    last = harmonic(mid[count - 1], pltpu.roll(mid[0], 127, 1), scale)
    w_north.append(jnp.where(lane < 127, last, 0.0))
    w_south = [pltpu.roll(w_north[count - 1], 1, 1)] + w_north[:-1]
    out = []
    for p in range(count):
        w_z = (scale * ANISOTROPY) / mid[p]
        low = w_west[p] + w_east[p] + w_south[p] + w_north[p] + w_z
        full = low + w_z
        c = DAMPING / full
        out.append(
            (c, c * w_west[p], c * w_east[p], c * w_south[p], c * w_north[p], c * w_z, full / low, low / full, full / DAMPING)
        )
    return out


def terrain_weights(mid, west, east, open_west, open_east):
    lane = iota(mid[0].shape, 1)

    def share(own, other):
        both = own + other
        return 2.0 * other * other / (both * both)

    out = []
    for p in range(4):
        south = mid[p - 1] if p else pltpu.roll(mid[3], 1, 1)
        north = mid[p + 1] if p < 3 else pltpu.roll(mid[0], 127, 1)
        g_south, g_north = share(mid[p], south), share(mid[p], north)
        out.append(
            (
                jnp.where(open_west, share(mid[p], west[p]), 0.0),
                jnp.where(open_east, share(mid[p], east[p]), 0.0),
                g_south if p else jnp.where(lane > 0, g_south, 0.0),
                g_north if p < 3 else jnp.where(lane < 127, g_north, 0.0),
                -ANISOTROPY / (mid[p] * mid[p]),
            )
        )
    return out


def north_of(v, q, p):
    return v[q][p + 1] if p + 1 < len(v[q]) else pltpu.roll(v[q][0], 127, 1)


def south_of(v, q, p):
    return v[q][p - 1] if p else pltpu.roll(v[q][-1], 1, 1)


def above(v, q, p, top):
    return v[q + 1][p] if q + 1 < len(v) else jnp.where(top, 0.0, pltpu.roll(v[0][p], 7, 0))


def below(v, q, p, bottom):
    return v[q - 1][p] if q else jnp.where(bottom, 0.0, pltpu.roll(v[-1][p], 1, 0))


def around(v, v_west, v_east, w, bottom, top):
    out = []
    for q in range(len(v)):
        line = []
        for p in range(len(v[q])):
            total = w(CZ, p) * (above(v, q, p, top) + below(v, q, p, bottom))
            total = total + w(CS, p) * south_of(v, q, p) + w(CN, p) * north_of(v, q, p)
            if v_west is not None:
                total = total + w(CW, p) * v_west[q][p]
            if v_east is not None:
                total = total + w(CE, p) * v_east[q][p]
            line.append(total)
        out.append(line)
    return out


def swept(v, v_west, v_east, start, w, bottom, top):
    near = around(v, v_west, v_east, w, bottom, top)
    out = []
    for q in range(len(v)):
        line = []
        for p in range(len(v[q])):
            move = near[q][p] if q else near[q][p] * jnp.where(bottom, w(RHO, p), 1.0)
            line.append((1.0 - DAMPING) * v[q][p] + start[q][p] + move)
        out.append(line)
    return out


def restricted(v, v_west, v_east, start, w, bottom, top):
    near = around(v, v_west, v_east, w, bottom, top)
    half = len(v) // 2
    out = [[0.0] * half for _ in range(half)]
    for q1 in range(half):
        for p in range(len(v)):
            part = 0.0
            for q in (2 * q1, 2 * q1 + 1):
                own = -DAMPING * v[q][p] if start is None else start[q][p] - DAMPING * v[q][p]
                if q == 0:
                    own = own * jnp.where(bottom, w(SIG, p), 1.0)
                part = part + (near[q][p] + own)
            out[q1][p // 2] = out[q1][p // 2] + w(DINV, p) * part
    return out


def edge_restricted(v, kind, w):
    half = len(v) // 2
    return [
        [sum((w(DINV, p) * w(kind, p)) * (v[2 * q1][p] + v[2 * q1 + 1][p]) for p in (2 * p1, 2 * p1 + 1)) for p1 in range(half)]
        for q1 in range(half)
    ]


def edge_swept(v, kind, w, bottom):
    return [
        [w(kind, p) * (v[q][p] if q else v[q][p] * jnp.where(bottom, w(RHO, p), 1.0)) for p in range(len(v[q]))]
        for q in range(len(v))
    ]


def added(a, b):
    return [[s + t for s, t in zip(x, y)] for x, y in zip(a, b)]


def first_guess(f, w, bottom):
    return [
        [w(C, p) * (f[q][p] if q else f[q][p] * jnp.where(bottom, w(RHO, p), 1.0)) for p in range(len(f[q]))]
        for q in range(len(f))
    ]


def grid_of(block, count):
    return [[block[q * count + p] for p in range(count)] for q in range(count)]


def table(ref, row):
    @functools.cache
    def weight(kind, p):
        return ref[kind, p, pl.ds(row, 1), :]

    return weight


def put_row(ref, row, tiles):
    count = len(tiles)
    for q in range(count):
        for p in range(count):
            ref[row, q * count + p] = tiles[q][p]


def kernel(
    n_dir, n_gx,
    cot, pot, height, adjoint, gradient,
    h_in, c_in, p_in, a_out, mixed,
    hs, fs, ps, ds, w0, de, d1, w1, df, d2s, d2, w2,
    v0, v1, v2, v3,
    packet, from_west, from_east, from_west2, from_east2, from_west3, from_east3, f2own, f2r, f1, u0, u1, u2, u3,
    gn, er,
    local_sem, send_sem, recv_sem,
):
    me_dir, me = lax.axis_index("dir"), lax.axis_index("gx")

    def strip(offset):
        return {"gx": lax.rem(me + offset + 9 * n_gx, n_gx)}

    barrier = pltpu.get_barrier_semaphore()
    greeted = [o for s in range(1, GREET + 1) for o in (-s, s)]
    for offset in greeted:
        pl.semaphore_signal(barrier, inc=1, device_id=strip(offset), device_id_type=MESH)
    for step in range(1, n_dir):
        pl.semaphore_signal(
            barrier, inc=1, device_id={"dir": lax.rem(me_dir + step, n_dir)}, device_id_type=MESH
        )

    height_in = pltpu.make_async_copy(height, h_in, local_sem.at[0])
    cot_in = pltpu.make_async_copy(cot.at[0], c_in, local_sem.at[1])
    pot_in = pltpu.make_async_copy(pot.at[0], p_in, local_sem.at[2])
    height_in.start()
    cot_in.start()
    pot_in.start()

    sent = []

    def send(source, target, device):
        index = len(sent)
        copy = pltpu.make_async_remote_copy(
            src_ref=source, dst_ref=target, send_sem=send_sem.at[index], recv_sem=recv_sem.at[index],
            device_id=device, device_id_type=MESH,
        )
        copy.start()
        sent.append(copy)
        return copy

    bottom, top = iota((8, 128), 0) == 0, iota((8, 128), 0) == 7

    for p in range(4):
        ds[p, 24:32, :] = jnp.ones((8, 128), jnp.float32)
    d2[...] = jnp.ones(d2.shape, jnp.float32)
    d1[...] = jnp.ones(d1.shape, jnp.float32)

    height_in.wait()
    raw = h_in[...]
    for p, cl in enumerate(spread_lanes([raw[:, 128 * c : 128 * c + 128] for c in range(4)])):
        hs[3, 4 * p : 4 * p + 4, :] = CEILING - cl

    pl.semaphore_wait(barrier, len(greeted) + n_dir - 1)
    depth_copies = [send(hs.at[3], hs.at[3 - o], strip(o)) for o in (-1, 1, -2, 2, -3, 3)]

    def spread_row(source, target, row, slot):
        block = source[row]
        for p, cl in enumerate(spread_lanes([block[:, 128 * c : 128 * c + 128] for c in range(4)])):
            target[slot, p] = cl

    cot_in.wait()
    for x in range(0, 4):
        spread_row(c_in, fs, x, x + 4)
    field_copies = [
        send(fs.at[pl.ds(4, 4)], fs.at[pl.ds(4 - 4 * o, 4)], strip(o)) for o in (-1, 1)
    ]

    pot_in.wait()
    for x in range(0, 4):
        spread_row(p_in, ps, x, x + 1)
    potential_copies = [send(ps.at[1], ps.at[5], strip(-1)), send(ps.at[4], ps.at[0], strip(1))]

    def field_row(ref, slot):
        return [[ref[slot, p, pl.ds(q, 8, stride=4), :] for p in range(4)] for q in range(4)]

    for copy in depth_copies:
        copy.wait_recv()
    for o in range(7):
        for p in range(4):
            ds[p, 4 * o : 4 * o + 4, :] = hs[o, 4 * p : 4 * p + 4, :]
    for p1 in range(2):
        de[p1] = ds[2 * p1] + ds[2 * p1 + 1]
    for p1 in range(2):
        d1[p1, 0:16, :] = 0.25 * (de[p1, pl.ds(0, 16, stride=2), :] + de[p1, pl.ds(1, 16, stride=2), :])
    df[...] = d1[0] + d1[1]
    d2s[1] = 0.25 * (df[pl.ds(0, 8, stride=2), :] + df[pl.ds(1, 8, stride=2), :])
    d2_copies = [send(d2s.at[1], d2s.at[1 - s], strip(7 * s)) for s in (-1, 1)]

    def faces(rows, per_strip, first):
        size = n_gx * per_strip
        place = (me * per_strip + first + REACH * size + iota((rows, 128), 0)) & (size - 1)
        return place != 0, place != size - 1

    open_west, open_east = faces(16, 4, -4)
    mid = [ds[p, 8:24, :] for p in range(4)]
    west = [ds[p, 7:23, :] for p in range(4)]
    east = [ds[p, 9:25, :] for p in range(4)]
    for p, kinds in enumerate(level_weights(mid, west, east, open_west, open_east, 1.0)):
        for kind, value in enumerate(kinds):
            w0[kind, p] = value
    open_west, open_east = faces(16, 2, -5)
    mid1 = [d1[p, 1:17, :] for p in range(2)]
    west1 = [d1[p, 0:16, :] for p in range(2)]
    east1 = [d1[p, 2:18, :] for p in range(2)]
    for p, kinds in enumerate(level_weights(mid1, west1, east1, open_west, open_east, 2.0)):
        for kind, value in enumerate(kinds):
            w1[kind, p] = value

    def guess_row(i):
        put_row(v0, i, first_guess(field_row(fs, i), table(w0, i), bottom))

    def row_of(ref, i, count=4):
        return grid_of(ref[i], count)

    def smooth_rows(source, target, low, high):
        have = {i: row_of(source, i) for i in range(low - 1, high + 1)}
        for i in range(low, high):
            put_row(target, i, swept(have[i], have[i - 1], have[i + 1], row_of(v0, i), table(w0, i), bottom, top))

    for i in range(4, 8):
        guess_row(i)
    have = [None] + [row_of(v0, i) for i in range(4, 8)] + [None]
    put_row(v1, 3, edge_swept(have[1], CE, table(w0, 3), bottom))
    for i in range(4, 8):
        put_row(v1, i, swept(have[i - 3], have[i - 4], have[i - 2], have[i - 3], table(w0, i), bottom, top))
    put_row(v1, 8, edge_swept(have[4], CW, table(w0, 8), bottom))
    have = [None] + [row_of(v1, i) for i in range(3, 9)] + [None]
    rest = {i: restricted(have[i - 2], have[i - 3], have[i - 1], row_of(v0, i) if 4 <= i <= 7 else None, table(w0, i), bottom, top) for i in range(3, 9)}
    rest[2] = edge_restricted(have[1], CE, table(w0, 2))
    rest[9] = edge_restricted(have[6], CW, table(w0, 9))
    f1p = [added(rest[2 * i + 2], rest[2 * i + 3]) for i in range(4)]
    for q in range(2):
        for p in range(2):
            packet[2 * q + p] = f1p[0][q][p]
            packet[9 + 2 * q + p] = f1p[3][q][p]

    begin = {i: first_guess(f1p[i - 4], table(w1, i), bottom) for i in range(4, 8)}
    next_row = {i: swept(begin[i], begin.get(i - 1), begin.get(i + 1), begin[i], table(w1, i), bottom, top) for i in range(4, 8)}
    next_row[3] = edge_swept(begin[4], CE, table(w1, 3), bottom)
    next_row[8] = edge_swept(begin[7], CW, table(w1, 8), bottom)
    rest = {
        i: restricted(next_row[i], next_row.get(i - 1), next_row.get(i + 1), begin.get(i), table(w1, i), bottom, top)
        for i in range(3, 9)
    }
    rest[2] = edge_restricted(next_row[3], CE, table(w1, 2))
    rest[9] = edge_restricted(next_row[8], CW, table(w1, 9))
    f2p = [sum(rest[i][0][0] for i in rows) for rows in ((2,), (3, 4), (5, 6), (7, 8), (9,))]
    for k in range(5):
        packet[4 + k] = f2p[k]
    sum_copies = [
        send(packet.at[pl.ds(0, 7)], from_east, strip(-1)),
        send(packet.at[pl.ds(6, 7)], from_west, strip(1)),
        send(packet.at[pl.ds(4, 2)], from_east2, strip(-2)),
        send(packet.at[pl.ds(7, 2)], from_west2, strip(2)),
        send(packet.at[4], from_east3.at[0], strip(-3)),
        send(packet.at[8], from_west3.at[0], strip(3)),
    ]

    for copy in d2_copies:
        copy.wait_recv()
    d2[0:8, :] = d2s[0]
    d2[7:15, :] = d2s[1]
    d2[14:22, :] = d2s[2]
    open_west, open_east = faces(24, 1, -9)
    for kind, value in enumerate(
        level_weights([d2[1:25, :]], [d2[0:24, :]], [d2[2:26, :]], open_west, open_east, 4.0)[0]
    ):
        w2[kind, 0] = value

    for copy in sum_copies:
        copy.wait_recv()
    f2own[0] = (f2p[1] + from_west[0]) + (from_east[4] + from_west2[0]) + from_west3[0]
    f2own[1] = (f2p[2] + from_west[1]) + (from_east[5] + from_west2[1]) + from_east2[0]
    f2own[2] = (f2p[3] + from_west[2]) + (from_east[6] + from_east2[1]) + from_east3[0]
    slots = (-9, -6, -3, 3, 6, 9)
    row_copies = [
        send(f2own.at[pl.ds(0, 2)], f2r.at[5, pl.ds(0, 2)], strip(-9)),
        send(f2own.at[pl.ds(1, 2)], f2r.at[0, pl.ds(1, 2)], strip(9)),
    ]
    row_copies += [send(f2own, f2r.at[slots.index(-o)], strip(o)) for o in (-6, 6, -3, 3)]
    for q in range(2):
        for p in range(2):
            f1[6, 2 * q + p] = f1p[1][q][p] + from_west[3 + 2 * q + p]
            f1[7, 2 * q + p] = f1p[2][q][p] + from_east[2 * q + p]
    terrain = terrain_weights(
        [ds[p, 8:24, :] for p in range(4)], [ds[p, 7:23, :] for p in range(4)], [ds[p, 9:25, :] for p in range(4)],
        *faces(16, 4, -4),
    )
    for p, kinds in enumerate(terrain):
        for kind, value in enumerate(kinds):
            w0[GW + kind, p] = value
    for copy in field_copies:
        copy.wait_recv()
    for i in range(0, 4):
        guess_row(i)
    for i in range(8, 12):
        guess_row(i)
    smooth_rows(v0, v1, 1, 11)
    f1_copies = [send(f1.at[pl.ds(6, 2)], f1.at[pl.ds(6 - 2 * o, 2)], strip(o)) for o in (-1, 1, -2, 2)]
    f1_copies += [send(f1.at[6], f1.at[12], strip(-3)), send(f1.at[7], f1.at[1], strip(3))]

    for copy in row_copies:
        copy.wait_recv()
    start = []
    for o in range(-REACH, REACH + 1):
        block = (o + 10) // 3 * 3 - 9
        source = f2own[o + 1] if block == 0 else f2r[slots.index(block), o - block + 1]
        start.append(first_guess([[source]], table(w2, o + REACH), bottom))
    now = start
    for sweep in range(7):
        later = [None] * len(now)
        for i in range(sweep + 1, len(now) - sweep - 1):
            later[i] = swept(now[i], now[i - 1], now[i + 1], start[i], table(w2, i), bottom, top)
        now = later

    for copy in f1_copies:
        copy.wait_recv()
    for i in range(0, 12):
        put_row(u0, i, first_guess(grid_of(f1[i + 1], 2), table(w1, i), bottom))
    for i in range(1, 11):
        rows = [row_of(u0, i + d, 2) for d in (0, -1, 1)]
        put_row(u1, i, swept(*rows, row_of(u0, i, 2), table(w1, i), bottom, top))
    for i in range(1, 11):
        fix = now[(i - 5) // 2 + REACH][0][0]
        put_row(u1, i, [[t + fix for t in line] for line in row_of(u1, i, 2)])
    for source, target, low, high in ((u1, u2, 2, 10), (u2, u3, 3, 9)):
        for i in range(low, high):
            rows = [row_of(source, i + d, 2) for d in (0, -1, 1)]
            put_row(target, i, swept(*rows, row_of(u0, i, 2), table(w1, i), bottom, top))

    def corrected_row(i):
        fix = row_of(u3, (i - 4 + 8) // 2 + 1, 2)
        now_row = row_of(v1, i)
        put_row(v1, i, [[now_row[q][p] + fix[q // 2][p // 2] for p in range(4)] for q in range(4)])

    for i in range(1, 11):
        corrected_row(i)
    smooth_rows(v1, v2, 2, 10)
    smooth_rows(v2, v3, 3, 9)

    for copy in potential_copies:
        copy.wait_recv()

    def terrain_row(x):
        w = table(w0, x + 4)
        a, a_west, a_east = (row_of(v3, x + 4 + d) for d in (0, -1, 1))
        b, b_west, b_east = (field_row(ps, x + 1 + d) for d in (0, -1, 1))
        zeros = jnp.zeros((8, 128), jnp.float32)
        by_z, by_west, by_east, by_north = ([zeros] * 4 for _ in range(4))
        for q in range(4):
            for p in range(4):
                by_z[p] += (above(a, q, p, top) - a[q][p]) * (above(b, q, p, top) - b[q][p])
                by_west[p] += (a[q][p] - a_west[q][p]) * (b[q][p] - b_west[q][p])
                by_east[p] += (a_east[q][p] - a[q][p]) * (b_east[q][p] - b[q][p])
                by_north[p] += (north_of(a, q, p) - a[q][p]) * (north_of(b, q, p) - b[q][p])
        out = []
        for p in range(4):
            by_south = by_north[p - 1] if p else pltpu.roll(by_north[3], 1, 1)
            total = w(GW, p) * by_west[p] + w(GE, p) * by_east[p] + w(GN, p) * by_north[p]
            total = total + w(GS, p) * by_south + w(GZ, p) * by_z[p]
            out.append(jnp.sum(total, axis=0, keepdims=True))
        return out

    sums = [terrain_row(x) for x in range(4)]
    blank = jnp.zeros((4, 128), jnp.float32)
    packed = [jnp.concatenate([sums[x][p] for x in range(4)] + [blank], axis=0) for p in range(4)]
    for c, tile in enumerate(join_lanes(packed)):
        gn[c] = tile
    dir_copies = []
    for step in range(1, n_dir):
        target = lax.rem(me_dir + step, n_dir)
        dir_copies.append(send(gn.at[target // (n_dir // 4)], er.at[step - 1], {"dir": target}))

    def natural_row(x):
        now_row = row_of(v3, x + 4)
        for p in range(4):
            for q in range(4):
                mixed[x, p, pl.ds(q, 8, stride=4), :] = now_row[q][p]
        for c, tile in enumerate(join_lanes([mixed[x, p] for p in range(4)])):
            a_out[x, :, 128 * c : 128 * c + 128] = tile

    for i in range(0, 4):
        natural_row(i)
    out_copy = pltpu.make_async_copy(a_out, adjoint.at[0], local_sem.at[3])
    out_copy.start()

    for copy in dir_copies:
        copy.wait_recv()
    total = gn[me_dir // (n_dir // 4)]
    for step in range(1, n_dir):
        total = total + er[step - 1]
    part = lax.rem(me_dir, n_dir // 4)
    mine = total
    width = gradient.shape[1]
    for k in range(1, 128 // width):
        mine = jnp.where(iota((8, 128), 0) * 0 + part == k, pltpu.roll(total, 128 - k * width, 1), mine)
    gradient[...] = mine[0:4, 0:width]

    out_copy.wait()
    for copy in sent:
        copy.wait_send()


def body(cotangent, potential, height):
    n_dir, n_gx = lax.axis_size("dir"), lax.axis_size("gx")
    f32 = jnp.float32
    shapes = [
        (4, 512), (4, 32, 512), (4, 32, 512), (4, 32, 512), (4, 4, 32, 128),
        (7, 16, 128), (12, 4, 32, 128), (6, 4, 32, 128), (4, 32, 128), (14, 4, 16, 128),
        (2, 32, 128), (2, 24, 128), (9, 2, 16, 128), (24, 128), (3, 8, 128), (32, 128), (9, 1, 24, 128),
        (12, 16, 8, 128), (12, 16, 8, 128), (12, 16, 8, 128), (12, 16, 8, 128),
        (13, 8, 128), (7, 8, 128), (7, 8, 128), (2, 8, 128), (2, 8, 128), (1, 8, 128), (1, 8, 128), (3, 8, 128), (6, 3, 8, 128), (14, 4, 8, 128),
        (12, 4, 8, 128), (12, 4, 8, 128), (12, 4, 8, 128), (12, 4, 8, 128),
        (4, 8, 128), (n_dir - 1, 8, 128),
    ]
    copies = 6 + 2 + 2 + 2 + 6 + 6 + 6 + n_dir - 1
    return pl.pallas_call(
        functools.partial(kernel, n_dir, n_gx),
        out_shape=(
            pltpu.VMEM(cotangent.shape, f32),
            pltpu.VMEM((height.shape[0], height.shape[1] // n_dir), f32),
        ),
        in_specs=[pl.BlockSpec(memory_space=pltpu.HBM)] * 3,
        out_specs=(pl.BlockSpec(memory_space=pl.ANY), pl.BlockSpec(memory_space=pltpu.VMEM)),
        scratch_shapes=[pltpu.VMEM(shape, f32) for shape in shapes]
        + [pltpu.SemaphoreType.DMA((4,)), pltpu.SemaphoreType.DMA((copies,)), pltpu.SemaphoreType.DMA((copies,))],
        compiler_params=pltpu.CompilerParams(
            collective_id=0, has_side_effects=True, vmem_limit_bytes=60 * 1024 * 1024
        ),
        name="vcycle",
    )(cotangent, potential, height)


def solution(mesh):
    placed = (P("dir", "gx", None, None), P("dir", "gx", None, None), P("gx", None))
    return jax.shard_map(
        body,
        mesh=mesh,
        in_specs=placed,
        out_specs=(P("dir", "gx", None, None), P("gx", "dir")),
        check_vma=False,
    )
```

```python
import functools

import jax
import jax.numpy as jnp
from jax import lax
from jax.experimental import pallas as pl
from jax.experimental.pallas import tpu as pltpu
from jax.sharding import PartitionSpec as P

MESH = pl.DeviceIdType.MESH
DAMPING = 0.7
ANISOTROPY = 4.0
CEILING = 1.5
REACH = 9
GREET = 4
C, CW, CE, CS, CN, CZ, RHO, SIG, DINV = range(9)
GW, GE, GS, GN, GZ = range(9, 14)


def iota(shape, dim):
    return lax.broadcasted_iota(jnp.int32, shape, dim)


def spread_lanes(cols):
    shape = cols[0].shape
    lane = iota(shape, 1)
    block, inner = lane >> 5, lane & 31
    turned = [
        jnp.take_along_axis(col, 4 * inner + ((block - c) & 3), axis=1, mode="promise_in_bounds")
        for c, col in enumerate(cols)
    ]
    out = []
    for p in range(4):
        mixed = turned[(3 - p) % 4]
        for b in range(3):
            mixed = jnp.where(block == b, turned[(b - p) % 4], mixed)
        out.append(mixed if p == 0 else pltpu.roll(mixed, 128 - 32 * p, 1))
    return out


def join_lanes(classes):
    shape = classes[0].shape
    lane = iota(shape, 1)
    block = lane >> 5
    turned = [cl if p == 0 else pltpu.roll(cl, 32 * p, 1) for p, cl in enumerate(classes)]
    out = []
    for c in range(4):
        mixed = turned[(3 - c) % 4]
        for b in range(3):
            mixed = jnp.where(block == b, turned[(b - c) % 4], mixed)
        source = (((lane + c) & 3) << 5) + (lane >> 2)
        out.append(jnp.take_along_axis(mixed, source, axis=1, mode="promise_in_bounds"))
    return out


def harmonic(a, b, scale):
    return scale * 2.0 * a * b / (a + b)


def level_weights(mid, west, east, open_west, open_east, scale):
    count = len(mid)
    lane = iota(mid[0].shape, 1)
    w_west = [jnp.where(open_west, harmonic(a, b, scale), 0.0) for a, b in zip(mid, west)]
    w_east = [jnp.where(open_east, harmonic(a, b, scale), 0.0) for a, b in zip(mid, east)]
    w_north = [harmonic(mid[p], mid[p + 1], scale) for p in range(count - 1)]
    last = harmonic(mid[count - 1], pltpu.roll(mid[0], 127, 1), scale)
    w_north.append(jnp.where(lane < 127, last, 0.0))
    w_south = [pltpu.roll(w_north[count - 1], 1, 1)] + w_north[:-1]
    out = []
    for p in range(count):
        w_z = (scale * ANISOTROPY) / mid[p]
        low = w_west[p] + w_east[p] + w_south[p] + w_north[p] + w_z
        full = low + w_z
        c = DAMPING / full
        out.append(
            (c, c * w_west[p], c * w_east[p], c * w_south[p], c * w_north[p], c * w_z, full / low, low / full, full / DAMPING)
        )
    return out


def terrain_weights(mid, west, east, open_west, open_east):
    lane = iota(mid[0].shape, 1)

    def share(own, other):
        both = own + other
        return 2.0 * other * other / (both * both)

    out = []
    for p in range(4):
        south = mid[p - 1] if p else pltpu.roll(mid[3], 1, 1)
        north = mid[p + 1] if p < 3 else pltpu.roll(mid[0], 127, 1)
        g_south, g_north = share(mid[p], south), share(mid[p], north)
        out.append(
            (
                jnp.where(open_west, share(mid[p], west[p]), 0.0),
                jnp.where(open_east, share(mid[p], east[p]), 0.0),
                g_south if p else jnp.where(lane > 0, g_south, 0.0),
                g_north if p < 3 else jnp.where(lane < 127, g_north, 0.0),
                -ANISOTROPY / (mid[p] * mid[p]),
            )
        )
    return out


def north_of(v, q, p):
    return v[q][p + 1] if p + 1 < len(v[q]) else pltpu.roll(v[q][0], 127, 1)


def south_of(v, q, p):
    return v[q][p - 1] if p else pltpu.roll(v[q][-1], 1, 1)


def above(v, q, p, top):
    return v[q + 1][p] if q + 1 < len(v) else jnp.where(top, 0.0, pltpu.roll(v[0][p], 7, 0))


def below(v, q, p, bottom):
    return v[q - 1][p] if q else jnp.where(bottom, 0.0, pltpu.roll(v[-1][p], 1, 0))


def around(v, v_west, v_east, w, bottom, top):
    out = []
    for q in range(len(v)):
        line = []
        for p in range(len(v[q])):
            total = w(CZ, p) * (above(v, q, p, top) + below(v, q, p, bottom))
            total = total + w(CS, p) * south_of(v, q, p) + w(CN, p) * north_of(v, q, p)
            if v_west is not None:
                total = total + w(CW, p) * v_west[q][p]
            if v_east is not None:
                total = total + w(CE, p) * v_east[q][p]
            line.append(total)
        out.append(line)
    return out


def swept(v, v_west, v_east, start, w, bottom, top):
    near = around(v, v_west, v_east, w, bottom, top)
    out = []
    for q in range(len(v)):
        line = []
        for p in range(len(v[q])):
            move = near[q][p] if q else near[q][p] * jnp.where(bottom, w(RHO, p), 1.0)
            line.append((1.0 - DAMPING) * v[q][p] + start[q][p] + move)
        out.append(line)
    return out


def restricted(v, v_west, v_east, start, w, bottom, top):
    near = around(v, v_west, v_east, w, bottom, top)
    half = len(v) // 2
    out = [[0.0] * half for _ in range(half)]
    for q1 in range(half):
        for p in range(len(v)):
            part = 0.0
            for q in (2 * q1, 2 * q1 + 1):
                own = -DAMPING * v[q][p] if start is None else start[q][p] - DAMPING * v[q][p]
                if q == 0:
                    own = own * jnp.where(bottom, w(SIG, p), 1.0)
                part = part + (near[q][p] + own)
            out[q1][p // 2] = out[q1][p // 2] + w(DINV, p) * part
    return out


def edge_restricted(v, kind, w):
    half = len(v) // 2
    return [
        [sum((w(DINV, p) * w(kind, p)) * (v[2 * q1][p] + v[2 * q1 + 1][p]) for p in (2 * p1, 2 * p1 + 1)) for p1 in range(half)]
        for q1 in range(half)
    ]


def edge_swept(v, kind, w, bottom):
    return [
        [w(kind, p) * (v[q][p] if q else v[q][p] * jnp.where(bottom, w(RHO, p), 1.0)) for p in range(len(v[q]))]
        for q in range(len(v))
    ]


def added(a, b):
    return [[s + t for s, t in zip(x, y)] for x, y in zip(a, b)]


def first_guess(f, w, bottom):
    return [
        [w(C, p) * (f[q][p] if q else f[q][p] * jnp.where(bottom, w(RHO, p), 1.0)) for p in range(len(f[q]))]
        for q in range(len(f))
    ]


def grid_of(block, count):
    return [[block[q * count + p] for p in range(count)] for q in range(count)]


def table(ref, row):
    @functools.cache
    def weight(kind, p):
        return ref[kind, p, pl.ds(row, 1), :]

    return weight


def put_row(ref, row, tiles):
    count = len(tiles)
    for q in range(count):
        for p in range(count):
            ref[row, q * count + p] = tiles[q][p]


def kernel(
    n_dir, n_gx,
    cot, pot, height, adjoint, gradient,
    h_in, c_in, p_in, a_out, mixed,
    hs, fs, ps, ds, w0, de, d1, w1, df, d2s, d2, w2,
    v0, v1, v2, v3,
    packet, from_west, from_east, from_west2, from_east2, from_west3, from_east3, f2own, f2r, end_row, end_depth, f1, u0, u1, u2, u3,
    gn, er,
    local_sem, send_sem, recv_sem,
):
    me_dir, me = lax.axis_index("dir"), lax.axis_index("gx")

    def inside(offset):
        return me + offset < n_gx if offset > 0 else me + offset >= 0

    barrier = pltpu.get_barrier_semaphore()
    greetings = n_dir - 1
    for offset in [o for s in range(1, GREET + 1) for o in (-s, s)]:

        @pl.when(inside(offset))
        def _():
            pl.semaphore_signal(barrier, inc=1, device_id={"gx": me + offset}, device_id_type=MESH)

        greetings = greetings + inside(offset).astype(jnp.int32)
    for step in range(1, n_dir):
        pl.semaphore_signal(
            barrier, inc=1, device_id={"dir": lax.rem(me_dir + step, n_dir)}, device_id_type=MESH
        )

    height_in = pltpu.make_async_copy(height, h_in, local_sem.at[0])
    cot_in = pltpu.make_async_copy(cot.at[0], c_in, local_sem.at[1])
    pot_in = pltpu.make_async_copy(pot.at[0], p_in, local_sem.at[2])
    height_in.start()
    cot_in.start()
    pot_in.start()

    sent, by_offset = [], {}

    def copy_to(source, target, device):
        index = len(sent)
        copy = pltpu.make_async_remote_copy(
            src_ref=source, dst_ref=target, send_sem=send_sem.at[index], recv_sem=recv_sem.at[index],
            device_id=device, device_id_type=MESH,
        )
        sent.append(copy)
        return copy

    def send(source, target, offset):
        copy = copy_to(source, target, {"gx": me + offset})
        by_offset.setdefault(offset, []).append(copy)
        pl.when(inside(offset))(copy.start)
        return copy, target, offset

    def arrive(copies, filler=0.0):
        for copy, target, offset in copies:

            @pl.when(inside(-offset))
            def _():
                copy.wait_recv()

            @pl.when(jnp.logical_not(inside(-offset)))
            def _():
                target[...] = jnp.full(target.shape, filler, jnp.float32)

    bottom, top = iota((8, 128), 0) == 0, iota((8, 128), 0) == 7

    for p in range(4):
        ds[p, 24:32, :] = jnp.ones((8, 128), jnp.float32)
    d2[...] = jnp.ones(d2.shape, jnp.float32)
    d1[...] = jnp.ones(d1.shape, jnp.float32)

    height_in.wait()
    raw = h_in[...]
    for p, cl in enumerate(spread_lanes([raw[:, 128 * c : 128 * c + 128] for c in range(4)])):
        hs[3, 4 * p : 4 * p + 4, :] = CEILING - cl

    pl.semaphore_wait(barrier, greetings)
    depth_copies = [send(hs.at[3], hs.at[3 - o], o) for o in (-1, 1, -2, 2, -3, 3)]

    def spread_row(source, target, row, slot):
        block = source[row]
        for p, cl in enumerate(spread_lanes([block[:, 128 * c : 128 * c + 128] for c in range(4)])):
            target[slot, p] = cl

    cot_in.wait()
    for x in range(0, 4):
        spread_row(c_in, fs, x, x + 4)
    field_copies = [
        send(fs.at[pl.ds(4, 4)], fs.at[pl.ds(4 - 4 * o, 4)], o) for o in (-1, 1)
    ]

    pot_in.wait()
    for x in range(0, 4):
        spread_row(p_in, ps, x, x + 1)
    potential_copies = [send(ps.at[1], ps.at[5], -1), send(ps.at[4], ps.at[0], 1)]

    def field_row(ref, slot):
        return [[ref[slot, p, pl.ds(q, 8, stride=4), :] for p in range(4)] for q in range(4)]

    arrive(depth_copies, 1.0)
    for o in range(7):
        for p in range(4):
            ds[p, 4 * o : 4 * o + 4, :] = hs[o, 4 * p : 4 * p + 4, :]
    for p1 in range(2):
        de[p1] = ds[2 * p1] + ds[2 * p1 + 1]
    for p1 in range(2):
        d1[p1, 0:16, :] = 0.25 * (de[p1, pl.ds(0, 16, stride=2), :] + de[p1, pl.ds(1, 16, stride=2), :])
    df[...] = d1[0] + d1[1]
    d2s[1] = 0.25 * (df[pl.ds(0, 8, stride=2), :] + df[pl.ds(1, 8, stride=2), :])
    d2_copies = [send(d2s.at[1], d2s.at[1 - s], 7 * s) for s in (-1, 1)]
    end_depths = []
    for end, (home, sign) in enumerate(((0, 1), (n_gx - 1, -1))):
        for away in (4, 5, 6):
            copy = copy_to(d2s.at[1], end_depth.at[end], {"gx": me + sign * away})
            pl.when(me == home)(copy.start)
            end_depths.append((copy, end, home, home + sign * away, 7 - sign * away))

    def faces(rows, per_strip, first):
        size = n_gx * per_strip
        place = (me * per_strip + first + REACH * size + iota((rows, 128), 0)) & (size - 1)
        return place != 0, place != size - 1

    open_west, open_east = faces(16, 4, -4)
    mid = [ds[p, 8:24, :] for p in range(4)]
    west = [ds[p, 7:23, :] for p in range(4)]
    east = [ds[p, 9:25, :] for p in range(4)]
    for p, kinds in enumerate(level_weights(mid, west, east, open_west, open_east, 1.0)):
        for kind, value in enumerate(kinds):
            w0[kind, p] = value
    open_west, open_east = faces(16, 2, -5)
    mid1 = [d1[p, 1:17, :] for p in range(2)]
    west1 = [d1[p, 0:16, :] for p in range(2)]
    east1 = [d1[p, 2:18, :] for p in range(2)]
    for p, kinds in enumerate(level_weights(mid1, west1, east1, open_west, open_east, 2.0)):
        for kind, value in enumerate(kinds):
            w1[kind, p] = value

    def guess_row(i):
        put_row(v0, i, first_guess(field_row(fs, i), table(w0, i), bottom))

    def row_of(ref, i, count=4):
        return grid_of(ref[i], count)

    def smooth_rows(source, target, low, high):
        have = {i: row_of(source, i) for i in range(low - 1, high + 1)}
        for i in range(low, high):
            put_row(target, i, swept(have[i], have[i - 1], have[i + 1], row_of(v0, i), table(w0, i), bottom, top))

    for i in range(4, 8):
        guess_row(i)
    have = [None] + [row_of(v0, i) for i in range(4, 8)] + [None]
    put_row(v1, 3, edge_swept(have[1], CE, table(w0, 3), bottom))
    for i in range(4, 8):
        put_row(v1, i, swept(have[i - 3], have[i - 4], have[i - 2], have[i - 3], table(w0, i), bottom, top))
    put_row(v1, 8, edge_swept(have[4], CW, table(w0, 8), bottom))
    have = [None] + [row_of(v1, i) for i in range(3, 9)] + [None]
    rest = {i: restricted(have[i - 2], have[i - 3], have[i - 1], row_of(v0, i) if 4 <= i <= 7 else None, table(w0, i), bottom, top) for i in range(3, 9)}
    rest[2] = edge_restricted(have[1], CE, table(w0, 2))
    rest[9] = edge_restricted(have[6], CW, table(w0, 9))
    f1p = [added(rest[2 * i + 2], rest[2 * i + 3]) for i in range(4)]
    for q in range(2):
        for p in range(2):
            packet[2 * q + p] = f1p[0][q][p]
            packet[9 + 2 * q + p] = f1p[3][q][p]

    begin = {i: first_guess(f1p[i - 4], table(w1, i), bottom) for i in range(4, 8)}
    next_row = {i: swept(begin[i], begin.get(i - 1), begin.get(i + 1), begin[i], table(w1, i), bottom, top) for i in range(4, 8)}
    next_row[3] = edge_swept(begin[4], CE, table(w1, 3), bottom)
    next_row[8] = edge_swept(begin[7], CW, table(w1, 8), bottom)
    rest = {
        i: restricted(next_row[i], next_row.get(i - 1), next_row.get(i + 1), begin.get(i), table(w1, i), bottom, top)
        for i in range(3, 9)
    }
    rest[2] = edge_restricted(next_row[3], CE, table(w1, 2))
    rest[9] = edge_restricted(next_row[8], CW, table(w1, 9))
    f2p = [sum(rest[i][0][0] for i in rows) for rows in ((2,), (3, 4), (5, 6), (7, 8), (9,))]
    for k in range(5):
        packet[4 + k] = f2p[k]
    sum_copies = [
        send(packet.at[pl.ds(0, 7)], from_east, -1),
        send(packet.at[pl.ds(6, 7)], from_west, 1),
        send(packet.at[pl.ds(4, 2)], from_east2, -2),
        send(packet.at[pl.ds(7, 2)], from_west2, 2),
        send(packet.at[4], from_east3.at[0], -3),
        send(packet.at[8], from_west3.at[0], 3),
    ]

    arrive(d2_copies, 1.0)
    d2[0:8, :] = d2s[0]
    d2[7:15, :] = d2s[1]
    d2[14:22, :] = d2s[2]
    for copy, end, _, place, first in end_depths:

        @pl.when(me == place)
        def _():
            copy.wait_recv()
            d2[first : first + 7, :] = end_depth[end, 0:7, :]

    open_west, open_east = faces(24, 1, -9)
    for kind, value in enumerate(
        level_weights([d2[1:25, :]], [d2[0:24, :]], [d2[2:26, :]], open_west, open_east, 4.0)[0]
    ):
        w2[kind, 0] = value

    arrive(sum_copies)
    f2own[0] = (f2p[1] + from_west[0]) + (from_east[4] + from_west2[0]) + from_west3[0]
    f2own[1] = (f2p[2] + from_west[1]) + (from_east[5] + from_west2[1]) + from_east2[0]
    f2own[2] = (f2p[3] + from_west[2]) + (from_east[6] + from_east2[1]) + from_east3[0]
    slots = (-9, -6, -3, 3, 6, 9)
    row_copies = [
        send(f2own.at[pl.ds(0, 2)], f2r.at[5, pl.ds(0, 2)], -9),
        send(f2own.at[pl.ds(1, 2)], f2r.at[0, pl.ds(1, 2)], 9),
    ]
    row_copies += [send(f2own, f2r.at[slots.index(-o)], o) for o in (-6, 6, -3, 3)]
    end_copies = []
    for end, (home, sign) in enumerate(((0, 1), (n_gx - 1, -1))):
        for block in (3, 6, 9):
            copy = copy_to(f2own.at[1], end_row.at[end], {"gx": me + sign * (block - 1)})
            pl.when(me == home)(copy.start)
            end_copies.append((copy, end, home, home + sign * (block - 1), slots.index(-sign * block)))
    for q in range(2):
        for p in range(2):
            f1[6, 2 * q + p] = f1p[1][q][p] + from_west[3 + 2 * q + p]
            f1[7, 2 * q + p] = f1p[2][q][p] + from_east[2 * q + p]
    terrain = terrain_weights(
        [ds[p, 8:24, :] for p in range(4)], [ds[p, 7:23, :] for p in range(4)], [ds[p, 9:25, :] for p in range(4)],
        *faces(16, 4, -4),
    )
    for p, kinds in enumerate(terrain):
        for kind, value in enumerate(kinds):
            w0[GW + kind, p] = value
    arrive(field_copies)
    for i in range(0, 4):
        guess_row(i)
    for i in range(8, 12):
        guess_row(i)
    smooth_rows(v0, v1, 1, 11)
    f1_copies = [send(f1.at[pl.ds(6, 2)], f1.at[pl.ds(6 - 2 * o, 2)], o) for o in (-1, 1, -2, 2)]
    f1_copies += [send(f1.at[6], f1.at[12], -3), send(f1.at[7], f1.at[1], 3)]

    arrive(row_copies)
    for copy, end, _, place, slot in end_copies:

        @pl.when(me == place)
        def _():
            copy.wait_recv()
            f2r[slot, 2 - 2 * end] = end_row[end]

    start = []
    for o in range(-REACH, REACH + 1):
        block = (o + 10) // 3 * 3 - 9
        source = f2own[o + 1] if block == 0 else f2r[slots.index(block), o - block + 1]
        start.append(first_guess([[source]], table(w2, o + REACH), bottom))
    now = start
    for sweep in range(7):
        later = [None] * len(now)
        for i in range(sweep + 1, len(now) - sweep - 1):
            later[i] = swept(now[i], now[i - 1], now[i + 1], start[i], table(w2, i), bottom, top)
        now = later

    arrive(f1_copies)
    for i in range(0, 12):
        put_row(u0, i, first_guess(grid_of(f1[i + 1], 2), table(w1, i), bottom))
    for i in range(1, 11):
        rows = [row_of(u0, i + d, 2) for d in (0, -1, 1)]
        put_row(u1, i, swept(*rows, row_of(u0, i, 2), table(w1, i), bottom, top))
    for i in range(1, 11):
        fix = now[(i - 5) // 2 + REACH][0][0]
        put_row(u1, i, [[t + fix for t in line] for line in row_of(u1, i, 2)])
    for source, target, low, high in ((u1, u2, 2, 10), (u2, u3, 3, 9)):
        for i in range(low, high):
            rows = [row_of(source, i + d, 2) for d in (0, -1, 1)]
            put_row(target, i, swept(*rows, row_of(u0, i, 2), table(w1, i), bottom, top))

    def corrected_row(i):
        fix = row_of(u3, (i - 4 + 8) // 2 + 1, 2)
        now_row = row_of(v1, i)
        put_row(v1, i, [[now_row[q][p] + fix[q // 2][p // 2] for p in range(4)] for q in range(4)])

    for i in range(1, 11):
        corrected_row(i)
    smooth_rows(v1, v2, 2, 10)
    smooth_rows(v2, v3, 3, 9)

    arrive(potential_copies)

    def terrain_row(x):
        w = table(w0, x + 4)
        a, a_west, a_east = (row_of(v3, x + 4 + d) for d in (0, -1, 1))
        b, b_west, b_east = (field_row(ps, x + 1 + d) for d in (0, -1, 1))
        zeros = jnp.zeros((8, 128), jnp.float32)
        by_z, by_west, by_east, by_north = ([zeros] * 4 for _ in range(4))
        for q in range(4):
            for p in range(4):
                by_z[p] += (above(a, q, p, top) - a[q][p]) * (above(b, q, p, top) - b[q][p])
                by_west[p] += (a[q][p] - a_west[q][p]) * (b[q][p] - b_west[q][p])
                by_east[p] += (a_east[q][p] - a[q][p]) * (b_east[q][p] - b[q][p])
                by_north[p] += (north_of(a, q, p) - a[q][p]) * (north_of(b, q, p) - b[q][p])
        out = []
        for p in range(4):
            by_south = by_north[p - 1] if p else pltpu.roll(by_north[3], 1, 1)
            total = w(GW, p) * by_west[p] + w(GE, p) * by_east[p] + w(GN, p) * by_north[p]
            total = total + w(GS, p) * by_south + w(GZ, p) * by_z[p]
            out.append(jnp.sum(total, axis=0, keepdims=True))
        return out

    sums = [terrain_row(x) for x in range(4)]
    blank = jnp.zeros((4, 128), jnp.float32)
    packed = [jnp.concatenate([sums[x][p] for x in range(4)] + [blank], axis=0) for p in range(4)]
    for c, tile in enumerate(join_lanes(packed)):
        gn[c] = tile
    dir_copies = []
    for step in range(1, n_dir):
        target = lax.rem(me_dir + step, n_dir)
        dir_copies.append(copy_to(gn.at[target // (n_dir // 4)], er.at[step - 1], {"dir": target}))
        dir_copies[-1].start()

    def natural_row(x):
        now_row = row_of(v3, x + 4)
        for p in range(4):
            for q in range(4):
                mixed[x, p, pl.ds(q, 8, stride=4), :] = now_row[q][p]
        for c, tile in enumerate(join_lanes([mixed[x, p] for p in range(4)])):
            a_out[x, :, 128 * c : 128 * c + 128] = tile

    for i in range(0, 4):
        natural_row(i)
    out_copy = pltpu.make_async_copy(a_out, adjoint.at[0], local_sem.at[3])
    out_copy.start()

    for copy in dir_copies:
        copy.wait_recv()
    total = gn[me_dir // (n_dir // 4)]
    for step in range(1, n_dir):
        total = total + er[step - 1]
    part = lax.rem(me_dir, n_dir // 4)
    mine = total
    width = gradient.shape[1]
    for k in range(1, 128 // width):
        mine = jnp.where(iota((8, 128), 0) * 0 + part == k, pltpu.roll(total, 128 - k * width, 1), mine)
    gradient[...] = mine[0:4, 0:width]

    out_copy.wait()
    for copy in dir_copies:
        copy.wait_send()
    for copy, _, home, _, _ in end_depths + end_copies:
        pl.when(me == home)(copy.wait_send)
    for offset, copies in by_offset.items():

        @pl.when(inside(offset))
        def _():
            for copy in copies:
                copy.wait_send()


def body(cotangent, potential, height):
    n_dir, n_gx = lax.axis_size("dir"), lax.axis_size("gx")
    f32 = jnp.float32
    shapes = [
        (4, 512), (4, 32, 512), (4, 32, 512), (4, 32, 512), (4, 4, 32, 128),
        (7, 16, 128), (12, 4, 32, 128), (6, 4, 32, 128), (4, 32, 128), (14, 4, 16, 128),
        (2, 32, 128), (2, 24, 128), (9, 2, 16, 128), (24, 128), (3, 8, 128), (32, 128), (9, 1, 24, 128),
        (12, 16, 8, 128), (12, 16, 8, 128), (12, 16, 8, 128), (12, 16, 8, 128),
        (13, 8, 128), (7, 8, 128), (7, 8, 128), (2, 8, 128), (2, 8, 128), (1, 8, 128), (1, 8, 128), (3, 8, 128), (6, 3, 8, 128), (2, 8, 128), (2, 8, 128), (14, 4, 8, 128),
        (12, 4, 8, 128), (12, 4, 8, 128), (12, 4, 8, 128), (12, 4, 8, 128),
        (4, 8, 128), (n_dir - 1, 8, 128),
    ]
    copies = 6 + 2 + 2 + 2 + 6 + 6 + 6 + 6 + 6 + n_dir - 1
    return pl.pallas_call(
        functools.partial(kernel, n_dir, n_gx),
        out_shape=(
            pltpu.VMEM(cotangent.shape, f32),
            pltpu.VMEM((height.shape[0], height.shape[1] // n_dir), f32),
        ),
        in_specs=[pl.BlockSpec(memory_space=pltpu.HBM)] * 3,
        out_specs=(pl.BlockSpec(memory_space=pl.ANY), pl.BlockSpec(memory_space=pltpu.VMEM)),
        scratch_shapes=[pltpu.VMEM(shape, f32) for shape in shapes]
        + [pltpu.SemaphoreType.DMA((4,)), pltpu.SemaphoreType.DMA((copies,)), pltpu.SemaphoreType.DMA((copies,))],
        compiler_params=pltpu.CompilerParams(
            collective_id=0, has_side_effects=True, vmem_limit_bytes=60 * 1024 * 1024
        ),
        name="vcycle",
    )(cotangent, potential, height)


def solution(mesh):
    placed = (P("dir", "gx", None, None), P("dir", "gx", None, None), P("gx", None))
    return jax.shard_map(
        body,
        mesh=mesh,
        in_specs=placed,
        out_specs=(P("dir", "gx", None, None), P("gx", "dir")),
        check_vma=False,
    )
```

```python
import functools

import jax
import jax.numpy as jnp
from jax import lax
from jax.experimental import pallas as pl
from jax.experimental.pallas import tpu as pltpu
from jax.sharding import PartitionSpec as P

MESH = pl.DeviceIdType.MESH
DAMPING = 0.7
ANISOTROPY = 4.0
CEILING = 1.5
REACH = 9
GREET = 4
C, CW, CE, CS, CN, CZ, RHO, SIG, DINV = range(9)
GW, GE, GS, GN, GZ = range(9, 14)


def iota(shape, dim):
    return lax.broadcasted_iota(jnp.int32, shape, dim)


def spread_lanes(cols):
    shape = cols[0].shape
    lane = iota(shape, 1)
    block, inner = lane >> 5, lane & 31
    turned = [
        jnp.take_along_axis(col, 4 * inner + ((block - c) & 3), axis=1, mode="promise_in_bounds")
        for c, col in enumerate(cols)
    ]
    out = []
    for p in range(4):
        mixed = turned[(3 - p) % 4]
        for b in range(3):
            mixed = jnp.where(block == b, turned[(b - p) % 4], mixed)
        out.append(mixed if p == 0 else pltpu.roll(mixed, 128 - 32 * p, 1))
    return out


def join_lanes(classes):
    shape = classes[0].shape
    lane = iota(shape, 1)
    block = lane >> 5
    turned = [cl if p == 0 else pltpu.roll(cl, 32 * p, 1) for p, cl in enumerate(classes)]
    out = []
    for c in range(4):
        mixed = turned[(3 - c) % 4]
        for b in range(3):
            mixed = jnp.where(block == b, turned[(b - c) % 4], mixed)
        source = (((lane + c) & 3) << 5) + (lane >> 2)
        out.append(jnp.take_along_axis(mixed, source, axis=1, mode="promise_in_bounds"))
    return out


def harmonic(a, b, scale):
    return scale * 2.0 * a * b / (a + b)


def level_weights(mid, west, east, open_west, open_east, scale):
    count = len(mid)
    lane = iota(mid[0].shape, 1)
    w_west = [jnp.where(open_west, harmonic(a, b, scale), 0.0) for a, b in zip(mid, west)]
    w_east = [jnp.where(open_east, harmonic(a, b, scale), 0.0) for a, b in zip(mid, east)]
    w_north = [harmonic(mid[p], mid[p + 1], scale) for p in range(count - 1)]
    last = harmonic(mid[count - 1], pltpu.roll(mid[0], 127, 1), scale)
    w_north.append(jnp.where(lane < 127, last, 0.0))
    w_south = [pltpu.roll(w_north[count - 1], 1, 1)] + w_north[:-1]
    out = []
    for p in range(count):
        w_z = (scale * ANISOTROPY) / mid[p]
        low = w_west[p] + w_east[p] + w_south[p] + w_north[p] + w_z
        full = low + w_z
        c = DAMPING / full
        out.append(
            (c, c * w_west[p], c * w_east[p], c * w_south[p], c * w_north[p], c * w_z, full / low, low / full, full / DAMPING)
        )
    return out


def terrain_weights(mid, west, east, open_west, open_east):
    lane = iota(mid[0].shape, 1)

    def share(own, other):
        both = own + other
        return 2.0 * other * other / (both * both)

    out = []
    for p in range(4):
        south = mid[p - 1] if p else pltpu.roll(mid[3], 1, 1)
        north = mid[p + 1] if p < 3 else pltpu.roll(mid[0], 127, 1)
        g_south, g_north = share(mid[p], south), share(mid[p], north)
        out.append(
            (
                jnp.where(open_west, share(mid[p], west[p]), 0.0),
                jnp.where(open_east, share(mid[p], east[p]), 0.0),
                g_south if p else jnp.where(lane > 0, g_south, 0.0),
                g_north if p < 3 else jnp.where(lane < 127, g_north, 0.0),
                -ANISOTROPY / (mid[p] * mid[p]),
            )
        )
    return out


def north_of(v, q, p):
    return v[q][p + 1] if p + 1 < len(v[q]) else pltpu.roll(v[q][0], 127, 1)


def south_of(v, q, p):
    return v[q][p - 1] if p else pltpu.roll(v[q][-1], 1, 1)


def above(v, q, p, top):
    return v[q + 1][p] if q + 1 < len(v) else jnp.where(top, 0.0, pltpu.roll(v[0][p], 7, 0))


def below(v, q, p, bottom):
    return v[q - 1][p] if q else jnp.where(bottom, 0.0, pltpu.roll(v[-1][p], 1, 0))


def around(v, v_west, v_east, w, bottom, top):
    out = []
    for q in range(len(v)):
        line = []
        for p in range(len(v[q])):
            total = w(CZ, p) * (above(v, q, p, top) + below(v, q, p, bottom))
            total = total + w(CS, p) * south_of(v, q, p) + w(CN, p) * north_of(v, q, p)
            if v_west is not None:
                total = total + w(CW, p) * v_west[q][p]
            if v_east is not None:
                total = total + w(CE, p) * v_east[q][p]
            line.append(total)
        out.append(line)
    return out


def swept(v, v_west, v_east, start, w, bottom, top):
    near = around(v, v_west, v_east, w, bottom, top)
    out = []
    for q in range(len(v)):
        line = []
        for p in range(len(v[q])):
            move = near[q][p] if q else near[q][p] * jnp.where(bottom, w(RHO, p), 1.0)
            line.append((1.0 - DAMPING) * v[q][p] + start[q][p] + move)
        out.append(line)
    return out


def restricted(v, v_west, v_east, start, w, bottom, top):
    near = around(v, v_west, v_east, w, bottom, top)
    half = len(v) // 2
    out = [[0.0] * half for _ in range(half)]
    for q1 in range(half):
        for p in range(len(v)):
            part = 0.0
            for q in (2 * q1, 2 * q1 + 1):
                own = -DAMPING * v[q][p] if start is None else start[q][p] - DAMPING * v[q][p]
                if q == 0:
                    own = own * jnp.where(bottom, w(SIG, p), 1.0)
                part = part + (near[q][p] + own)
            out[q1][p // 2] = out[q1][p // 2] + w(DINV, p) * part
    return out


def edge_restricted(v, kind, w):
    half = len(v) // 2
    return [
        [sum((w(DINV, p) * w(kind, p)) * (v[2 * q1][p] + v[2 * q1 + 1][p]) for p in (2 * p1, 2 * p1 + 1)) for p1 in range(half)]
        for q1 in range(half)
    ]


def edge_swept(v, kind, w, bottom):
    return [
        [w(kind, p) * (v[q][p] if q else v[q][p] * jnp.where(bottom, w(RHO, p), 1.0)) for p in range(len(v[q]))]
        for q in range(len(v))
    ]


def added(a, b):
    return [[s + t for s, t in zip(x, y)] for x, y in zip(a, b)]


def first_guess(f, w, bottom):
    return [
        [w(C, p) * (f[q][p] if q else f[q][p] * jnp.where(bottom, w(RHO, p), 1.0)) for p in range(len(f[q]))]
        for q in range(len(f))
    ]


def grid_of(block, count):
    return [[block[q * count + p] for p in range(count)] for q in range(count)]


def table(ref, row):
    @functools.cache
    def weight(kind, p):
        return ref[kind, p, pl.ds(row, 1), :]

    return weight


def put_row(ref, row, tiles):
    count = len(tiles)
    for q in range(count):
        for p in range(count):
            ref[row, q * count + p] = tiles[q][p]


def kernel(
    n_dir, n_gx,
    cot, pot, height, adjoint, gradient,
    h_in, c_in, p_in, a_out, mixed,
    hs, fs, ps, ds, w0, de, d1, w1, df, d2s, d2, w2,
    v0, v1, v2, v3,
    packet, from_west, from_east, from_west2, from_east2, from_west3, from_east3, f2own, f2r, end_row, end_depth, f1,
    gn, er, es,
    local_sem, send_sem, recv_sem,
):
    me_dir, me = lax.axis_index("dir"), lax.axis_index("gx")

    def inside(offset):
        return me + offset < n_gx if offset > 0 else me + offset >= 0

    barrier = pltpu.get_barrier_semaphore()
    greetings = n_dir - 1
    for offset in [o for s in range(1, GREET + 1) for o in (-s, s)]:

        @pl.when(inside(offset))
        def _():
            pl.semaphore_signal(barrier, inc=1, device_id={"gx": me + offset}, device_id_type=MESH)

        greetings = greetings + inside(offset).astype(jnp.int32)

    for offset in (-1, 1):

        @pl.when(inside(offset))
        def _():
            for step in range(1, n_dir):
                there = {"dir": lax.rem(me_dir + step, n_dir), "gx": me + offset}
                pl.semaphore_signal(barrier, inc=1, device_id=there, device_id_type=MESH)

        greetings = greetings + (n_dir - 1) * inside(offset).astype(jnp.int32)
    for step in range(1, n_dir):
        pl.semaphore_signal(
            barrier, inc=1, device_id={"dir": lax.rem(me_dir + step, n_dir)}, device_id_type=MESH
        )

    height_in = pltpu.make_async_copy(height, h_in, local_sem.at[0])
    cot_in = pltpu.make_async_copy(cot.at[0], c_in, local_sem.at[1])
    pot_in = pltpu.make_async_copy(pot.at[0], p_in, local_sem.at[2])
    height_in.start()
    cot_in.start()
    pot_in.start()

    sent, by_offset = [], {}

    def copy_to(source, target, device):
        index = len(sent)
        copy = pltpu.make_async_remote_copy(
            src_ref=source, dst_ref=target, send_sem=send_sem.at[index], recv_sem=recv_sem.at[index],
            device_id=device, device_id_type=MESH,
        )
        sent.append(copy)
        return copy

    def send(source, target, offset):
        copy = copy_to(source, target, {"gx": me + offset})
        by_offset.setdefault(offset, []).append(copy)
        pl.when(inside(offset))(copy.start)
        return copy, target, offset

    def arrive(copies, filler=0.0):
        for copy, target, offset in copies:

            @pl.when(inside(-offset))
            def _():
                copy.wait_recv()

            @pl.when(jnp.logical_not(inside(-offset)))
            def _():
                target[...] = jnp.full(target.shape, filler, jnp.float32)

    bottom, top = iota((8, 128), 0) == 0, iota((8, 128), 0) == 7

    for p in range(4):
        ds[p, 24:32, :] = jnp.ones((8, 128), jnp.float32)
    d2[...] = jnp.ones(d2.shape, jnp.float32)
    d1[...] = jnp.ones(d1.shape, jnp.float32)

    height_in.wait()
    raw = h_in[...]
    for p, cl in enumerate(spread_lanes([raw[:, 128 * c : 128 * c + 128] for c in range(4)])):
        hs[3, 4 * p : 4 * p + 4, :] = CEILING - cl

    pl.semaphore_wait(barrier, greetings)
    depth_copies = [send(hs.at[3], hs.at[3 - o], o) for o in (-1, 1, -2, 2, -3, 3)]

    def spread_row(source, target, row, slot):
        block = source[row]
        for p, cl in enumerate(spread_lanes([block[:, 128 * c : 128 * c + 128] for c in range(4)])):
            target[slot, p] = cl

    cot_in.wait()
    for x in range(0, 4):
        spread_row(c_in, fs, x, x + 4)
    field_copies = [
        send(fs.at[pl.ds(4, 3)], fs.at[pl.ds(8, 3)], -1),
        send(fs.at[pl.ds(5, 3)], fs.at[pl.ds(1, 3)], 1),
    ]

    pot_in.wait()
    for x in range(0, 4):
        spread_row(p_in, ps, x, x + 1)
    potential_copies = [send(ps.at[1], ps.at[5], -1), send(ps.at[4], ps.at[0], 1)]

    def field_row(ref, slot):
        return [[ref[slot, p, pl.ds(q, 8, stride=4), :] for p in range(4)] for q in range(4)]

    arrive(depth_copies, 1.0)
    for o in range(7):
        for p in range(4):
            ds[p, 4 * o : 4 * o + 4, :] = hs[o, 4 * p : 4 * p + 4, :]
    for p1 in range(2):
        de[p1] = ds[2 * p1] + ds[2 * p1 + 1]
    for p1 in range(2):
        d1[p1, 0:16, :] = 0.25 * (de[p1, pl.ds(0, 16, stride=2), :] + de[p1, pl.ds(1, 16, stride=2), :])
    df[...] = d1[0] + d1[1]
    d2s[1] = 0.25 * (df[pl.ds(0, 8, stride=2), :] + df[pl.ds(1, 8, stride=2), :])
    d2_copies = [send(d2s.at[1], d2s.at[1 - s], 7 * s) for s in (-1, 1)]
    end_depths = []
    for end, (home, sign) in enumerate(((0, 1), (n_gx - 1, -1))):
        for away in (4, 5, 6):
            copy = copy_to(d2s.at[1], end_depth.at[end], {"gx": me + sign * away})
            pl.when(me == home)(copy.start)
            end_depths.append((copy, end, home, home + sign * away, 7 - sign * away))

    def faces(rows, per_strip, first):
        size = n_gx * per_strip
        place = (me * per_strip + first + REACH * size + iota((rows, 128), 0)) & (size - 1)
        return place != 0, place != size - 1

    open_west, open_east = faces(16, 4, -4)
    mid = [ds[p, 8:24, :] for p in range(4)]
    west = [ds[p, 7:23, :] for p in range(4)]
    east = [ds[p, 9:25, :] for p in range(4)]
    for p, kinds in enumerate(level_weights(mid, west, east, open_west, open_east, 1.0)):
        for kind, value in enumerate(kinds):
            w0[kind, p] = value
    open_west, open_east = faces(16, 2, -5)
    mid1 = [d1[p, 1:17, :] for p in range(2)]
    west1 = [d1[p, 0:16, :] for p in range(2)]
    east1 = [d1[p, 2:18, :] for p in range(2)]
    for p, kinds in enumerate(level_weights(mid1, west1, east1, open_west, open_east, 2.0)):
        for kind, value in enumerate(kinds):
            w1[kind, p] = value

    def guess_row(i):
        put_row(v0, i, first_guess(field_row(fs, i), table(w0, i), bottom))

    def row_of(ref, i, count=4):
        return grid_of(ref[i], count)

    def smooth_rows(source, target, low, high):
        have = {i: row_of(source, i) for i in range(low - 1, high + 1)}
        for i in range(low, high):
            put_row(target, i, swept(have[i], have[i - 1], have[i + 1], row_of(v0, i), table(w0, i), bottom, top))

    for i in range(4, 8):
        guess_row(i)
    have = [None] + [row_of(v0, i) for i in range(4, 8)] + [None]
    put_row(v1, 3, edge_swept(have[1], CE, table(w0, 3), bottom))
    for i in range(4, 8):
        put_row(v1, i, swept(have[i - 3], have[i - 4], have[i - 2], have[i - 3], table(w0, i), bottom, top))
    put_row(v1, 8, edge_swept(have[4], CW, table(w0, 8), bottom))
    have = [None] + [row_of(v1, i) for i in range(3, 9)] + [None]
    rest = {i: restricted(have[i - 2], have[i - 3], have[i - 1], row_of(v0, i) if 4 <= i <= 7 else None, table(w0, i), bottom, top) for i in range(3, 9)}
    rest[2] = edge_restricted(have[1], CE, table(w0, 2))
    rest[9] = edge_restricted(have[6], CW, table(w0, 9))
    f1p = [added(rest[2 * i + 2], rest[2 * i + 3]) for i in range(4)]
    for q in range(2):
        for p in range(2):
            packet[2 * q + p] = f1p[0][q][p]
            packet[9 + 2 * q + p] = f1p[3][q][p]

    begin = {i: first_guess(f1p[i - 4], table(w1, i), bottom) for i in range(4, 8)}
    next_row = {i: swept(begin[i], begin.get(i - 1), begin.get(i + 1), begin[i], table(w1, i), bottom, top) for i in range(4, 8)}
    next_row[3] = edge_swept(begin[4], CE, table(w1, 3), bottom)
    next_row[8] = edge_swept(begin[7], CW, table(w1, 8), bottom)
    rest = {
        i: restricted(next_row[i], next_row.get(i - 1), next_row.get(i + 1), begin.get(i), table(w1, i), bottom, top)
        for i in range(3, 9)
    }
    rest[2] = edge_restricted(next_row[3], CE, table(w1, 2))
    rest[9] = edge_restricted(next_row[8], CW, table(w1, 9))
    f2p = [sum(rest[i][0][0] for i in rows) for rows in ((2,), (3, 4), (5, 6), (7, 8), (9,))]
    for k in range(5):
        packet[4 + k] = f2p[k]
    sum_copies = [
        send(packet.at[pl.ds(0, 7)], from_east, -1),
        send(packet.at[pl.ds(6, 7)], from_west, 1),
        send(packet.at[pl.ds(4, 2)], from_east2, -2),
        send(packet.at[pl.ds(7, 2)], from_west2, 2),
        send(packet.at[4], from_east3.at[0], -3),
        send(packet.at[8], from_west3.at[0], 3),
    ]

    arrive(d2_copies, 1.0)
    d2[0:8, :] = d2s[0]
    d2[7:15, :] = d2s[1]
    d2[14:22, :] = d2s[2]
    for copy, end, _, place, first in end_depths:

        @pl.when(me == place)
        def _():
            copy.wait_recv()
            d2[first : first + 7, :] = end_depth[end, 0:7, :]

    open_west, open_east = faces(24, 1, -9)
    for kind, value in enumerate(
        level_weights([d2[1:25, :]], [d2[0:24, :]], [d2[2:26, :]], open_west, open_east, 4.0)[0]
    ):
        w2[kind, 0] = value

    arrive(sum_copies)
    f2own[0] = (f2p[1] + from_west[0]) + (from_east[4] + from_west2[0]) + from_west3[0]
    f2own[1] = (f2p[2] + from_west[1]) + (from_east[5] + from_west2[1]) + from_east2[0]
    f2own[2] = (f2p[3] + from_west[2]) + (from_east[6] + from_east2[1]) + from_east3[0]
    slots = (-9, -6, -3, 3, 6, 9)
    row_copies = [
        send(f2own.at[pl.ds(0, 2)], f2r.at[5, pl.ds(0, 2)], -9),
        send(f2own.at[pl.ds(1, 2)], f2r.at[0, pl.ds(1, 2)], 9),
    ]
    row_copies += [send(f2own, f2r.at[slots.index(-o)], o) for o in (-6, 6, -3, 3)]
    end_copies = []
    for end, (home, sign) in enumerate(((0, 1), (n_gx - 1, -1))):
        for block in (3, 6, 9):
            copy = copy_to(f2own.at[1], end_row.at[end], {"gx": me + sign * (block - 1)})
            pl.when(me == home)(copy.start)
            end_copies.append((copy, end, home, home + sign * (block - 1), slots.index(-sign * block)))
    for q in range(2):
        for p in range(2):
            f1[6, 2 * q + p] = f1p[1][q][p] + from_west[3 + 2 * q + p]
            f1[7, 2 * q + p] = f1p[2][q][p] + from_east[2 * q + p]
    terrain = terrain_weights(
        [ds[p, 8:24, :] for p in range(4)], [ds[p, 7:23, :] for p in range(4)], [ds[p, 9:25, :] for p in range(4)],
        *faces(16, 4, -4),
    )
    for p, kinds in enumerate(terrain):
        for kind, value in enumerate(kinds):
            w0[GW + kind, p] = value
    arrive(field_copies)
    for i in range(1, 4):
        guess_row(i)
    for i in range(8, 11):
        guess_row(i)
    smooth_rows(v0, v1, 2, 10)
    f1_copies = [send(f1.at[pl.ds(6, 2)], f1.at[pl.ds(6 - 2 * o, 2)], o) for o in (-1, 1, -2, 2)]

    arrive(row_copies)
    for copy, end, _, place, slot in end_copies:

        @pl.when(me == place)
        def _():
            copy.wait_recv()
            f2r[slot, 2 - 2 * end] = end_row[end]

    start = []
    for o in range(-REACH, REACH + 1):
        block = (o + 10) // 3 * 3 - 9
        source = f2own[o + 1] if block == 0 else f2r[slots.index(block), o - block + 1]
        start.append(first_guess([[source]], table(w2, o + REACH), bottom))
    now = start
    for sweep in range(7):
        later = [None] * len(now)
        for i in range(sweep + 1, len(now) - sweep - 1):
            later[i] = swept(now[i], now[i - 1], now[i + 1], start[i], table(w2, i), bottom, top)
        now = later

    arrive(f1_copies)
    begin = {i: first_guess(grid_of(f1[i + 1], 2), table(w1, i), bottom) for i in range(1, 11)}
    fixed = {}
    for i in range(2, 10):
        fix = now[(i - 5) // 2 + REACH][0][0]
        row = swept(begin[i], begin[i - 1], begin[i + 1], begin[i], table(w1, i), bottom, top)
        fixed[i] = [[t + fix for t in line] for line in row]
    for low, high in ((3, 9), (4, 8)):
        fixed = {
            i: swept(fixed[i], fixed[i - 1], fixed[i + 1], begin[i], table(w1, i), bottom, top) for i in range(low, high)
        }

    have = {i: row_of(v1, i) for i in range(2, 10)}
    for i in range(2, 10):
        fix = fixed[(i - 4 + 8) // 2 + 1]
        put_row(v3, i, [[have[i][q][p] + fix[q // 2][p // 2] for p in range(4)] for q in range(4)])
    smooth_rows(v3, v2, 3, 9)
    smooth_rows(v2, v1, 4, 8)

    arrive(potential_copies)

    def terrain_row(x):
        w = table(w0, x + 4)
        a = row_of(v1, x + 4)
        a_west, a_east = (row_of(v1, x + 4 + d) if 0 <= x + d <= 3 else None for d in (-1, 1))
        b, b_west, b_east = (field_row(ps, x + 1 + d) for d in (0, -1, 1))
        zeros = jnp.zeros((8, 128), jnp.float32)
        by_z, by_west, by_east, by_north = ([zeros] * 4 for _ in range(4))
        for q in range(4):
            for p in range(4):
                by_z[p] += (above(a, q, p, top) - a[q][p]) * (above(b, q, p, top) - b[q][p])
                rise = a[q][p] - a_west[q][p] if a_west else a[q][p]
                by_west[p] += rise * (b[q][p] - b_west[q][p])
                rise = a_east[q][p] - a[q][p] if a_east else -a[q][p]
                by_east[p] += rise * (b_east[q][p] - b[q][p])
                by_north[p] += (north_of(a, q, p) - a[q][p]) * (north_of(b, q, p) - b[q][p])
        out = []
        for p in range(4):
            by_south = by_north[p - 1] if p else pltpu.roll(by_north[3], 1, 1)
            total = w(GW, p) * by_west[p] + w(GE, p) * by_east[p] + w(GN, p) * by_north[p]
            total = total + w(GS, p) * by_south + w(GZ, p) * by_z[p]
            out.append(total)
        if x == 0:
            parts[0] = [table(w0, 3)(GE, p) * by_west[p] for p in range(4)]
        if x == 3:
            parts[5] = [table(w0, 8)(GW, p) * by_east[p] for p in range(4)]
        parts[x + 1] = out

    parts = {}
    for x in range(4):
        terrain_row(x)
    blank = jnp.zeros((2, 128), jnp.float32)
    packed = [
        jnp.concatenate([jnp.sum(parts[k][p], axis=0, keepdims=True) for k in range(6)] + [blank], axis=0) for p in range(4)
    ]
    for c, tile in enumerate(join_lanes(packed)):
        gn[c] = tile
    dir_copies, side_copies = [], {-1: [], 1: []}
    for step in range(n_dir):
        target = lax.rem(me_dir + step, n_dir)
        source = gn.at[target // (n_dir // 4)]
        if step:
            dir_copies.append(copy_to(source, er.at[step - 1], {"dir": target}))
            dir_copies[-1].start()
        for offset, slot in ((-1, 1), (1, 0)):
            there = {"dir": target, "gx": me + offset}
            side_copies[offset].append(copy_to(source, es.at[slot, step], there))
    for offset in (-1, 1):

        @pl.when(inside(offset))
        def _():
            for copy in side_copies[offset]:
                copy.start()

    def natural_row(x):
        now_row = row_of(v1, x + 4)
        for p in range(4):
            for q in range(4):
                mixed[x, p, pl.ds(q, 8, stride=4), :] = now_row[q][p]
        for c, tile in enumerate(join_lanes([mixed[x, p] for p in range(4)])):
            a_out[x, :, 128 * c : 128 * c + 128] = tile

    for i in range(0, 4):
        natural_row(i)
    out_copy = pltpu.make_async_copy(a_out, adjoint.at[0], local_sem.at[3])
    out_copy.start()

    for copy in dir_copies:
        copy.wait_recv()
    total = gn[me_dir // (n_dir // 4)]
    for step in range(1, n_dir):
        total = total + er[step - 1]
    for offset, slot, row, place in ((1, 0, 5, 1), (-1, 1, 0, 4)):

        @pl.when(inside(-offset))
        def _():
            for copy in side_copies[offset]:
                copy.wait_recv()

        @pl.when(jnp.logical_not(inside(-offset)))
        def _():
            es[slot] = jnp.zeros(es.shape[1:], jnp.float32)

        side = es[slot, 0]
        for step in range(1, n_dir):
            side = side + es[slot, step]
        total = total + jnp.where(iota((8, 128), 0) == place, pltpu.roll(side, (place - row) % 8, 0), 0.0)
    part = lax.rem(me_dir, n_dir // 4)
    mine = total
    width = gradient.shape[1]
    for k in range(1, 128 // width):
        mine = jnp.where(iota((8, 128), 0) * 0 + part == k, pltpu.roll(total, 128 - k * width, 1), mine)
    gradient[...] = mine[1:5, 0:width]

    out_copy.wait()
    for copy in dir_copies:
        copy.wait_send()
    for offset in (-1, 1):

        @pl.when(inside(offset))
        def _():
            for copy in side_copies[offset]:
                copy.wait_send()

    for copy, _, home, _, _ in end_depths + end_copies:
        pl.when(me == home)(copy.wait_send)
    for offset, copies in by_offset.items():

        @pl.when(inside(offset))
        def _():
            for copy in copies:
                copy.wait_send()


def body(cotangent, potential, height):
    n_dir, n_gx = lax.axis_size("dir"), lax.axis_size("gx")
    f32 = jnp.float32
    shapes = [
        (4, 512), (4, 32, 512), (4, 32, 512), (4, 32, 512), (4, 4, 32, 128),
        (7, 16, 128), (12, 4, 32, 128), (6, 4, 32, 128), (4, 32, 128), (14, 4, 16, 128),
        (2, 32, 128), (2, 24, 128), (9, 2, 16, 128), (24, 128), (3, 8, 128), (32, 128), (9, 1, 24, 128),
        (12, 16, 8, 128), (12, 16, 8, 128), (12, 16, 8, 128), (12, 16, 8, 128),
        (13, 8, 128), (7, 8, 128), (7, 8, 128), (2, 8, 128), (2, 8, 128), (1, 8, 128), (1, 8, 128), (3, 8, 128), (6, 3, 8, 128), (2, 8, 128), (2, 8, 128), (14, 4, 8, 128),
        (4, 8, 128), (n_dir - 1, 8, 128), (2, n_dir, 8, 128),
    ]
    copies = 6 + 2 + 2 + 2 + 6 + 6 + 6 + 6 + 4 + n_dir - 1 + 2 * n_dir
    return pl.pallas_call(
        functools.partial(kernel, n_dir, n_gx),
        out_shape=(
            pltpu.VMEM(cotangent.shape, f32),
            pltpu.VMEM((height.shape[0], height.shape[1] // n_dir), f32),
        ),
        in_specs=[pl.BlockSpec(memory_space=pltpu.HBM)] * 3,
        out_specs=(pl.BlockSpec(memory_space=pl.ANY), pl.BlockSpec(memory_space=pltpu.VMEM)),
        scratch_shapes=[pltpu.VMEM(shape, f32) for shape in shapes]
        + [pltpu.SemaphoreType.DMA((4,)), pltpu.SemaphoreType.DMA((copies,)), pltpu.SemaphoreType.DMA((copies,))],
        compiler_params=pltpu.CompilerParams(
            collective_id=0, has_side_effects=True, vmem_limit_bytes=60 * 1024 * 1024
        ),
        name="vcycle",
    )(cotangent, potential, height)


def solution(mesh):
    placed = (P("dir", "gx", None, None), P("dir", "gx", None, None), P("gx", None))
    return jax.shard_map(
        body,
        mesh=mesh,
        in_specs=placed,
        out_specs=(P("dir", "gx", None, None), P("gx", "dir")),
        check_vma=False,
    )
```

```python
import functools

import jax
import jax.numpy as jnp
from jax import lax
from jax.experimental import pallas as pl
from jax.experimental.pallas import tpu as pltpu
from jax.sharding import PartitionSpec as P

MESH = pl.DeviceIdType.MESH
DAMPING = 0.7
ANISOTROPY = 4.0
CEILING = 1.5
REACH = 9
GREET = 4
C, CW, CE, CS, CN, CZ, RHO, SIG, DINV = range(9)
GW, GE, GS, GN, GZ = range(9, 14)


def iota(shape, dim):
    return lax.broadcasted_iota(jnp.int32, shape, dim)


def spread_lanes(cols):
    shape = cols[0].shape
    lane = iota(shape, 1)
    block, inner = lane >> 5, lane & 31
    turned = [
        jnp.take_along_axis(col, 4 * inner + ((block - c) & 3), axis=1, mode="promise_in_bounds")
        for c, col in enumerate(cols)
    ]
    out = []
    for p in range(4):
        mixed = turned[(3 - p) % 4]
        for b in range(3):
            mixed = jnp.where(block == b, turned[(b - p) % 4], mixed)
        out.append(mixed if p == 0 else pltpu.roll(mixed, 128 - 32 * p, 1))
    return out


def join_lanes(classes):
    shape = classes[0].shape
    lane = iota(shape, 1)
    block = lane >> 5
    turned = [cl if p == 0 else pltpu.roll(cl, 32 * p, 1) for p, cl in enumerate(classes)]
    out = []
    for c in range(4):
        mixed = turned[(3 - c) % 4]
        for b in range(3):
            mixed = jnp.where(block == b, turned[(b - c) % 4], mixed)
        source = (((lane + c) & 3) << 5) + (lane >> 2)
        out.append(jnp.take_along_axis(mixed, source, axis=1, mode="promise_in_bounds"))
    return out


def harmonic(a, b, scale):
    return scale * 2.0 * a * b / (a + b)


def level_weights(mid, west, east, open_west, open_east, scale):
    count = len(mid)
    lane = iota(mid[0].shape, 1)
    w_west = [jnp.where(open_west, harmonic(a, b, scale), 0.0) for a, b in zip(mid, west)]
    w_east = [jnp.where(open_east, harmonic(a, b, scale), 0.0) for a, b in zip(mid, east)]
    w_north = [harmonic(mid[p], mid[p + 1], scale) for p in range(count - 1)]
    last = harmonic(mid[count - 1], pltpu.roll(mid[0], 127, 1), scale)
    w_north.append(jnp.where(lane < 127, last, 0.0))
    w_south = [pltpu.roll(w_north[count - 1], 1, 1)] + w_north[:-1]
    out = []
    for p in range(count):
        w_z = (scale * ANISOTROPY) / mid[p]
        low = w_west[p] + w_east[p] + w_south[p] + w_north[p] + w_z
        full = low + w_z
        c = DAMPING / full
        out.append(
            (c, c * w_west[p], c * w_east[p], c * w_south[p], c * w_north[p], c * w_z, full / low, low / full, full / DAMPING)
        )
    return out


def terrain_weights(mid, west, east, open_west, open_east):
    lane = iota(mid[0].shape, 1)

    def share(own, other):
        both = own + other
        return 2.0 * other * other / (both * both)

    out = []
    for p in range(4):
        south = mid[p - 1] if p else pltpu.roll(mid[3], 1, 1)
        north = mid[p + 1] if p < 3 else pltpu.roll(mid[0], 127, 1)
        g_south, g_north = share(mid[p], south), share(mid[p], north)
        out.append(
            (
                jnp.where(open_west, share(mid[p], west[p]), 0.0),
                jnp.where(open_east, share(mid[p], east[p]), 0.0),
                g_south if p else jnp.where(lane > 0, g_south, 0.0),
                g_north if p < 3 else jnp.where(lane < 127, g_north, 0.0),
                -ANISOTROPY / (mid[p] * mid[p]),
            )
        )
    return out


def north_of(v, q, p):
    return v[q][p + 1] if p + 1 < len(v[q]) else pltpu.roll(v[q][0], 127, 1)


def south_of(v, q, p):
    return v[q][p - 1] if p else pltpu.roll(v[q][-1], 1, 1)


def above(v, q, p, top):
    return v[q + 1][p] if q + 1 < len(v) else jnp.where(top, 0.0, pltpu.roll(v[0][p], 7, 0))


def below(v, q, p, bottom):
    return v[q - 1][p] if q else jnp.where(bottom, 0.0, pltpu.roll(v[-1][p], 1, 0))


def around(v, v_west, v_east, w, bottom, top):
    out = []
    for q in range(len(v)):
        line = []
        for p in range(len(v[q])):
            total = w(CZ, p) * (above(v, q, p, top) + below(v, q, p, bottom))
            total = total + w(CS, p) * south_of(v, q, p) + w(CN, p) * north_of(v, q, p)
            if v_west is not None:
                total = total + w(CW, p) * v_west[q][p]
            if v_east is not None:
                total = total + w(CE, p) * v_east[q][p]
            line.append(total)
        out.append(line)
    return out


def swept(v, v_west, v_east, start, w, bottom, top):
    near = around(v, v_west, v_east, w, bottom, top)
    out = []
    for q in range(len(v)):
        line = []
        for p in range(len(v[q])):
            move = near[q][p] if q else near[q][p] * jnp.where(bottom, w(RHO, p), 1.0)
            line.append((1.0 - DAMPING) * v[q][p] + start[q][p] + move)
        out.append(line)
    return out


def restricted(v, v_west, v_east, start, w, bottom, top):
    near = around(v, v_west, v_east, w, bottom, top)
    half = len(v) // 2
    out = [[0.0] * half for _ in range(half)]
    for q1 in range(half):
        for p in range(len(v)):
            part = 0.0
            for q in (2 * q1, 2 * q1 + 1):
                own = -DAMPING * v[q][p] if start is None else start[q][p] - DAMPING * v[q][p]
                if q == 0:
                    own = own * jnp.where(bottom, w(SIG, p), 1.0)
                part = part + (near[q][p] + own)
            out[q1][p // 2] = out[q1][p // 2] + w(DINV, p) * part
    return out


def edge_restricted(v, kind, w):
    half = len(v) // 2
    return [
        [sum((w(DINV, p) * w(kind, p)) * (v[2 * q1][p] + v[2 * q1 + 1][p]) for p in (2 * p1, 2 * p1 + 1)) for p1 in range(half)]
        for q1 in range(half)
    ]


def edge_swept(v, kind, w, bottom):
    return [
        [w(kind, p) * (v[q][p] if q else v[q][p] * jnp.where(bottom, w(RHO, p), 1.0)) for p in range(len(v[q]))]
        for q in range(len(v))
    ]


def added(a, b):
    return [[s + t for s, t in zip(x, y)] for x, y in zip(a, b)]


def first_guess(f, w, bottom):
    return [
        [w(C, p) * (f[q][p] if q else f[q][p] * jnp.where(bottom, w(RHO, p), 1.0)) for p in range(len(f[q]))]
        for q in range(len(f))
    ]


def grid_of(block, count):
    return [[block[q * count + p] for p in range(count)] for q in range(count)]


def table(ref, row):
    @functools.cache
    def weight(kind, p):
        return ref[kind, p, pl.ds(row, 1), :]

    return weight


def put_row(ref, row, tiles):
    count = len(tiles)
    for q in range(count):
        for p in range(count):
            ref[row, q * count + p] = tiles[q][p]


def kernel(
    n_dir, n_gx,
    cot, pot, height, adjoint, gradient,
    h_in, c_in, p_in, a_out, mixed,
    hs, fs, ps, ds, w0, de, d1, w1, df, d2s, d2, w2,
    v0, v1, v2, v3,
    packet, from_west, from_east, from_west2, from_east2, from_west3, from_east3, f2own, f2r, end_row, end_depth, f1,
    gn, er,
    local_sem, send_sem, recv_sem,
):
    me_dir, me = lax.axis_index("dir"), lax.axis_index("gx")

    def inside(offset):
        return me + offset < n_gx if offset > 0 else me + offset >= 0

    barrier = pltpu.get_barrier_semaphore()
    greetings = n_dir - 1
    for offset in [o for s in range(1, GREET + 1) for o in (-s, s)]:

        @pl.when(inside(offset))
        def _():
            pl.semaphore_signal(barrier, inc=1, device_id={"gx": me + offset}, device_id_type=MESH)

        greetings = greetings + inside(offset).astype(jnp.int32)
    for step in range(1, n_dir):
        pl.semaphore_signal(
            barrier, inc=1, device_id={"dir": lax.rem(me_dir + step, n_dir)}, device_id_type=MESH
        )

    height_in = pltpu.make_async_copy(height, h_in, local_sem.at[0])
    cot_in = pltpu.make_async_copy(cot.at[0], c_in, local_sem.at[1])
    pot_in = pltpu.make_async_copy(pot.at[0], p_in, local_sem.at[2])
    height_in.start()
    cot_in.start()
    pot_in.start()

    sent, by_offset = [], {}

    def copy_to(source, target, device):
        index = len(sent)
        copy = pltpu.make_async_remote_copy(
            src_ref=source, dst_ref=target, send_sem=send_sem.at[index], recv_sem=recv_sem.at[index],
            device_id=device, device_id_type=MESH,
        )
        sent.append(copy)
        return copy

    def send(source, target, offset):
        copy = copy_to(source, target, {"gx": me + offset})
        by_offset.setdefault(offset, []).append(copy)
        pl.when(inside(offset))(copy.start)
        return copy, target, offset

    def arrive(copies):
        for copy, _, offset in copies:
            pl.when(inside(-offset))(copy.wait_recv)

    slots = (-9, -6, -3, 3, 6, 9)
    for offset, ones, zeros in (
        (-1, (hs.at[2],), (fs.at[pl.ds(0, 4)], ps.at[0], from_west, f1.at[pl.ds(4, 2)])),
        (1, (hs.at[4],), (fs.at[pl.ds(8, 4)], ps.at[5], from_east, f1.at[pl.ds(8, 2)])),
        (-2, (hs.at[1],), (from_west2, f1.at[pl.ds(2, 2)])),
        (2, (hs.at[5],), (from_east2, f1.at[pl.ds(10, 2)])),
        (-3, (hs.at[0],), (from_west3, f1.at[1], f2r.at[2])),
        (3, (hs.at[6],), (from_east3, f1.at[12], f2r.at[3])),
        (-6, (), (f2r.at[1],)),
        (6, (), (f2r.at[4],)),
        (-7, (d2s.at[0],), ()),
        (7, (d2s.at[2],), ()),
        (-9, (), (f2r.at[0, pl.ds(1, 2)],)),
        (9, (), (f2r.at[5, pl.ds(0, 2)],)),
    ):

        @pl.when(jnp.logical_not(inside(offset)))
        def _():
            for ref in ones:
                ref[...] = jnp.ones(ref.shape, jnp.float32)
            for ref in zeros:
                ref[...] = jnp.zeros(ref.shape, jnp.float32)

    bottom, top = iota((8, 128), 0) == 0, iota((8, 128), 0) == 7

    for p in range(4):
        ds[p, 24:32, :] = jnp.ones((8, 128), jnp.float32)
    d2[...] = jnp.ones(d2.shape, jnp.float32)
    d1[...] = jnp.ones(d1.shape, jnp.float32)

    height_in.wait()
    raw = h_in[...]
    for p, cl in enumerate(spread_lanes([raw[:, 128 * c : 128 * c + 128] for c in range(4)])):
        hs[3, 4 * p : 4 * p + 4, :] = CEILING - cl

    pl.semaphore_wait(barrier, greetings)
    depth_copies = [send(hs.at[3], hs.at[3 - o], o) for o in (-3, 3, -2, 2, -1, 1)]

    def spread_row(source, target, row, slot):
        block = source[row]
        for p, cl in enumerate(spread_lanes([block[:, 128 * c : 128 * c + 128] for c in range(4)])):
            target[slot, p] = cl

    cot_in.wait()
    for x in range(0, 4):
        spread_row(c_in, fs, x, x + 4)
    field_copies = [
        send(fs.at[pl.ds(4, 4)], fs.at[pl.ds(4 - 4 * o, 4)], o) for o in (-1, 1)
    ]

    pot_in.wait()
    for x in range(0, 4):
        spread_row(p_in, ps, x, x + 1)
    potential_copies = [send(ps.at[1], ps.at[5], -1), send(ps.at[4], ps.at[0], 1)]

    def field_row(ref, slot):
        return [[ref[slot, p, pl.ds(q, 8, stride=4), :] for p in range(4)] for q in range(4)]

    arrive(depth_copies)
    for o in range(7):
        for p in range(4):
            ds[p, 4 * o : 4 * o + 4, :] = hs[o, 4 * p : 4 * p + 4, :]
    for p1 in range(2):
        de[p1] = ds[2 * p1] + ds[2 * p1 + 1]
    for p1 in range(2):
        d1[p1, 0:16, :] = 0.25 * (de[p1, pl.ds(0, 16, stride=2), :] + de[p1, pl.ds(1, 16, stride=2), :])
    df[...] = d1[0] + d1[1]
    d2s[1] = 0.25 * (df[pl.ds(0, 8, stride=2), :] + df[pl.ds(1, 8, stride=2), :])
    def faces(rows, per_strip, first):
        size = n_gx * per_strip
        place = (me * per_strip + first + REACH * size + iota((rows, 128), 0)) & (size - 1)
        return place != 0, place != size - 1

    open_west, open_east = faces(16, 4, -4)
    mid = [ds[p, 8:24, :] for p in range(4)]
    west = [ds[p, 7:23, :] for p in range(4)]
    east = [ds[p, 9:25, :] for p in range(4)]
    for p, kinds in enumerate(level_weights(mid, west, east, open_west, open_east, 1.0)):
        for kind, value in enumerate(kinds):
            w0[kind, p] = value
    open_west, open_east = faces(16, 2, -5)
    mid1 = [d1[p, 1:17, :] for p in range(2)]
    west1 = [d1[p, 0:16, :] for p in range(2)]
    east1 = [d1[p, 2:18, :] for p in range(2)]
    for p, kinds in enumerate(level_weights(mid1, west1, east1, open_west, open_east, 2.0)):
        for kind, value in enumerate(kinds):
            w1[kind, p] = value

    def guess_row(i):
        put_row(v0, i, first_guess(field_row(fs, i), table(w0, i), bottom))

    def row_of(ref, i, count=4):
        return grid_of(ref[i], count)

    def smooth_rows(source, target, low, high):
        have = {i: row_of(source, i) for i in range(low - 1, high + 1)}
        for i in range(low, high):
            put_row(target, i, swept(have[i], have[i - 1], have[i + 1], row_of(v0, i), table(w0, i), bottom, top))

    for i in range(4, 8):
        guess_row(i)
    have = [None] + [row_of(v0, i) for i in range(4, 8)] + [None]
    put_row(v1, 3, edge_swept(have[1], CE, table(w0, 3), bottom))
    for i in range(4, 8):
        put_row(v1, i, swept(have[i - 3], have[i - 4], have[i - 2], have[i - 3], table(w0, i), bottom, top))
    put_row(v1, 8, edge_swept(have[4], CW, table(w0, 8), bottom))
    have = [None] + [row_of(v1, i) for i in range(3, 9)] + [None]
    rest = {i: restricted(have[i - 2], have[i - 3], have[i - 1], row_of(v0, i) if 4 <= i <= 7 else None, table(w0, i), bottom, top) for i in range(3, 9)}
    rest[2] = edge_restricted(have[1], CE, table(w0, 2))
    rest[9] = edge_restricted(have[6], CW, table(w0, 9))
    f1p = [added(rest[2 * i + 2], rest[2 * i + 3]) for i in range(4)]
    for q in range(2):
        for p in range(2):
            packet[2 * q + p] = f1p[0][q][p]
            packet[9 + 2 * q + p] = f1p[3][q][p]

    begin = {i: first_guess(f1p[i - 4], table(w1, i), bottom) for i in range(4, 8)}
    next_row = {i: swept(begin[i], begin.get(i - 1), begin.get(i + 1), begin[i], table(w1, i), bottom, top) for i in range(4, 8)}
    next_row[3] = edge_swept(begin[4], CE, table(w1, 3), bottom)
    next_row[8] = edge_swept(begin[7], CW, table(w1, 8), bottom)
    rest = {
        i: restricted(next_row[i], next_row.get(i - 1), next_row.get(i + 1), begin.get(i), table(w1, i), bottom, top)
        for i in range(3, 9)
    }
    rest[2] = edge_restricted(next_row[3], CE, table(w1, 2))
    rest[9] = edge_restricted(next_row[8], CW, table(w1, 9))
    f2p = [sum(rest[i][0][0] for i in rows) for rows in ((2,), (3, 4), (5, 6), (7, 8), (9,))]
    for k in range(5):
        packet[4 + k] = f2p[k]
    sum_copies = [
        send(packet.at[pl.ds(0, 7)], from_east, -1),
        send(packet.at[pl.ds(6, 7)], from_west, 1),
        send(packet.at[pl.ds(4, 2)], from_east2, -2),
        send(packet.at[pl.ds(7, 2)], from_west2, 2),
        send(packet.at[4], from_east3.at[0], -3),
        send(packet.at[8], from_west3.at[0], 3),
    ]

    d2_copies = [send(d2s.at[1], d2s.at[1 - s], 7 * s) for s in (-1, 1)]
    end_depths = []
    for end, (home, sign) in enumerate(((0, 1), (n_gx - 1, -1))):
        for away in (4, 5, 6):
            copy = copy_to(d2s.at[1], end_depth.at[end], {"gx": me + sign * away})
            pl.when(me == home)(copy.start)
            end_depths.append((copy, end, home, home + sign * away, 7 - sign * away))

    arrive(sum_copies)
    f2own[0] = (f2p[1] + from_west[0]) + (from_east[4] + from_west2[0]) + from_west3[0]
    f2own[1] = (f2p[2] + from_west[1]) + (from_east[5] + from_west2[1]) + from_east2[0]
    f2own[2] = (f2p[3] + from_west[2]) + (from_east[6] + from_east2[1]) + from_east3[0]
    row_copies = [
        send(f2own.at[pl.ds(0, 2)], f2r.at[5, pl.ds(0, 2)], -9),
        send(f2own.at[pl.ds(1, 2)], f2r.at[0, pl.ds(1, 2)], 9),
    ]
    row_copies += [send(f2own, f2r.at[slots.index(-o)], o) for o in (-6, 6, -3, 3)]
    end_copies = []
    for end, (home, sign) in enumerate(((0, 1), (n_gx - 1, -1))):
        for block in (3, 6, 9):
            copy = copy_to(f2own.at[1], end_row.at[end], {"gx": me + sign * (block - 1)})
            pl.when(me == home)(copy.start)
            end_copies.append((copy, end, home, home + sign * (block - 1), slots.index(-sign * block)))
    for q in range(2):
        for p in range(2):
            f1[6, 2 * q + p] = f1p[1][q][p] + from_west[3 + 2 * q + p]
            f1[7, 2 * q + p] = f1p[2][q][p] + from_east[2 * q + p]
    arrive(d2_copies)
    d2[0:8, :] = d2s[0]
    d2[7:15, :] = d2s[1]
    d2[14:22, :] = d2s[2]
    for copy, end, _, place, first in end_depths:

        @pl.when(me == place)
        def _():
            copy.wait_recv()
            d2[first : first + 7, :] = end_depth[end, 0:7, :]

    open_west, open_east = faces(24, 1, -9)
    for kind, value in enumerate(
        level_weights([d2[1:25, :]], [d2[0:24, :]], [d2[2:26, :]], open_west, open_east, 4.0)[0]
    ):
        w2[kind, 0] = value

    terrain = terrain_weights(
        [ds[p, 8:24, :] for p in range(4)], [ds[p, 7:23, :] for p in range(4)], [ds[p, 9:25, :] for p in range(4)],
        *faces(16, 4, -4),
    )
    for p, kinds in enumerate(terrain):
        for kind, value in enumerate(kinds):
            w0[GW + kind, p] = value
    arrive(field_copies)
    for i in range(0, 4):
        guess_row(i)
    for i in range(8, 12):
        guess_row(i)
    smooth_rows(v0, v1, 1, 11)
    f1_copies = [send(f1.at[pl.ds(6, 2)], f1.at[pl.ds(6 - 2 * o, 2)], o) for o in (-1, 1, -2, 2)]
    f1_copies += [send(f1.at[6], f1.at[12], -3), send(f1.at[7], f1.at[1], 3)]

    arrive(row_copies)
    for copy, end, _, place, slot in end_copies:

        @pl.when(me == place)
        def _():
            copy.wait_recv()
            f2r[slot, 2 - 2 * end] = end_row[end]

    start = []
    for o in range(-REACH, REACH + 1):
        block = (o + 10) // 3 * 3 - 9
        source = f2own[o + 1] if block == 0 else f2r[slots.index(block), o - block + 1]
        start.append(first_guess([[source]], table(w2, o + REACH), bottom))
    now = start
    for sweep in range(7):
        later = [None] * len(now)
        for i in range(sweep + 1, len(now) - sweep - 1):
            later[i] = swept(now[i], now[i - 1], now[i + 1], start[i], table(w2, i), bottom, top)
        now = later

    arrive(f1_copies)
    begin = {i: first_guess(grid_of(f1[i + 1], 2), table(w1, i), bottom) for i in range(0, 12)}
    fixed = {}
    for i in range(1, 11):
        fix = now[(i - 5) // 2 + REACH][0][0]
        row = swept(begin[i], begin[i - 1], begin[i + 1], begin[i], table(w1, i), bottom, top)
        fixed[i] = [[t + fix for t in line] for line in row]
    for low, high in ((2, 10), (3, 9)):
        fixed = {
            i: swept(fixed[i], fixed[i - 1], fixed[i + 1], begin[i], table(w1, i), bottom, top) for i in range(low, high)
        }

    have = {i: row_of(v1, i) for i in range(1, 11)}
    for i in range(1, 11):
        fix = fixed[(i - 4 + 8) // 2 + 1]
        put_row(v3, i, [[have[i][q][p] + fix[q // 2][p // 2] for p in range(4)] for q in range(4)])
    smooth_rows(v3, v2, 2, 10)
    smooth_rows(v2, v1, 3, 9)

    arrive(potential_copies)

    def terrain_row(x):
        w = table(w0, x + 4)
        a, a_west, a_east = (row_of(v1, x + 4 + d) for d in (0, -1, 1))
        b, b_west, b_east = (field_row(ps, x + 1 + d) for d in (0, -1, 1))
        zeros = jnp.zeros((8, 128), jnp.float32)
        by_z, by_west, by_east, by_north = ([zeros] * 4 for _ in range(4))
        for q in range(4):
            for p in range(4):
                by_z[p] += (above(a, q, p, top) - a[q][p]) * (above(b, q, p, top) - b[q][p])
                by_west[p] += (a[q][p] - a_west[q][p]) * (b[q][p] - b_west[q][p])
                by_east[p] += (a_east[q][p] - a[q][p]) * (b_east[q][p] - b[q][p])
                by_north[p] += (north_of(a, q, p) - a[q][p]) * (north_of(b, q, p) - b[q][p])
        out = []
        for p in range(4):
            by_south = by_north[p - 1] if p else pltpu.roll(by_north[3], 1, 1)
            total = w(GW, p) * by_west[p] + w(GE, p) * by_east[p] + w(GN, p) * by_north[p]
            total = total + w(GS, p) * by_south + w(GZ, p) * by_z[p]
            out.append(jnp.sum(total, axis=0, keepdims=True))
        return out

    sums = [terrain_row(x) for x in range(4)]
    blank = jnp.zeros((4, 128), jnp.float32)
    packed = [jnp.concatenate([sums[x][p] for x in range(4)] + [blank], axis=0) for p in range(4)]
    for c, tile in enumerate(join_lanes(packed)):
        gn[c] = tile
    dir_copies = []
    for step in sorted(range(1, n_dir), key=lambda k: abs(2 * k - n_dir)):
        target = lax.rem(me_dir + step, n_dir)
        dir_copies.append(copy_to(gn.at[target // (n_dir // 4)], er.at[step - 1], {"dir": target}))
        dir_copies[-1].start()

    def natural_row(x):
        now_row = row_of(v1, x + 4)
        for p in range(4):
            for q in range(4):
                mixed[x, p, pl.ds(q, 8, stride=4), :] = now_row[q][p]
        for c, tile in enumerate(join_lanes([mixed[x, p] for p in range(4)])):
            a_out[x, :, 128 * c : 128 * c + 128] = tile

    for i in range(0, 4):
        natural_row(i)
    out_copy = pltpu.make_async_copy(a_out, adjoint.at[0], local_sem.at[3])
    out_copy.start()

    for copy, _, home, _, _ in end_depths + end_copies:
        pl.when(me == home)(copy.wait_send)
    for offset, copies in by_offset.items():

        @pl.when(inside(offset))
        def _():
            for copy in copies:
                copy.wait_send()

    for copy in dir_copies:
        copy.wait_recv()
    total = gn[me_dir // (n_dir // 4)]
    for step in range(1, n_dir):
        total = total + er[step - 1]
    part = lax.rem(me_dir, n_dir // 4)
    mine = total
    width = gradient.shape[1]
    for k in range(1, 128 // width):
        mine = jnp.where(iota((8, 128), 0) * 0 + part == k, pltpu.roll(total, 128 - k * width, 1), mine)
    gradient[...] = mine[0:4, 0:width]

    out_copy.wait()
    for copy in dir_copies:
        copy.wait_send()


def body(cotangent, potential, height):
    n_dir, n_gx = lax.axis_size("dir"), lax.axis_size("gx")
    f32 = jnp.float32
    shapes = [
        (4, 512), (4, 32, 512), (4, 32, 512), (4, 32, 512), (4, 4, 32, 128),
        (7, 16, 128), (12, 4, 32, 128), (6, 4, 32, 128), (4, 32, 128), (14, 4, 16, 128),
        (2, 32, 128), (2, 24, 128), (9, 2, 16, 128), (24, 128), (3, 8, 128), (32, 128), (9, 1, 24, 128),
        (12, 16, 8, 128), (12, 16, 8, 128), (12, 16, 8, 128), (12, 16, 8, 128),
        (13, 8, 128), (7, 8, 128), (7, 8, 128), (2, 8, 128), (2, 8, 128), (1, 8, 128), (1, 8, 128), (3, 8, 128), (6, 3, 8, 128), (2, 8, 128), (2, 8, 128), (14, 4, 8, 128),
        (4, 8, 128), (n_dir - 1, 8, 128),
    ]
    copies = 6 + 2 + 2 + 2 + 6 + 6 + 6 + 6 + 6 + n_dir - 1
    return pl.pallas_call(
        functools.partial(kernel, n_dir, n_gx),
        out_shape=(
            pltpu.VMEM(cotangent.shape, f32),
            pltpu.VMEM((height.shape[0], height.shape[1] // n_dir), f32),
        ),
        in_specs=[pl.BlockSpec(memory_space=pltpu.HBM)] * 3,
        out_specs=(pl.BlockSpec(memory_space=pl.ANY), pl.BlockSpec(memory_space=pltpu.VMEM)),
        scratch_shapes=[pltpu.VMEM(shape, f32) for shape in shapes]
        + [pltpu.SemaphoreType.DMA((4,)), pltpu.SemaphoreType.DMA((copies,)), pltpu.SemaphoreType.DMA((copies,))],
        compiler_params=pltpu.CompilerParams(
            collective_id=0, has_side_effects=True, vmem_limit_bytes=60 * 1024 * 1024
        ),
        name="vcycle",
    )(cotangent, potential, height)


def solution(mesh):
    placed = (P("dir", "gx", None, None), P("dir", "gx", None, None), P("gx", None))
    return jax.shard_map(
        body,
        mesh=mesh,
        in_specs=placed,
        out_specs=(P("dir", "gx", None, None), P("gx", "dir")),
        check_vma=False,
    )
```

```python
import functools

import jax
import jax.numpy as jnp
from jax import lax
from jax.experimental import pallas as pl
from jax.experimental.pallas import tpu as pltpu
from jax.sharding import PartitionSpec as P

MESH = pl.DeviceIdType.MESH
DAMPING = 0.7
ANISOTROPY = 4.0
CEILING = 1.5
REACH = 9
GREET = 4
C, CW, CE, CS, CN, CZ, RHO, SIG, DINV = range(9)
GW, GE, GS, GN, GZ = range(9, 14)


def iota(shape, dim):
    return lax.broadcasted_iota(jnp.int32, shape, dim)


def spread_lanes(cols):
    shape = cols[0].shape
    lane = iota(shape, 1)
    block, inner = lane >> 5, lane & 31
    turned = [
        jnp.take_along_axis(col, 4 * inner + ((block - c) & 3), axis=1, mode="promise_in_bounds")
        for c, col in enumerate(cols)
    ]
    out = []
    for p in range(4):
        mixed = turned[(3 - p) % 4]
        for b in range(3):
            mixed = jnp.where(block == b, turned[(b - p) % 4], mixed)
        out.append(mixed if p == 0 else pltpu.roll(mixed, 128 - 32 * p, 1))
    return out


def join_lanes(classes):
    shape = classes[0].shape
    lane = iota(shape, 1)
    block = lane >> 5
    turned = [cl if p == 0 else pltpu.roll(cl, 32 * p, 1) for p, cl in enumerate(classes)]
    out = []
    for c in range(4):
        mixed = turned[(3 - c) % 4]
        for b in range(3):
            mixed = jnp.where(block == b, turned[(b - c) % 4], mixed)
        source = (((lane + c) & 3) << 5) + (lane >> 2)
        out.append(jnp.take_along_axis(mixed, source, axis=1, mode="promise_in_bounds"))
    return out


def harmonic(a, b, scale):
    return scale * 2.0 * a * b / (a + b)


def level_weights(mid, west, east, open_west, open_east, scale):
    count = len(mid)
    lane = iota(mid[0].shape, 1)
    w_west = [jnp.where(open_west, harmonic(a, b, scale), 0.0) for a, b in zip(mid, west)]
    w_east = [jnp.where(open_east, harmonic(a, b, scale), 0.0) for a, b in zip(mid, east)]
    w_north = [harmonic(mid[p], mid[p + 1], scale) for p in range(count - 1)]
    last = harmonic(mid[count - 1], pltpu.roll(mid[0], 127, 1), scale)
    w_north.append(jnp.where(lane < 127, last, 0.0))
    w_south = [pltpu.roll(w_north[count - 1], 1, 1)] + w_north[:-1]
    out = []
    for p in range(count):
        w_z = (scale * ANISOTROPY) / mid[p]
        low = w_west[p] + w_east[p] + w_south[p] + w_north[p] + w_z
        full = low + w_z
        c = DAMPING / full
        out.append(
            (c, c * w_west[p], c * w_east[p], c * w_south[p], c * w_north[p], c * w_z, full / low, low / full, full / DAMPING)
        )
    return out


def terrain_weights(mid, west, east, open_west, open_east):
    lane = iota(mid[0].shape, 1)

    def share(own, other):
        both = own + other
        return 2.0 * other * other / (both * both)

    out = []
    for p in range(4):
        south = mid[p - 1] if p else pltpu.roll(mid[3], 1, 1)
        north = mid[p + 1] if p < 3 else pltpu.roll(mid[0], 127, 1)
        g_south, g_north = share(mid[p], south), share(mid[p], north)
        out.append(
            (
                jnp.where(open_west, share(mid[p], west[p]), 0.0),
                jnp.where(open_east, share(mid[p], east[p]), 0.0),
                g_south if p else jnp.where(lane > 0, g_south, 0.0),
                g_north if p < 3 else jnp.where(lane < 127, g_north, 0.0),
                -ANISOTROPY / (mid[p] * mid[p]),
            )
        )
    return out


def north_of(v, q, p):
    return v[q][p + 1] if p + 1 < len(v[q]) else pltpu.roll(v[q][0], 127, 1)


def south_of(v, q, p):
    return v[q][p - 1] if p else pltpu.roll(v[q][-1], 1, 1)


def above(v, q, p, top):
    return v[q + 1][p] if q + 1 < len(v) else jnp.where(top, 0.0, pltpu.roll(v[0][p], 7, 0))


def below(v, q, p, bottom):
    return v[q - 1][p] if q else jnp.where(bottom, 0.0, pltpu.roll(v[-1][p], 1, 0))


def around(v, v_west, v_east, w, bottom, top):
    out = []
    for q in range(len(v)):
        line = []
        for p in range(len(v[q])):
            total = w(CZ, p) * (above(v, q, p, top) + below(v, q, p, bottom))
            total = total + w(CS, p) * south_of(v, q, p) + w(CN, p) * north_of(v, q, p)
            if v_west is not None:
                total = total + w(CW, p) * v_west[q][p]
            if v_east is not None:
                total = total + w(CE, p) * v_east[q][p]
            line.append(total)
        out.append(line)
    return out


def swept(v, v_west, v_east, start, w, bottom, top):
    near = around(v, v_west, v_east, w, bottom, top)
    out = []
    for q in range(len(v)):
        line = []
        for p in range(len(v[q])):
            move = near[q][p] if q else near[q][p] * jnp.where(bottom, w(RHO, p), 1.0)
            line.append((1.0 - DAMPING) * v[q][p] + start[q][p] + move)
        out.append(line)
    return out


def restricted(v, v_west, v_east, start, w, bottom, top):
    near = around(v, v_west, v_east, w, bottom, top)
    half = len(v) // 2
    out = [[0.0] * half for _ in range(half)]
    for q1 in range(half):
        for p in range(len(v)):
            part = 0.0
            for q in (2 * q1, 2 * q1 + 1):
                own = -DAMPING * v[q][p] if start is None else start[q][p] - DAMPING * v[q][p]
                if q == 0:
                    own = own * jnp.where(bottom, w(SIG, p), 1.0)
                part = part + (near[q][p] + own)
            out[q1][p // 2] = out[q1][p // 2] + w(DINV, p) * part
    return out


def edge_restricted(v, kind, w):
    half = len(v) // 2
    return [
        [sum((w(DINV, p) * w(kind, p)) * (v[2 * q1][p] + v[2 * q1 + 1][p]) for p in (2 * p1, 2 * p1 + 1)) for p1 in range(half)]
        for q1 in range(half)
    ]


def edge_swept(v, kind, w, bottom):
    return [
        [w(kind, p) * (v[q][p] if q else v[q][p] * jnp.where(bottom, w(RHO, p), 1.0)) for p in range(len(v[q]))]
        for q in range(len(v))
    ]


def added(a, b):
    return [[s + t for s, t in zip(x, y)] for x, y in zip(a, b)]


def first_guess(f, w, bottom):
    return [
        [w(C, p) * (f[q][p] if q else f[q][p] * jnp.where(bottom, w(RHO, p), 1.0)) for p in range(len(f[q]))]
        for q in range(len(f))
    ]


def grid_of(block, count):
    return [[block[q * count + p] for p in range(count)] for q in range(count)]


def table(ref, row):
    @functools.cache
    def weight(kind, p):
        return ref[kind, p, pl.ds(row, 1), :]

    return weight


def put_row(ref, row, tiles):
    count = len(tiles)
    for q in range(count):
        for p in range(count):
            ref[row, q * count + p] = tiles[q][p]


def kernel(
    n_dir, n_gx,
    cot, pot, height, adjoint, gradient,
    h_in, c_in, p_in, a_out, mixed,
    hs, fs, ps, ds, w0, de, d1, w1, df, d2s, d2, w2,
    v0, v1, v2, v3,
    packet, from_west, from_east, from_west2, from_east2, from_west3, from_east3, f2own, f2r, end_row, end_depth, f1,
    gn, er,
    local_sem, send_sem, recv_sem,
):
    me_dir, me = lax.axis_index("dir"), lax.axis_index("gx")

    def inside(offset):
        return me + offset < n_gx if offset > 0 else me + offset >= 0

    barrier = pltpu.get_barrier_semaphore()
    greetings = n_dir - 1
    for offset in [o for s in range(1, GREET + 1) for o in (-s, s)]:

        @pl.when(inside(offset))
        def _():
            pl.semaphore_signal(barrier, inc=1, device_id={"gx": me + offset}, device_id_type=MESH)

        greetings = greetings + inside(offset).astype(jnp.int32)
    for step in range(1, n_dir):
        pl.semaphore_signal(
            barrier, inc=1, device_id={"dir": lax.rem(me_dir + step, n_dir)}, device_id_type=MESH
        )

    height_in = pltpu.make_async_copy(height, h_in, local_sem.at[0])
    cot_in = pltpu.make_async_copy(cot.at[0], c_in, local_sem.at[1])
    pot_in = pltpu.make_async_copy(pot.at[0], p_in, local_sem.at[2])
    height_in.start()
    cot_in.start()
    pot_in.start()

    sent, by_offset = [], {}

    def copy_to(source, target, device):
        index = len(sent)
        copy = pltpu.make_async_remote_copy(
            src_ref=source, dst_ref=target, send_sem=send_sem.at[index], recv_sem=recv_sem.at[index],
            device_id=device, device_id_type=MESH,
        )
        sent.append(copy)
        return copy

    def send(source, target, offset, start=True):
        copy = copy_to(source, target, {"gx": me + offset})
        by_offset.setdefault(offset, []).append(copy)
        if start:
            pl.when(inside(offset))(copy.start)
        return copy, target, offset

    def send_sides(to_west, to_east):
        copies = [send(*to_west, -1, start=False), send(*to_east, 1, start=False)]
        odd = lax.rem(me, 2) == 1
        pl.when(odd & inside(1))(copies[1][0].start)
        pl.when(inside(-1))(copies[0][0].start)
        pl.when(jnp.logical_not(odd) & inside(1))(copies[1][0].start)
        return copies

    def arrive(copies):
        for copy, _, offset in copies:
            pl.when(inside(-offset))(copy.wait_recv)

    slots = (-9, -6, -3, 3, 6, 9)
    for offset, ones, zeros in (
        (-1, (hs.at[2],), (fs.at[pl.ds(0, 4)], ps.at[0], from_west, f1.at[pl.ds(4, 2)])),
        (1, (hs.at[4],), (fs.at[pl.ds(8, 4)], ps.at[5], from_east, f1.at[pl.ds(8, 2)])),
        (-2, (hs.at[1],), (from_west2, f1.at[pl.ds(2, 2)])),
        (2, (hs.at[5],), (from_east2, f1.at[pl.ds(10, 2)])),
        (-3, (hs.at[0],), (from_west3, f1.at[1], f2r.at[2])),
        (3, (hs.at[6],), (from_east3, f1.at[12], f2r.at[3])),
        (-6, (), (f2r.at[1],)),
        (6, (), (f2r.at[4],)),
        (-7, (d2s.at[0],), ()),
        (7, (d2s.at[2],), ()),
        (-9, (), (f2r.at[0, pl.ds(1, 2)],)),
        (9, (), (f2r.at[5, pl.ds(0, 2)],)),
    ):

        @pl.when(jnp.logical_not(inside(offset)))
        def _():
            for ref in ones:
                ref[...] = jnp.ones(ref.shape, jnp.float32)
            for ref in zeros:
                ref[...] = jnp.zeros(ref.shape, jnp.float32)

    bottom, top = iota((8, 128), 0) == 0, iota((8, 128), 0) == 7

    for p in range(4):
        ds[p, 24:32, :] = jnp.ones((8, 128), jnp.float32)
    d2[...] = jnp.ones(d2.shape, jnp.float32)
    d1[...] = jnp.ones(d1.shape, jnp.float32)

    height_in.wait()
    raw = h_in[...]
    for p, cl in enumerate(spread_lanes([raw[:, 128 * c : 128 * c + 128] for c in range(4)])):
        hs[3, 4 * p : 4 * p + 4, :] = CEILING - cl

    pl.semaphore_wait(barrier, greetings)
    depth_copies = [send(hs.at[3], hs.at[3 - o], o) for o in (-3, 3, -2, 2, -1, 1)]

    def spread_row(source, target, row, slot):
        block = source[row]
        for p, cl in enumerate(spread_lanes([block[:, 128 * c : 128 * c + 128] for c in range(4)])):
            target[slot, p] = cl

    cot_in.wait()
    for x in range(0, 4):
        spread_row(c_in, fs, x, x + 4)
    field_copies = send_sides((fs.at[pl.ds(4, 4)], fs.at[pl.ds(8, 4)]), (fs.at[pl.ds(4, 4)], fs.at[pl.ds(0, 4)]))

    pot_in.wait()
    for x in range(0, 4):
        spread_row(p_in, ps, x, x + 1)
    potential_copies = send_sides((ps.at[1], ps.at[5]), (ps.at[4], ps.at[0]))

    def field_row(ref, slot):
        return [[ref[slot, p, pl.ds(q, 8, stride=4), :] for p in range(4)] for q in range(4)]

    arrive(depth_copies)
    for o in range(7):
        for p in range(4):
            ds[p, 4 * o : 4 * o + 4, :] = hs[o, 4 * p : 4 * p + 4, :]
    for p1 in range(2):
        de[p1] = ds[2 * p1] + ds[2 * p1 + 1]
    for p1 in range(2):
        d1[p1, 0:16, :] = 0.25 * (de[p1, pl.ds(0, 16, stride=2), :] + de[p1, pl.ds(1, 16, stride=2), :])
    df[...] = d1[0] + d1[1]
    d2s[1] = 0.25 * (df[pl.ds(0, 8, stride=2), :] + df[pl.ds(1, 8, stride=2), :])
    def faces(rows, per_strip, first):
        size = n_gx * per_strip
        place = (me * per_strip + first + REACH * size + iota((rows, 128), 0)) & (size - 1)
        return place != 0, place != size - 1

    open_west, open_east = faces(16, 4, -4)
    mid = [ds[p, 8:24, :] for p in range(4)]
    west = [ds[p, 7:23, :] for p in range(4)]
    east = [ds[p, 9:25, :] for p in range(4)]
    for p, kinds in enumerate(level_weights(mid, west, east, open_west, open_east, 1.0)):
        for kind, value in enumerate(kinds):
            w0[kind, p] = value
    open_west, open_east = faces(16, 2, -5)
    mid1 = [d1[p, 1:17, :] for p in range(2)]
    west1 = [d1[p, 0:16, :] for p in range(2)]
    east1 = [d1[p, 2:18, :] for p in range(2)]
    for p, kinds in enumerate(level_weights(mid1, west1, east1, open_west, open_east, 2.0)):
        for kind, value in enumerate(kinds):
            w1[kind, p] = value

    def guess_row(i):
        put_row(v0, i, first_guess(field_row(fs, i), table(w0, i), bottom))

    def row_of(ref, i, count=4):
        return grid_of(ref[i], count)

    def smooth_rows(source, target, low, high):
        have = {i: row_of(source, i) for i in range(low - 1, high + 1)}
        for i in range(low, high):
            put_row(target, i, swept(have[i], have[i - 1], have[i + 1], row_of(v0, i), table(w0, i), bottom, top))

    for i in range(4, 8):
        guess_row(i)
    have = [None] + [row_of(v0, i) for i in range(4, 8)] + [None]
    put_row(v1, 3, edge_swept(have[1], CE, table(w0, 3), bottom))
    for i in range(4, 8):
        put_row(v1, i, swept(have[i - 3], have[i - 4], have[i - 2], have[i - 3], table(w0, i), bottom, top))
    put_row(v1, 8, edge_swept(have[4], CW, table(w0, 8), bottom))
    have = [None] + [row_of(v1, i) for i in range(3, 9)] + [None]
    rest = {i: restricted(have[i - 2], have[i - 3], have[i - 1], row_of(v0, i) if 4 <= i <= 7 else None, table(w0, i), bottom, top) for i in range(3, 9)}
    rest[2] = edge_restricted(have[1], CE, table(w0, 2))
    rest[9] = edge_restricted(have[6], CW, table(w0, 9))
    f1p = [added(rest[2 * i + 2], rest[2 * i + 3]) for i in range(4)]
    for q in range(2):
        for p in range(2):
            packet[2 * q + p] = f1p[0][q][p]
            packet[9 + 2 * q + p] = f1p[3][q][p]

    begin = {i: first_guess(f1p[i - 4], table(w1, i), bottom) for i in range(4, 8)}
    next_row = {i: swept(begin[i], begin.get(i - 1), begin.get(i + 1), begin[i], table(w1, i), bottom, top) for i in range(4, 8)}
    next_row[3] = edge_swept(begin[4], CE, table(w1, 3), bottom)
    next_row[8] = edge_swept(begin[7], CW, table(w1, 8), bottom)
    rest = {
        i: restricted(next_row[i], next_row.get(i - 1), next_row.get(i + 1), begin.get(i), table(w1, i), bottom, top)
        for i in range(3, 9)
    }
    rest[2] = edge_restricted(next_row[3], CE, table(w1, 2))
    rest[9] = edge_restricted(next_row[8], CW, table(w1, 9))
    f2p = [sum(rest[i][0][0] for i in rows) for rows in ((2,), (3, 4), (5, 6), (7, 8), (9,))]
    for k in range(5):
        packet[4 + k] = f2p[k]
    sum_copies = [
        send(packet.at[pl.ds(0, 7)], from_east, -1),
        send(packet.at[pl.ds(6, 7)], from_west, 1),
        send(packet.at[pl.ds(4, 2)], from_east2, -2),
        send(packet.at[pl.ds(7, 2)], from_west2, 2),
        send(packet.at[4], from_east3.at[0], -3),
        send(packet.at[8], from_west3.at[0], 3),
    ]

    d2_copies = [send(d2s.at[1], d2s.at[1 - s], 7 * s) for s in (-1, 1)]
    end_depths = []
    for end, (home, sign) in enumerate(((0, 1), (n_gx - 1, -1))):
        for away in (4, 5, 6):
            copy = copy_to(d2s.at[1], end_depth.at[end], {"gx": me + sign * away})
            pl.when(me == home)(copy.start)
            end_depths.append((copy, end, home, home + sign * away, 7 - sign * away))

    arrive(sum_copies)
    f2own[0] = (f2p[1] + from_west[0]) + (from_east[4] + from_west2[0]) + from_west3[0]
    f2own[1] = (f2p[2] + from_west[1]) + (from_east[5] + from_west2[1]) + from_east2[0]
    f2own[2] = (f2p[3] + from_west[2]) + (from_east[6] + from_east2[1]) + from_east3[0]
    row_copies = [
        send(f2own.at[pl.ds(0, 2)], f2r.at[5, pl.ds(0, 2)], -9),
        send(f2own.at[pl.ds(1, 2)], f2r.at[0, pl.ds(1, 2)], 9),
    ]
    row_copies += [send(f2own, f2r.at[slots.index(-o)], o) for o in (-6, 6, -3, 3)]
    end_copies = []
    for end, (home, sign) in enumerate(((0, 1), (n_gx - 1, -1))):
        for block in (3, 6, 9):
            copy = copy_to(f2own.at[1], end_row.at[end], {"gx": me + sign * (block - 1)})
            pl.when(me == home)(copy.start)
            end_copies.append((copy, end, home, home + sign * (block - 1), slots.index(-sign * block)))
    for q in range(2):
        for p in range(2):
            f1[6, 2 * q + p] = f1p[1][q][p] + from_west[3 + 2 * q + p]
            f1[7, 2 * q + p] = f1p[2][q][p] + from_east[2 * q + p]
    arrive(d2_copies)
    d2[0:8, :] = d2s[0]
    d2[7:15, :] = d2s[1]
    d2[14:22, :] = d2s[2]
    for copy, end, _, place, first in end_depths:

        @pl.when(me == place)
        def _():
            copy.wait_recv()
            d2[first : first + 7, :] = end_depth[end, 0:7, :]

    open_west, open_east = faces(24, 1, -9)
    for kind, value in enumerate(
        level_weights([d2[1:25, :]], [d2[0:24, :]], [d2[2:26, :]], open_west, open_east, 4.0)[0]
    ):
        w2[kind, 0] = value

    terrain = terrain_weights(
        [ds[p, 8:24, :] for p in range(4)], [ds[p, 7:23, :] for p in range(4)], [ds[p, 9:25, :] for p in range(4)],
        *faces(16, 4, -4),
    )
    for p, kinds in enumerate(terrain):
        for kind, value in enumerate(kinds):
            w0[GW + kind, p] = value
    f1_copies = [send(f1.at[pl.ds(6, 2)], f1.at[pl.ds(6 - 2 * o, 2)], o) for o in (-1, 1, -2, 2)]
    f1_copies += [send(f1.at[6], f1.at[12], -3), send(f1.at[7], f1.at[1], 3)]
    arrive(field_copies)
    for i in range(0, 4):
        guess_row(i)
    for i in range(8, 12):
        guess_row(i)
    smooth_rows(v0, v1, 1, 11)

    arrive(row_copies)
    for copy, end, _, place, slot in end_copies:

        @pl.when(me == place)
        def _():
            copy.wait_recv()
            f2r[slot, 2 - 2 * end] = end_row[end]

    start = []
    for o in range(-REACH, REACH + 1):
        block = (o + 10) // 3 * 3 - 9
        source = f2own[o + 1] if block == 0 else f2r[slots.index(block), o - block + 1]
        start.append(first_guess([[source]], table(w2, o + REACH), bottom))
    now = start
    for sweep in range(7):
        later = [None] * len(now)
        for i in range(sweep + 1, len(now) - sweep - 1):
            later[i] = swept(now[i], now[i - 1], now[i + 1], start[i], table(w2, i), bottom, top)
        now = later

    arrive(f1_copies)
    begin = {i: first_guess(grid_of(f1[i + 1], 2), table(w1, i), bottom) for i in range(0, 12)}
    fixed = {}
    for i in range(1, 11):
        fix = now[(i - 5) // 2 + REACH][0][0]
        row = swept(begin[i], begin[i - 1], begin[i + 1], begin[i], table(w1, i), bottom, top)
        fixed[i] = [[t + fix for t in line] for line in row]
    for low, high in ((2, 10), (3, 9)):
        fixed = {
            i: swept(fixed[i], fixed[i - 1], fixed[i + 1], begin[i], table(w1, i), bottom, top) for i in range(low, high)
        }

    have = {i: row_of(v1, i) for i in range(1, 11)}
    for i in range(1, 11):
        fix = fixed[(i - 4 + 8) // 2 + 1]
        put_row(v3, i, [[have[i][q][p] + fix[q // 2][p // 2] for p in range(4)] for q in range(4)])
    smooth_rows(v3, v2, 2, 10)
    smooth_rows(v2, v1, 3, 9)

    arrive(potential_copies)

    def terrain_row(x):
        w = table(w0, x + 4)
        a, a_west, a_east = (row_of(v1, x + 4 + d) for d in (0, -1, 1))
        b, b_west, b_east = (field_row(ps, x + 1 + d) for d in (0, -1, 1))
        zeros = jnp.zeros((8, 128), jnp.float32)
        by_z, by_west, by_east, by_north = ([zeros] * 4 for _ in range(4))
        for q in range(4):
            for p in range(4):
                by_z[p] += (above(a, q, p, top) - a[q][p]) * (above(b, q, p, top) - b[q][p])
                by_west[p] += (a[q][p] - a_west[q][p]) * (b[q][p] - b_west[q][p])
                by_east[p] += (a_east[q][p] - a[q][p]) * (b_east[q][p] - b[q][p])
                by_north[p] += (north_of(a, q, p) - a[q][p]) * (north_of(b, q, p) - b[q][p])
        out = []
        for p in range(4):
            by_south = by_north[p - 1] if p else pltpu.roll(by_north[3], 1, 1)
            total = w(GW, p) * by_west[p] + w(GE, p) * by_east[p] + w(GN, p) * by_north[p]
            total = total + w(GS, p) * by_south + w(GZ, p) * by_z[p]
            out.append(jnp.sum(total, axis=0, keepdims=True))
        return out

    sums = [terrain_row(x) for x in range(4)]
    blank = jnp.zeros((4, 128), jnp.float32)
    packed = [jnp.concatenate([sums[x][p] for x in range(4)] + [blank], axis=0) for p in range(4)]
    for c, tile in enumerate(join_lanes(packed)):
        gn[c] = tile
    dir_copies = []
    for step in sorted(range(1, n_dir), key=lambda k: abs(2 * k - n_dir)):
        target = lax.rem(me_dir + step, n_dir)
        dir_copies.append(copy_to(gn.at[target // (n_dir // 4)], er.at[step - 1], {"dir": target}))
        dir_copies[-1].start()

    def natural_row(x):
        now_row = row_of(v1, x + 4)
        for p in range(4):
            for q in range(4):
                mixed[x, p, pl.ds(q, 8, stride=4), :] = now_row[q][p]
        for c, tile in enumerate(join_lanes([mixed[x, p] for p in range(4)])):
            a_out[x, :, 128 * c : 128 * c + 128] = tile

    for i in range(0, 4):
        natural_row(i)
    out_copy = pltpu.make_async_copy(a_out, adjoint.at[0], local_sem.at[3])
    out_copy.start()

    for copy, _, home, _, _ in end_depths + end_copies:
        pl.when(me == home)(copy.wait_send)
    for offset, copies in by_offset.items():

        @pl.when(inside(offset))
        def _():
            for copy in copies:
                copy.wait_send()

    for copy in dir_copies:
        copy.wait_recv()
    total = gn[me_dir // (n_dir // 4)]
    for step in range(1, n_dir):
        total = total + er[step - 1]
    part = lax.rem(me_dir, n_dir // 4)
    mine = total
    width = gradient.shape[1]
    for k in range(1, 128 // width):
        mine = jnp.where(iota((8, 128), 0) * 0 + part == k, pltpu.roll(total, 128 - k * width, 1), mine)
    gradient[...] = mine[0:4, 0:width]

    out_copy.wait()
    for copy in dir_copies:
        copy.wait_send()


def body(cotangent, potential, height):
    n_dir, n_gx = lax.axis_size("dir"), lax.axis_size("gx")
    f32 = jnp.float32
    shapes = [
        (4, 512), (4, 32, 512), (4, 32, 512), (4, 32, 512), (4, 4, 32, 128),
        (7, 16, 128), (12, 4, 32, 128), (6, 4, 32, 128), (4, 32, 128), (14, 4, 16, 128),
        (2, 32, 128), (2, 24, 128), (9, 2, 16, 128), (24, 128), (3, 8, 128), (32, 128), (9, 1, 24, 128),
        (12, 16, 8, 128), (12, 16, 8, 128), (12, 16, 8, 128), (12, 16, 8, 128),
        (13, 8, 128), (7, 8, 128), (7, 8, 128), (2, 8, 128), (2, 8, 128), (1, 8, 128), (1, 8, 128), (3, 8, 128), (6, 3, 8, 128), (2, 8, 128), (2, 8, 128), (14, 4, 8, 128),
        (4, 8, 128), (n_dir - 1, 8, 128),
    ]
    copies = 6 + 2 + 2 + 2 + 6 + 6 + 6 + 6 + 6 + n_dir - 1
    return pl.pallas_call(
        functools.partial(kernel, n_dir, n_gx),
        out_shape=(
            pltpu.VMEM(cotangent.shape, f32),
            pltpu.VMEM((height.shape[0], height.shape[1] // n_dir), f32),
        ),
        in_specs=[pl.BlockSpec(memory_space=pltpu.HBM)] * 3,
        out_specs=(pl.BlockSpec(memory_space=pl.ANY), pl.BlockSpec(memory_space=pltpu.VMEM)),
        scratch_shapes=[pltpu.VMEM(shape, f32) for shape in shapes]
        + [pltpu.SemaphoreType.DMA((4,)), pltpu.SemaphoreType.DMA((copies,)), pltpu.SemaphoreType.DMA((copies,))],
        compiler_params=pltpu.CompilerParams(
            collective_id=0, has_side_effects=True, vmem_limit_bytes=60 * 1024 * 1024
        ),
        name="vcycle",
    )(cotangent, potential, height)


def solution(mesh):
    placed = (P("dir", "gx", None, None), P("dir", "gx", None, None), P("gx", None))
    return jax.shard_map(
        body,
        mesh=mesh,
        in_specs=placed,
        out_specs=(P("dir", "gx", None, None), P("gx", "dir")),
        check_vma=False,
    )
```

```python
import functools

import jax
import jax.numpy as jnp
from jax import lax
from jax.experimental import pallas as pl
from jax.experimental.pallas import tpu as pltpu
from jax.sharding import PartitionSpec as P

MESH = pl.DeviceIdType.MESH
DAMPING = 0.7
ANISOTROPY = 4.0
CEILING = 1.5
REACH = 9
GREET = 4
C, CW, CE, CS, CN, CZ, RHO, SIG, DINV = range(9)
GW, GE, GS, GN, GZ = range(9, 14)


def iota(shape, dim):
    return lax.broadcasted_iota(jnp.int32, shape, dim)


def spread_lanes(cols):
    shape = cols[0].shape
    lane = iota(shape, 1)
    block, inner = lane >> 5, lane & 31
    turned = [
        jnp.take_along_axis(col, 4 * inner + ((block - c) & 3), axis=1, mode="promise_in_bounds")
        for c, col in enumerate(cols)
    ]
    out = []
    for p in range(4):
        mixed = turned[(3 - p) % 4]
        for b in range(3):
            mixed = jnp.where(block == b, turned[(b - p) % 4], mixed)
        out.append(mixed if p == 0 else pltpu.roll(mixed, 128 - 32 * p, 1))
    return out


def join_lanes(classes):
    shape = classes[0].shape
    lane = iota(shape, 1)
    block = lane >> 5
    turned = [cl if p == 0 else pltpu.roll(cl, 32 * p, 1) for p, cl in enumerate(classes)]
    out = []
    for c in range(4):
        mixed = turned[(3 - c) % 4]
        for b in range(3):
            mixed = jnp.where(block == b, turned[(b - c) % 4], mixed)
        source = (((lane + c) & 3) << 5) + (lane >> 2)
        out.append(jnp.take_along_axis(mixed, source, axis=1, mode="promise_in_bounds"))
    return out


def harmonic(a, b, scale):
    return scale * 2.0 * a * b / (a + b)


def level_weights(mid, west, east, open_west, open_east, scale):
    count = len(mid)
    lane = iota(mid[0].shape, 1)
    w_west = [jnp.where(open_west, harmonic(a, b, scale), 0.0) for a, b in zip(mid, west)]
    w_east = [jnp.where(open_east, harmonic(a, b, scale), 0.0) for a, b in zip(mid, east)]
    w_north = [harmonic(mid[p], mid[p + 1], scale) for p in range(count - 1)]
    last = harmonic(mid[count - 1], pltpu.roll(mid[0], 127, 1), scale)
    w_north.append(jnp.where(lane < 127, last, 0.0))
    w_south = [pltpu.roll(w_north[count - 1], 1, 1)] + w_north[:-1]
    out = []
    for p in range(count):
        w_z = (scale * ANISOTROPY) / mid[p]
        low = w_west[p] + w_east[p] + w_south[p] + w_north[p] + w_z
        full = low + w_z
        c = DAMPING / full
        out.append(
            (c, c * w_west[p], c * w_east[p], c * w_south[p], c * w_north[p], c * w_z, full / low, low / full, full / DAMPING)
        )
    return out


def terrain_weights(mid, west, east, open_west, open_east):
    lane = iota(mid[0].shape, 1)

    def share(own, other):
        both = own + other
        return 2.0 * other * other / (both * both)

    out = []
    for p in range(4):
        south = mid[p - 1] if p else pltpu.roll(mid[3], 1, 1)
        north = mid[p + 1] if p < 3 else pltpu.roll(mid[0], 127, 1)
        g_south, g_north = share(mid[p], south), share(mid[p], north)
        out.append(
            (
                jnp.where(open_west, share(mid[p], west[p]), 0.0),
                jnp.where(open_east, share(mid[p], east[p]), 0.0),
                g_south if p else jnp.where(lane > 0, g_south, 0.0),
                g_north if p < 3 else jnp.where(lane < 127, g_north, 0.0),
                -ANISOTROPY / (mid[p] * mid[p]),
            )
        )
    return out


def north_of(v, q, p):
    return v[q][p + 1] if p + 1 < len(v[q]) else pltpu.roll(v[q][0], 127, 1)


def south_of(v, q, p):
    return v[q][p - 1] if p else pltpu.roll(v[q][-1], 1, 1)


def above(v, q, p, top):
    return v[q + 1][p] if q + 1 < len(v) else jnp.where(top, 0.0, pltpu.roll(v[0][p], 7, 0))


def below(v, q, p, bottom):
    return v[q - 1][p] if q else jnp.where(bottom, 0.0, pltpu.roll(v[-1][p], 1, 0))


def around(v, v_west, v_east, w, bottom, top):
    out = []
    for q in range(len(v)):
        line = []
        for p in range(len(v[q])):
            total = w(CZ, p) * (above(v, q, p, top) + below(v, q, p, bottom))
            total = total + w(CS, p) * south_of(v, q, p) + w(CN, p) * north_of(v, q, p)
            if v_west is not None:
                total = total + w(CW, p) * v_west[q][p]
            if v_east is not None:
                total = total + w(CE, p) * v_east[q][p]
            line.append(total)
        out.append(line)
    return out


def swept(v, v_west, v_east, start, w, bottom, top):
    near = around(v, v_west, v_east, w, bottom, top)
    out = []
    for q in range(len(v)):
        line = []
        for p in range(len(v[q])):
            move = near[q][p] if q else near[q][p] * jnp.where(bottom, w(RHO, p), 1.0)
            line.append((1.0 - DAMPING) * v[q][p] + start[q][p] + move)
        out.append(line)
    return out


def restricted(v, v_west, v_east, start, w, bottom, top):
    near = around(v, v_west, v_east, w, bottom, top)
    half = len(v) // 2
    out = [[0.0] * half for _ in range(half)]
    for q1 in range(half):
        for p in range(len(v)):
            part = 0.0
            for q in (2 * q1, 2 * q1 + 1):
                own = -DAMPING * v[q][p] if start is None else start[q][p] - DAMPING * v[q][p]
                if q == 0:
                    own = own * jnp.where(bottom, w(SIG, p), 1.0)
                part = part + (near[q][p] + own)
            out[q1][p // 2] = out[q1][p // 2] + w(DINV, p) * part
    return out


def edge_restricted(v, kind, w):
    half = len(v) // 2
    return [
        [sum((w(DINV, p) * w(kind, p)) * (v[2 * q1][p] + v[2 * q1 + 1][p]) for p in (2 * p1, 2 * p1 + 1)) for p1 in range(half)]
        for q1 in range(half)
    ]


def edge_swept(v, kind, w, bottom):
    return [
        [w(kind, p) * (v[q][p] if q else v[q][p] * jnp.where(bottom, w(RHO, p), 1.0)) for p in range(len(v[q]))]
        for q in range(len(v))
    ]


def added(a, b):
    return [[s + t for s, t in zip(x, y)] for x, y in zip(a, b)]


def first_guess(f, w, bottom):
    return [
        [w(C, p) * (f[q][p] if q else f[q][p] * jnp.where(bottom, w(RHO, p), 1.0)) for p in range(len(f[q]))]
        for q in range(len(f))
    ]


def grid_of(block, count):
    return [[block[q * count + p] for p in range(count)] for q in range(count)]


def table(ref, row):
    @functools.cache
    def weight(kind, p):
        return ref[kind, p, pl.ds(row, 1), :]

    return weight


def put_row(ref, row, tiles):
    count = len(tiles)
    for q in range(count):
        for p in range(count):
            ref[row, q * count + p] = tiles[q][p]


def kernel(
    n_dir, n_gx,
    cot, pot, height, adjoint, gradient,
    h_in, c_in, p_in, a_out, mixed,
    hs, fs, ps, ds, w0, de, d1, w1, df, d2s, d2, w2,
    v0, v1, v2, v3,
    packet, from_west, from_east, from_west2, from_east2, from_west3, from_east3, f2own, f2r, end_row, end_depth, f1,
    gn, er,
    local_sem, send_sem, recv_sem,
):
    me_dir, me = lax.axis_index("dir"), lax.axis_index("gx")

    height_in = pltpu.make_async_copy(height, h_in, local_sem.at[0])
    cot_in = pltpu.make_async_copy(cot.at[0], c_in, local_sem.at[1])
    pot_in = pltpu.make_async_copy(pot.at[0], p_in, local_sem.at[2])
    height_in.start()
    cot_in.start()
    pot_in.start()

    def inside(offset):
        return me + offset < n_gx if offset > 0 else me + offset >= 0

    barrier = pltpu.get_barrier_semaphore()
    greetings = n_dir - 1
    for offset in [o for s in range(1, GREET + 1) for o in (-s, s)]:

        @pl.when(inside(offset))
        def _():
            pl.semaphore_signal(barrier, inc=1, device_id={"gx": me + offset}, device_id_type=MESH)

        greetings = greetings + inside(offset).astype(jnp.int32)
    for step in range(1, n_dir):
        pl.semaphore_signal(
            barrier, inc=1, device_id={"dir": lax.rem(me_dir + step, n_dir)}, device_id_type=MESH
        )

    sent, by_offset = [], {}

    def copy_to(source, target, device):
        index = len(sent)
        copy = pltpu.make_async_remote_copy(
            src_ref=source, dst_ref=target, send_sem=send_sem.at[index], recv_sem=recv_sem.at[index],
            device_id=device, device_id_type=MESH,
        )
        sent.append(copy)
        return copy

    def send(source, target, offset, start=True):
        copy = copy_to(source, target, {"gx": me + offset})
        by_offset.setdefault(offset, []).append(copy)
        if start:
            pl.when(inside(offset))(copy.start)
        return copy, target, offset

    def send_sides(to_west, to_east):
        copies = [send(*to_west, -1, start=False), send(*to_east, 1, start=False)]
        odd = lax.rem(me, 2) == 1
        pl.when(odd & inside(1))(copies[1][0].start)
        pl.when(inside(-1))(copies[0][0].start)
        pl.when(jnp.logical_not(odd) & inside(1))(copies[1][0].start)
        return copies

    def arrive(copies):
        for copy, _, offset in copies:
            pl.when(inside(-offset))(copy.wait_recv)

    slots = (-9, -6, -3, 3, 6, 9)
    for offset, ones, zeros in (
        (-1, (hs.at[2],), (fs.at[pl.ds(0, 4)], ps.at[0], from_west, f1.at[pl.ds(4, 2)])),
        (1, (hs.at[4],), (fs.at[pl.ds(8, 4)], ps.at[5], from_east, f1.at[pl.ds(8, 2)])),
        (-2, (hs.at[1],), (from_west2, f1.at[pl.ds(2, 2)])),
        (2, (hs.at[5],), (from_east2, f1.at[pl.ds(10, 2)])),
        (-3, (hs.at[0],), (from_west3, f1.at[1], f2r.at[2])),
        (3, (hs.at[6],), (from_east3, f1.at[12], f2r.at[3])),
        (-6, (), (f2r.at[1],)),
        (6, (), (f2r.at[4],)),
        (-7, (d2s.at[0],), ()),
        (7, (d2s.at[2],), ()),
        (-9, (), (f2r.at[0, pl.ds(1, 2)],)),
        (9, (), (f2r.at[5, pl.ds(0, 2)],)),
    ):

        @pl.when(jnp.logical_not(inside(offset)))
        def _():
            for ref in ones:
                ref[...] = jnp.ones(ref.shape, jnp.float32)
            for ref in zeros:
                ref[...] = jnp.zeros(ref.shape, jnp.float32)

    bottom, top = iota((8, 128), 0) == 0, iota((8, 128), 0) == 7

    for p in range(4):
        ds[p, 24:32, :] = jnp.ones((8, 128), jnp.float32)
    d2[...] = jnp.ones(d2.shape, jnp.float32)
    d1[...] = jnp.ones(d1.shape, jnp.float32)

    height_in.wait()
    raw = h_in[...]
    for p, cl in enumerate(spread_lanes([raw[:, 128 * c : 128 * c + 128] for c in range(4)])):
        hs[3, 4 * p : 4 * p + 4, :] = CEILING - cl

    pl.semaphore_wait(barrier, greetings)
    depth_copies = [send(hs.at[3], hs.at[3 - o], o) for o in (-3, 3, -2, 2, -1, 1)]

    def spread_row(source, target, row, slot):
        block = source[row]
        for p, cl in enumerate(spread_lanes([block[:, 128 * c : 128 * c + 128] for c in range(4)])):
            target[slot, p] = cl

    cot_in.wait()
    for x in range(0, 4):
        spread_row(c_in, fs, x, x + 4)
    field_copies = send_sides((fs.at[pl.ds(4, 4)], fs.at[pl.ds(8, 4)]), (fs.at[pl.ds(4, 4)], fs.at[pl.ds(0, 4)]))

    def field_row(ref, slot):
        return [[ref[slot, p, pl.ds(q, 8, stride=4), :] for p in range(4)] for q in range(4)]

    arrive(depth_copies)
    for o in range(7):
        for p in range(4):
            ds[p, 4 * o : 4 * o + 4, :] = hs[o, 4 * p : 4 * p + 4, :]
    for p1 in range(2):
        de[p1] = ds[2 * p1] + ds[2 * p1 + 1]
    for p1 in range(2):
        d1[p1, 0:16, :] = 0.25 * (de[p1, pl.ds(0, 16, stride=2), :] + de[p1, pl.ds(1, 16, stride=2), :])
    df[...] = d1[0] + d1[1]
    d2s[1] = 0.25 * (df[pl.ds(0, 8, stride=2), :] + df[pl.ds(1, 8, stride=2), :])
    def faces(rows, per_strip, first):
        size = n_gx * per_strip
        place = (me * per_strip + first + REACH * size + iota((rows, 128), 0)) & (size - 1)
        return place != 0, place != size - 1

    open_west, open_east = faces(16, 4, -4)
    mid = [ds[p, 8:24, :] for p in range(4)]
    west = [ds[p, 7:23, :] for p in range(4)]
    east = [ds[p, 9:25, :] for p in range(4)]
    for p, kinds in enumerate(level_weights(mid, west, east, open_west, open_east, 1.0)):
        for kind, value in enumerate(kinds):
            w0[kind, p] = value
    open_west, open_east = faces(16, 2, -5)
    mid1 = [d1[p, 1:17, :] for p in range(2)]
    west1 = [d1[p, 0:16, :] for p in range(2)]
    east1 = [d1[p, 2:18, :] for p in range(2)]
    for p, kinds in enumerate(level_weights(mid1, west1, east1, open_west, open_east, 2.0)):
        for kind, value in enumerate(kinds):
            w1[kind, p] = value

    def guess_row(i):
        put_row(v0, i, first_guess(field_row(fs, i), table(w0, i), bottom))

    def row_of(ref, i, count=4):
        return grid_of(ref[i], count)

    def smooth_rows(source, target, low, high):
        have = {i: row_of(source, i) for i in range(low - 1, high + 1)}
        for i in range(low, high):
            put_row(target, i, swept(have[i], have[i - 1], have[i + 1], row_of(v0, i), table(w0, i), bottom, top))

    for i in range(4, 8):
        guess_row(i)
    have = [None] + [row_of(v0, i) for i in range(4, 8)] + [None]
    put_row(v1, 3, edge_swept(have[1], CE, table(w0, 3), bottom))
    for i in range(4, 8):
        put_row(v1, i, swept(have[i - 3], have[i - 4], have[i - 2], have[i - 3], table(w0, i), bottom, top))
    put_row(v1, 8, edge_swept(have[4], CW, table(w0, 8), bottom))
    have = [None] + [row_of(v1, i) for i in range(3, 9)] + [None]
    rest = {i: restricted(have[i - 2], have[i - 3], have[i - 1], row_of(v0, i) if 4 <= i <= 7 else None, table(w0, i), bottom, top) for i in range(3, 9)}
    rest[2] = edge_restricted(have[1], CE, table(w0, 2))
    rest[9] = edge_restricted(have[6], CW, table(w0, 9))
    f1p = [added(rest[2 * i + 2], rest[2 * i + 3]) for i in range(4)]
    for q in range(2):
        for p in range(2):
            packet[2 * q + p] = f1p[0][q][p]
            packet[9 + 2 * q + p] = f1p[3][q][p]

    begin = {i: first_guess(f1p[i - 4], table(w1, i), bottom) for i in range(4, 8)}
    next_row = {i: swept(begin[i], begin.get(i - 1), begin.get(i + 1), begin[i], table(w1, i), bottom, top) for i in range(4, 8)}
    next_row[3] = edge_swept(begin[4], CE, table(w1, 3), bottom)
    next_row[8] = edge_swept(begin[7], CW, table(w1, 8), bottom)
    rest = {
        i: restricted(next_row[i], next_row.get(i - 1), next_row.get(i + 1), begin.get(i), table(w1, i), bottom, top)
        for i in range(3, 9)
    }
    rest[2] = edge_restricted(next_row[3], CE, table(w1, 2))
    rest[9] = edge_restricted(next_row[8], CW, table(w1, 9))
    f2p = [sum(rest[i][0][0] for i in rows) for rows in ((2,), (3, 4), (5, 6), (7, 8), (9,))]
    for k in range(5):
        packet[4 + k] = f2p[k]
    sum_copies = [
        send(packet.at[pl.ds(0, 7)], from_east, -1),
        send(packet.at[pl.ds(6, 7)], from_west, 1),
        send(packet.at[pl.ds(4, 2)], from_east2, -2),
        send(packet.at[pl.ds(7, 2)], from_west2, 2),
        send(packet.at[4], from_east3.at[0], -3),
        send(packet.at[8], from_west3.at[0], 3),
    ]

    d2_copies = [send(d2s.at[1], d2s.at[1 - s], 7 * s) for s in (-1, 1)]
    end_depths = []
    for end, (home, sign) in enumerate(((0, 1), (n_gx - 1, -1))):
        for away in (4, 5, 6):
            copy = copy_to(d2s.at[1], end_depth.at[end], {"gx": me + sign * away})
            pl.when(me == home)(copy.start)
            end_depths.append((copy, end, home, home + sign * away, 7 - sign * away))

    pot_in.wait()
    for x in range(0, 4):
        spread_row(p_in, ps, x, x + 1)

    arrive(sum_copies)
    f2own[0] = (f2p[1] + from_west[0]) + (from_east[4] + from_west2[0]) + from_west3[0]
    f2own[1] = (f2p[2] + from_west[1]) + (from_east[5] + from_west2[1]) + from_east2[0]
    f2own[2] = (f2p[3] + from_west[2]) + (from_east[6] + from_east2[1]) + from_east3[0]
    row_copies = [
        send(f2own.at[pl.ds(0, 2)], f2r.at[5, pl.ds(0, 2)], -9),
        send(f2own.at[pl.ds(1, 2)], f2r.at[0, pl.ds(1, 2)], 9),
    ]
    row_copies += [send(f2own, f2r.at[slots.index(-o)], o) for o in (-6, 6, -3, 3)]
    end_copies = []
    for end, (home, sign) in enumerate(((0, 1), (n_gx - 1, -1))):
        for block in (3, 6, 9):
            copy = copy_to(f2own.at[1], end_row.at[end], {"gx": me + sign * (block - 1)})
            pl.when(me == home)(copy.start)
            end_copies.append((copy, end, home, home + sign * (block - 1), slots.index(-sign * block)))
    for q in range(2):
        for p in range(2):
            f1[6, 2 * q + p] = f1p[1][q][p] + from_west[3 + 2 * q + p]
            f1[7, 2 * q + p] = f1p[2][q][p] + from_east[2 * q + p]
    arrive(d2_copies)
    d2[0:8, :] = d2s[0]
    d2[7:15, :] = d2s[1]
    d2[14:22, :] = d2s[2]
    for copy, end, _, place, first in end_depths:

        @pl.when(me == place)
        def _():
            copy.wait_recv()
            d2[first : first + 7, :] = end_depth[end, 0:7, :]

    open_west, open_east = faces(24, 1, -9)
    for kind, value in enumerate(
        level_weights([d2[1:25, :]], [d2[0:24, :]], [d2[2:26, :]], open_west, open_east, 4.0)[0]
    ):
        w2[kind, 0] = value

    terrain = terrain_weights(
        [ds[p, 8:24, :] for p in range(4)], [ds[p, 7:23, :] for p in range(4)], [ds[p, 9:25, :] for p in range(4)],
        *faces(16, 4, -4),
    )
    for p, kinds in enumerate(terrain):
        for kind, value in enumerate(kinds):
            w0[GW + kind, p] = value
    f1_copies = [send(f1.at[pl.ds(6, 2)], f1.at[pl.ds(6 - 2 * o, 2)], o) for o in (-1, 1, -2, 2)]
    f1_copies += [send(f1.at[6], f1.at[12], -3), send(f1.at[7], f1.at[1], 3)]
    arrive(field_copies)
    for i in range(0, 4):
        guess_row(i)
    for i in range(8, 12):
        guess_row(i)
    smooth_rows(v0, v1, 1, 11)
    potential_copies = send_sides((ps.at[1], ps.at[5]), (ps.at[4], ps.at[0]))

    arrive(row_copies)
    for copy, end, _, place, slot in end_copies:

        @pl.when(me == place)
        def _():
            copy.wait_recv()
            f2r[slot, 2 - 2 * end] = end_row[end]

    start = []
    for o in range(-REACH, REACH + 1):
        block = (o + 10) // 3 * 3 - 9
        source = f2own[o + 1] if block == 0 else f2r[slots.index(block), o - block + 1]
        start.append(first_guess([[source]], table(w2, o + REACH), bottom))
    now = start
    for sweep in range(7):
        later = [None] * len(now)
        for i in range(sweep + 1, len(now) - sweep - 1):
            later[i] = swept(now[i], now[i - 1], now[i + 1], start[i], table(w2, i), bottom, top)
        now = later

    arrive(f1_copies)
    begin = {i: first_guess(grid_of(f1[i + 1], 2), table(w1, i), bottom) for i in range(0, 12)}
    fixed = {}
    for i in range(1, 11):
        fix = now[(i - 5) // 2 + REACH][0][0]
        row = swept(begin[i], begin[i - 1], begin[i + 1], begin[i], table(w1, i), bottom, top)
        fixed[i] = [[t + fix for t in line] for line in row]
    for low, high in ((2, 10), (3, 9)):
        fixed = {
            i: swept(fixed[i], fixed[i - 1], fixed[i + 1], begin[i], table(w1, i), bottom, top) for i in range(low, high)
        }

    have = {i: row_of(v1, i) for i in range(1, 11)}
    for i in range(1, 11):
        fix = fixed[(i - 4 + 8) // 2 + 1]
        put_row(v3, i, [[have[i][q][p] + fix[q // 2][p // 2] for p in range(4)] for q in range(4)])
    smooth_rows(v3, v2, 2, 10)
    smooth_rows(v2, v1, 3, 9)

    arrive(potential_copies)

    def terrain_row(x):
        w = table(w0, x + 4)
        a, a_west, a_east = (row_of(v1, x + 4 + d) for d in (0, -1, 1))
        b, b_west, b_east = (field_row(ps, x + 1 + d) for d in (0, -1, 1))
        zeros = jnp.zeros((8, 128), jnp.float32)
        by_z, by_west, by_east, by_north = ([zeros] * 4 for _ in range(4))
        for q in range(4):
            for p in range(4):
                by_z[p] += (above(a, q, p, top) - a[q][p]) * (above(b, q, p, top) - b[q][p])
                by_west[p] += (a[q][p] - a_west[q][p]) * (b[q][p] - b_west[q][p])
                by_east[p] += (a_east[q][p] - a[q][p]) * (b_east[q][p] - b[q][p])
                by_north[p] += (north_of(a, q, p) - a[q][p]) * (north_of(b, q, p) - b[q][p])
        out = []
        for p in range(4):
            by_south = by_north[p - 1] if p else pltpu.roll(by_north[3], 1, 1)
            total = w(GW, p) * by_west[p] + w(GE, p) * by_east[p] + w(GN, p) * by_north[p]
            total = total + w(GS, p) * by_south + w(GZ, p) * by_z[p]
            out.append(jnp.sum(total, axis=0, keepdims=True))
        return out

    sums = [terrain_row(x) for x in range(4)]
    blank = jnp.zeros((4, 128), jnp.float32)
    packed = [jnp.concatenate([sums[x][p] for x in range(4)] + [blank], axis=0) for p in range(4)]
    for c, tile in enumerate(join_lanes(packed)):
        gn[c] = tile
    dir_copies = []
    for step in sorted(range(1, n_dir), key=lambda k: abs(2 * k - n_dir)):
        target = lax.rem(me_dir + step, n_dir)
        dir_copies.append(copy_to(gn.at[target // (n_dir // 4)], er.at[step - 1], {"dir": target}))
        dir_copies[-1].start()

    def natural_row(x):
        now_row = row_of(v1, x + 4)
        for p in range(4):
            for q in range(4):
                mixed[x, p, pl.ds(q, 8, stride=4), :] = now_row[q][p]
        for c, tile in enumerate(join_lanes([mixed[x, p] for p in range(4)])):
            a_out[x, :, 128 * c : 128 * c + 128] = tile

    for i in range(0, 4):
        natural_row(i)
    out_copy = pltpu.make_async_copy(a_out, adjoint.at[0], local_sem.at[3])
    out_copy.start()

    for copy, _, home, _, _ in end_depths + end_copies:
        pl.when(me == home)(copy.wait_send)
    for offset, copies in by_offset.items():

        @pl.when(inside(offset))
        def _():
            for copy in copies:
                copy.wait_send()

    for copy in dir_copies:
        copy.wait_recv()
    total = gn[me_dir // (n_dir // 4)]
    for step in range(1, n_dir):
        total = total + er[step - 1]
    part = lax.rem(me_dir, n_dir // 4)
    mine = total
    width = gradient.shape[1]
    for k in range(1, 128 // width):
        mine = jnp.where(iota((8, 128), 0) * 0 + part == k, pltpu.roll(total, 128 - k * width, 1), mine)
    gradient[...] = mine[0:4, 0:width]

    out_copy.wait()
    for copy in dir_copies:
        copy.wait_send()


def body(cotangent, potential, height):
    n_dir, n_gx = lax.axis_size("dir"), lax.axis_size("gx")
    f32 = jnp.float32
    shapes = [
        (4, 512), (4, 32, 512), (4, 32, 512), (4, 32, 512), (4, 4, 32, 128),
        (7, 16, 128), (12, 4, 32, 128), (6, 4, 32, 128), (4, 32, 128), (14, 4, 16, 128),
        (2, 32, 128), (2, 24, 128), (9, 2, 16, 128), (24, 128), (3, 8, 128), (32, 128), (9, 1, 24, 128),
        (12, 16, 8, 128), (12, 16, 8, 128), (12, 16, 8, 128), (12, 16, 8, 128),
        (13, 8, 128), (7, 8, 128), (7, 8, 128), (2, 8, 128), (2, 8, 128), (1, 8, 128), (1, 8, 128), (3, 8, 128), (6, 3, 8, 128), (2, 8, 128), (2, 8, 128), (14, 4, 8, 128),
        (4, 8, 128), (n_dir - 1, 8, 128),
    ]
    copies = 6 + 2 + 2 + 2 + 6 + 6 + 6 + 6 + 6 + n_dir - 1
    return pl.pallas_call(
        functools.partial(kernel, n_dir, n_gx),
        out_shape=(
            pltpu.VMEM(cotangent.shape, f32),
            pltpu.VMEM((height.shape[0], height.shape[1] // n_dir), f32),
        ),
        in_specs=[pl.BlockSpec(memory_space=pltpu.HBM)] * 3,
        out_specs=(pl.BlockSpec(memory_space=pl.ANY), pl.BlockSpec(memory_space=pltpu.VMEM)),
        scratch_shapes=[pltpu.VMEM(shape, f32) for shape in shapes]
        + [pltpu.SemaphoreType.DMA((4,)), pltpu.SemaphoreType.DMA((copies,)), pltpu.SemaphoreType.DMA((copies,))],
        compiler_params=pltpu.CompilerParams(
            collective_id=0, has_side_effects=True, vmem_limit_bytes=60 * 1024 * 1024
        ),
        name="vcycle",
    )(cotangent, potential, height)


def solution(mesh):
    placed = (P("dir", "gx", None, None), P("dir", "gx", None, None), P("gx", None))
    return jax.shard_map(
        body,
        mesh=mesh,
        in_specs=placed,
        out_specs=(P("dir", "gx", None, None), P("gx", "dir")),
        check_vma=False,
    )
```
